32 devices in a mesh: ctx: 4 (over y, x), rep: 8 (over z, core).
Axes of the slice: x: 2, y: 2, z: 4, core: 2. Of those that a mesh axis runs over, the one named last changes fastest.
Arguments:
- queries: bfloat16 [8, 512, 4096], P('rep', 'ctx'), may hold values from -200 to 200
- keys: bfloat16 [8, 512, 512], P('rep', 'ctx'), may hold values from -6 to 6
- values: bfloat16 [8, 512, 512], P('rep', 'ctx'), may hold values from -6 to 6
- mixer_input: bfloat16 [8, 512, 8192], P('rep', 'ctx'), may hold values from -6 to 6
- gate_input: bfloat16 [8, 512, 8192], P('rep', 'ctx'), may hold values from -6 to 6
- segment_ids: int32 [8, 512], P('rep'), may hold values from 0 to 2, never falling along the last dimension, each value on 1 to 256 neighbouring positions
- conv_weight: float32 [4, 8192], replicated, may hold values from -3 to 3
- conv_bias: float32 [8192], replicated, may hold values from -3 to 3
- select_weight: bfloat16 [544, 8192], P(None, 'rep'), may hold values from -0.0625 to 0.0625
- delta_weight: bfloat16 [512, 8192], P(None, 'rep'), may hold values from -0.25 to 0.25
- delta_bias: float32 [8192], replicated, may hold values from -12 to -3
- decay_log: float32 [8192, 16], replicated, may hold values from 0 to 2.77
- skip_gain: float32 [8192], replicated, may hold values from 0.5 to 1.5
Outputs:
- attended: bfloat16 [8, 512, 4096], P('rep', 'ctx')
- mixed: bfloat16 [8, 512, 8192], P('rep', 'ctx')
The draws below stay inside these ranges and needn't reach their ends.
All inputs are finite; a program needn't handle non-finite values.
Results may differ from the reference program's by a relative error of at most 0.012.
Values may be sent and summed in bfloat16 or wider, within the bound.
No kernel may reach another device: no remote copies, remote signals or barrier semaphores. Data moves between devices by JAX's collectives and lax.ppermute only.
A program may use at most 192 MiB of HBM per device.

```python
import math
import jax
import jax.numpy as jnp
import numpy as np
from jax import lax

ROLLOUT_LENGTH = 512
ROLLOUT_COUNT = 8
QUERY_HEADS = 32
KEY_VALUE_HEADS = 4
HEAD_WIDTH = 128
INNER = 8192
STATE = 16
RANK = 512


def shared_keys(key, pull_weight):
    starting_keys = jnp.clip(jax.random.normal(jax.random.fold_in(key, 101), (ROLLOUT_COUNT, ROLLOUT_LENGTH, KEY_VALUE_HEADS, HEAD_WIDTH), jnp.float32), -6.0, 6.0)
    perturb_scale = jax.random.uniform(jax.random.fold_in(key, 102), (ROLLOUT_COUNT, ROLLOUT_LENGTH, KEY_VALUE_HEADS), jnp.float32, 9.0, 27.0)
    places = jnp.arange(ROLLOUT_LENGTH)
    marked = ((places % 53 == 11) & (places >= 2)).astype(jnp.float32) * pull_weight
    margin = 2.0 * math.sqrt(HEAD_WIDTH) / (perturb_scale * HEAD_WIDTH)
    next_keys = jnp.roll(starting_keys, -1, axis=1)
    mark_ahead = jnp.roll(marked, -2)
    margin_ahead = jnp.roll(margin, -2, axis=1)
    complete_keys = starting_keys + mark_ahead[None, :, None, None] * (next_keys * (1.0 - margin_ahead[..., None]) - starting_keys)
    return complete_keys


def channel_bias(key):
    return jax.random.uniform(jax.random.fold_in(key, 201), (INNER,), jnp.float32, -12.0, -3.0)


def draw_keys(key, part):
    pull_weight = 0.0
    complete_keys = shared_keys(key, pull_weight)
    return complete_keys.reshape(ROLLOUT_COUNT, ROLLOUT_LENGTH, KEY_VALUE_HEADS * HEAD_WIDTH).astype(jnp.bfloat16)


def draw_queries(key, part):
    key = jax.random.fold_in(key, 7)
    query_groups = QUERY_HEADS // KEY_VALUE_HEADS
    perturb_rows = jnp.clip(jax.random.normal(key, (ROLLOUT_COUNT, ROLLOUT_LENGTH, KEY_VALUE_HEADS, query_groups, HEAD_WIDTH), jnp.float32), -6.0, 6.0)
    queries_all = perturb_rows
    return queries_all.reshape(ROLLOUT_COUNT, ROLLOUT_LENGTH, QUERY_HEADS * HEAD_WIDTH).astype(jnp.bfloat16)


def draw_delta_bias(key, part):
    bias_values = channel_bias(key)
    return bias_values.astype(jnp.float32)


def draw_delta_weight(key, part):
    bias_values = channel_bias(key)
    key = jax.random.fold_in(key, 17)
    spread_pick = jax.random.uniform(jax.random.fold_in(key, 1), (INNER,), jnp.float32, 0.3, 1.0)
    column_scale = spread_pick * (0.5 - bias_values) / 3.5
    noise = jnp.clip(jax.random.normal(jax.random.fold_in(key, 2), (RANK, INNER), jnp.float32), -6.0, 6.0)
    entries = noise * column_scale[None, :] / math.sqrt(RANK)
    return jnp.clip(entries, -0.25, 0.25).astype(jnp.bfloat16)


def shard_levels(key, dims, pieces, low, top_value):
    def one(dim, blocks):
        draws = jax.random.uniform(jax.random.fold_in(jax.random.fold_in(key, 6), dim), (blocks,), jnp.float32, low / len(pieces), top_value / len(pieces))
        return jnp.repeat(jnp.exp(draws), dims[dim] // blocks).reshape((-1,) + (1,) * (len(dims) - dim - 1))

    factor_of = one(*pieces[0])
    for cut in pieces[1:]:
        factor_of = factor_of * one(*cut)
    return factor_of


def split_up(number_of, total, most, skew):
    loads = [(1 << 20) // math.isqrt(grade ** skew) + 1 for grade in range(2, number_of + 1)]
    rest, given = total - most - (number_of - 1), [1] * (number_of - 1)
    while rest > 0:
        free = [i for i in range(number_of - 1) if given[i] < most]
        mass, left = sum([loads[i] for i in free]), rest
        for i in free:
            extra = min(most - given[i], max(1, left * loads[i] // mass), rest)
            given[i] = given[i] + extra
            rest = rest - extra
    return np.array([most] + given)


def uneven(key, amount, total, reach, skew):
    if amount == 2:
        one = jax.random.randint(key, (), max(1, total - reach), min(reach, total - 1) + 1)
        return jnp.stack([one, total - one])
    lengths = jnp.asarray(split_up(amount, total, reach, skew), jnp.int32)
    twos = (amount - 1) // 2
    source_of, taker = lengths[1:1 + 2 * twos:2], lengths[2:2 + 2 * twos:2]
    room = jnp.minimum(source_of - 1, reach - taker)
    shifted = jax.random.randint(jax.random.fold_in(key, 1), (twos,), 0, 1 << 20) % (room + 1)
    lengths = lengths.at[1:1 + 2 * twos:2].set(source_of - shifted).at[2:2 + 2 * twos:2].set(taker + shifted)
    return lengths[jax.random.permutation(jax.random.fold_in(key, 2), amount)]


def normal_values(key, dims, scale, most, shards=(), held_as=jnp.bfloat16):
    level = shard_levels(key, dims, shards, -0.22, 0.18) if shards else 1.0
    values = jax.random.normal(key, dims, jnp.float32) * scale * level
    return jnp.minimum(jnp.maximum(values, -most), most).astype(held_as)


def setup_inputs(seed: int = 0) -> dict:
    splits = jax.random.split(jax.random.key(seed), 14)
    return {
        "queries": draw_queries(jax.random.fold_in(splits[13], 71), 0),
        "keys": draw_keys(jax.random.fold_in(splits[13], 71), 0),
        "values": normal_values(splits[2], (ROLLOUT_COUNT, ROLLOUT_LENGTH, KEY_VALUE_HEADS * HEAD_WIDTH), 1.0, 6.0, ((0, 8), (1, 4))),
        "mixer_input": normal_values(splits[3], (ROLLOUT_COUNT, ROLLOUT_LENGTH, INNER), 1.0, 6.0, ((0, 8), (1, 4))),
        "gate_input": normal_values(splits[4], (ROLLOUT_COUNT, ROLLOUT_LENGTH, INNER), 1.0, 6.0, ((0, 8), (1, 4))),
        "segment_ids": jax.vmap(lambda own: jnp.searchsorted(jnp.cumsum(uneven(own, 3, ROLLOUT_LENGTH, ROLLOUT_LENGTH // 2, 0)), jnp.arange(ROLLOUT_LENGTH), side="right"))(jax.random.split(splits[5], ROLLOUT_COUNT)).reshape((ROLLOUT_COUNT, ROLLOUT_LENGTH)).astype(jnp.int32),
        "conv_weight": normal_values(splits[6], (4, INNER), 4 ** -0.5, 3.0, (), jnp.float32),
        "conv_bias": normal_values(splits[7], (INNER,), 0.5, 3.0, (), jnp.float32),
        "select_weight": normal_values(splits[8], (RANK + 2 * STATE, INNER), INNER ** -0.5, 0.0625, ((1, 8),)),
        "delta_weight": draw_delta_weight(jax.random.fold_in(splits[13], 71), 0),
        "delta_bias": draw_delta_bias(jax.random.fold_in(splits[13], 71), 0),
        "decay_log": jnp.clip(jax.random.uniform(splits[11], (INNER, STATE), jnp.float32, 0.0, 2.77), 0.0, 2.77),
        "skip_gain": jnp.clip(jax.random.uniform(splits[12], (INNER,), jnp.float32, 0.5, 1.5), 0.5, 1.5),
    }


def conv_layer(mixer_rows, seg_ids, conv_weight, conv_bias):
    padded = jnp.concatenate([jnp.zeros((3, mixer_rows.shape[1]), jnp.float32), mixer_rows.astype(jnp.float32)], axis=0)
    seg_pad = jnp.concatenate([jnp.full((3,), -1, jnp.int32), seg_ids.astype(jnp.int32)], axis=0)
    tok_rows = mixer_rows.shape[0]
    running = conv_bias[None, :] + jnp.zeros((tok_rows, mixer_rows.shape[1]), jnp.float32)
    for tap_index in range(4):
        match_seg = (seg_pad[tap_index:tap_index + tok_rows] == seg_ids).astype(jnp.float32)
        running = running + conv_weight[tap_index][None, :] * padded[tap_index:tap_index + tok_rows] * match_seg[:, None]
    return jax.nn.silu(running).astype(jnp.bfloat16)

def prepare(mixer_rows, seg_ids, conv_weight, conv_bias, select_weight, delta_weight, delta_bias):
    conv_out = conv_layer(mixer_rows, seg_ids, conv_weight, conv_bias)
    select = jnp.dot(conv_out, select_weight.T, preferred_element_type=jnp.float32)
    low_part = select[:, :RANK]
    low_norm = (low_part * lax.rsqrt(lax.optimization_barrier(jnp.mean(low_part * low_part, axis=-1, keepdims=True)) + 1e-06)).astype(jnp.bfloat16)
    delta = jax.nn.softplus(jnp.dot(low_norm, delta_weight, preferred_element_type=jnp.float32) + delta_bias).astype(jnp.bfloat16)
    return (conv_out, delta, select[:, RANK:RANK + STATE], select[:, RANK + STATE:])

def attend(query_rows, rows_of_keys, rows_of_values, seg_ids):
    query_groups = QUERY_HEADS // KEY_VALUE_HEADS
    rows_of_block = math.gcd(ROLLOUT_LENGTH, 512)
    score_scale = 1.0 / math.sqrt(HEAD_WIDTH)
    keys_widened = rows_of_keys.astype(jnp.float32).reshape(ROLLOUT_LENGTH, KEY_VALUE_HEADS, HEAD_WIDTH)
    values_widened = rows_of_values.astype(jnp.float32).reshape(ROLLOUT_LENGTH, KEY_VALUE_HEADS, HEAD_WIDTH)
    positions = jnp.arange(ROLLOUT_LENGTH).astype(jnp.int32)

    def query_block(block_index):
        first_row = (block_index * rows_of_block).astype(jnp.int32)
        queries_widened = lax.dynamic_slice_in_dim(query_rows, first_row, rows_of_block, 0).astype(jnp.float32)
        queries_widened = queries_widened.reshape(rows_of_block, KEY_VALUE_HEADS, query_groups, HEAD_WIDTH)
        seg_query = lax.dynamic_slice_in_dim(seg_ids, first_row, rows_of_block, 0)
        query_pos = first_row + jnp.arange(rows_of_block).astype(jnp.int32)
        scores = jnp.einsum('tkgd,skd->kgts', queries_widened, keys_widened) * score_scale
        allowed = (positions[None, :] <= query_pos[:, None]) & (seg_ids[None, :] == seg_query[:, None])
        scores = jnp.where(allowed, scores, -1e+30)
        row_max = lax.optimization_barrier(jnp.max(scores, axis=-1, keepdims=True))
        weights = jnp.where(allowed, jnp.exp(scores - row_max), 0.0)
        normaliser = lax.optimization_barrier(jnp.sum(weights, axis=-1))
        rounded = lax.optimization_barrier(weights.astype(jnp.bfloat16)).astype(jnp.float32)
        result = jnp.einsum('kgts,skd->kgtd', rounded, values_widened) / normaliser[..., None]
        return jnp.transpose(result, (2, 0, 1, 3)).reshape(rows_of_block, QUERY_HEADS * HEAD_WIDTH).astype(jnp.bfloat16)
    blocks = lax.map(query_block, jnp.arange(ROLLOUT_LENGTH // rows_of_block).astype(jnp.int32))
    return blocks.reshape(ROLLOUT_LENGTH, QUERY_HEADS * HEAD_WIDTH)

def reference(queries, keys, values, mixer_input, gate_input, segment_ids, conv_weight, conv_bias, select_weight, delta_weight, delta_bias, decay_log, skip_gain):
    attended = lax.map(lambda item: attend(item[0], item[1], item[2], item[3]), (queries, keys, values, segment_ids))
    conv_out, delta, in_map, out_map = lax.map(lambda item: prepare(item[0], item[1], conv_weight, conv_bias, select_weight, delta_weight, delta_bias), (mixer_input, segment_ids))
    same_seg = jnp.concatenate([jnp.zeros((ROLLOUT_COUNT, 1), jnp.float32), (segment_ids[:, 1:] == segment_ids[:, :-1]).astype(jnp.float32)], axis=1)
    decay_rates = -jnp.exp(decay_log)

    def advance(hidden_state, inputs):
        delta_row, conv_row, in_row, out_row, keep_flag, gate_row = inputs
        delta_f = delta_row.astype(jnp.float32)
        conv_f = conv_row.astype(jnp.float32)
        decay = jnp.exp(delta_f[:, :, None] * decay_rates[None]) * keep_flag[:, None, None]
        hidden_state = decay * hidden_state + (delta_f * conv_f)[:, :, None] * in_row[:, None, :]
        ssm_out = lax.optimization_barrier(jnp.sum(hidden_state * out_row[:, None, :], axis=-1))
        result = ((ssm_out + skip_gain[None, :] * conv_f) * jax.nn.silu(gate_row.astype(jnp.float32))).astype(jnp.bfloat16)
        return (hidden_state, result)
    inputs = tuple((jnp.swapaxes(array, 0, 1) for array in (delta, conv_out, in_map, out_map, same_seg, gate_input)))
    start_state = jnp.zeros((ROLLOUT_COUNT, INNER, STATE), jnp.float32)
    last_state, mixed = lax.scan(advance, start_state, inputs)
    return (attended, jnp.swapaxes(mixed, 0, 1))
```

```python
import functools
import math

import jax
import jax.numpy as jnp
from jax import lax
from jax.experimental import pallas as pl
from jax.experimental.pallas import tpu as pltpu
from jax.sharding import PartitionSpec as P

QUERY_HEADS = 32
KEY_VALUE_HEADS = 4
HEAD_WIDTH = 128
LANES = 128
SUBLANES = 8
LOG2E = 1.0 / math.log(2.0)
FAR = 1e30


def silu(value):
    return 0.5 * value * (1.0 + jnp.tanh(0.5 * value))


def attention_kernel(seg_q_ref, seg_k_ref, q_ref, *refs):
    key_refs, value_refs, out_ref = refs[0:-1:2], refs[1:-1:2], refs[-1]
    rows = q_ref.shape[0]
    span = seg_k_ref.shape[1]
    groups = QUERY_HEADS // KEY_VALUE_HEADS
    row = lax.broadcasted_iota(jnp.int32, (rows, span), 0) + (span - rows)
    col = lax.broadcasted_iota(jnp.int32, (rows, span), 1)
    allowed = (col <= row) & (seg_q_ref[...] == seg_k_ref[...])
    keys = jnp.concatenate([ref[...] for ref in key_refs], axis=0)
    vals = jnp.concatenate([ref[...] for ref in value_refs], axis=0)
    factor = LOG2E / math.sqrt(HEAD_WIDTH)
    for head in range(groups):
        lanes = slice(head * HEAD_WIDTH, (head + 1) * HEAD_WIDTH)
        scores = lax.dot_general(
            q_ref[:, lanes], keys, (((1,), (1,)), ((), ())), preferred_element_type=jnp.float32
        )
        scores = jnp.where(allowed, scores, -FAR)
        top = jnp.max(scores, axis=-1, keepdims=True)
        weights = jnp.exp2((scores - top) * factor)
        norm = jnp.sum(weights, axis=-1, keepdims=True)
        total = jnp.dot(weights.astype(jnp.bfloat16), vals, preferred_element_type=jnp.float32)
        out_ref[:, lanes] = (total / norm).astype(out_ref.dtype)


def attention(queries, blocks, seg_q, seg_k):
    rows = queries.shape[0]
    span = seg_k.shape[1]
    group_width = QUERY_HEADS // KEY_VALUE_HEADS * HEAD_WIDTH
    key_spec = pl.BlockSpec((rows, HEAD_WIDTH), lambda h: (0, h))
    value_spec = pl.BlockSpec((rows, HEAD_WIDTH), lambda h: (0, KEY_VALUE_HEADS + h))
    wide = pl.BlockSpec((rows, group_width), lambda h: (0, h))
    return pl.pallas_call(
        attention_kernel,
        grid=(KEY_VALUE_HEADS,),
        in_specs=[
            pl.BlockSpec((rows, 1), lambda h: (0, 0)),
            pl.BlockSpec((1, span), lambda h: (0, 0)),
            wide,
            *([key_spec, value_spec] * len(blocks)),
        ],
        out_specs=wide,
        out_shape=jax.ShapeDtypeStruct(queries.shape, jnp.bfloat16),
        compiler_params=pltpu.CompilerParams(vmem_limit_bytes=32 << 20),
        cost_estimate=pl.CostEstimate(
            flops=4 * rows * span * QUERY_HEADS * HEAD_WIDTH,
            bytes_accessed=4 * queries.size,
            transcendentals=rows * span * QUERY_HEADS,
        ),
        name="attention",
    )(seg_q, seg_k, queries, *[block for block in blocks for _ in range(2)])


def conv_select_kernel(place_ref, seg_ref, x_ref, weight_ref, bias_ref, select_ref, conv_ref, part_ref, masks, padded, total):
    step = pl.program_id(0)
    toks = seg_ref.shape[0]
    width = x_ref.shape[2]
    pieces = x_ref.shape[0]
    rows = x_ref.shape[1]

    @pl.when(step == 0)
    def _():
        seg = seg_ref[...]
        wide_seg = jnp.broadcast_to(seg, (toks, LANES)).astype(jnp.float32)
        padded[0:SUBLANES, 0:LANES] = jnp.full((SUBLANES, LANES), -1.0, jnp.float32)
        padded[SUBLANES : SUBLANES + toks, 0:LANES] = wide_seg
        for tap in range(3):
            before = padded[SUBLANES - 3 + tap : SUBLANES - 3 + tap + toks, 0:LANES]
            masks[tap] = jnp.where(before == wide_seg, 1.0, 0.0)
        padded[0:SUBLANES, :] = jnp.zeros((SUBLANES, width), jnp.float32)
        total[...] = jnp.zeros_like(total)

    for piece in range(pieces):
        padded[SUBLANES + piece * rows : SUBLANES + (piece + 1) * rows, :] = x_ref[piece].astype(jnp.float32)
    outs = []
    for tile in range(width // LANES):
        lanes = slice(tile * LANES, (tile + 1) * LANES)
        running = jnp.broadcast_to(bias_ref[0:1, lanes], (toks, LANES))
        for tap in range(4):
            moved = padded[SUBLANES - 3 + tap : SUBLANES - 3 + tap + toks, lanes]
            term = weight_ref[tap : tap + 1, lanes] * moved
            running = running + (term * masks[tap] if tap < 3 else term)
        conv = silu(running).astype(jnp.bfloat16)
        conv_ref[tile] = conv
        outs.append(conv)
    conv_all = jnp.concatenate(outs, axis=1) if len(outs) > 1 else outs[0]
    total[...] += lax.dot_general(
        conv_all, select_ref[0], (((1,), (1,)), ((), ())), preferred_element_type=jnp.float32
    )

    @pl.when(step == pl.num_programs(0) - 1)
    def _():
        for piece in range(pieces):
            part_ref[piece] = total[piece * rows : (piece + 1) * rows, :].astype(part_ref.dtype)


def conv_select(place, seg_col, pieces, conv_weight, conv_bias, select_parts):
    shards, outputs, width = select_parts.shape
    ctx, rows, _ = pieces.shape
    toks = ctx * rows
    tiles = width // LANES
    return pl.pallas_call(
        conv_select_kernel,
        grid_spec=pltpu.PrefetchScalarGridSpec(
            num_scalar_prefetch=1,
            grid=(shards,),
            in_specs=[
                pl.BlockSpec((toks, 1), lambda s, p: (0, 0)),
                pl.BlockSpec((ctx, rows, width), lambda s, p: (0, 0, s)),
                pl.BlockSpec((4, width), lambda s, p: (0, s * ctx + p[0])),
                pl.BlockSpec((1, width), lambda s, p: (0, s * ctx + p[0])),
                pl.BlockSpec((1, outputs, width), lambda s, p: (s, 0, 0)),
            ],
            out_specs=[
                pl.BlockSpec((tiles, toks, LANES), lambda s, p: (s, 0, 0)),
                pl.BlockSpec((ctx, rows, outputs), lambda s, p: (0, 0, 0)),
            ],
            scratch_shapes=[
                pltpu.VMEM((3, toks, LANES), jnp.float32),
                pltpu.VMEM((SUBLANES + toks, width), jnp.float32),
                pltpu.VMEM((toks, outputs), jnp.float32),
            ],
        ),
        out_shape=[
            jax.ShapeDtypeStruct((shards * tiles, toks, LANES), jnp.bfloat16),
            jax.ShapeDtypeStruct((ctx, rows, outputs), jnp.bfloat16),
        ],
        compiler_params=pltpu.CompilerParams(vmem_limit_bytes=40 << 20),
        cost_estimate=pl.CostEstimate(
            flops=2 * toks * shards * width * outputs,
            bytes_accessed=2 * pieces.size * 2 + 2 * select_parts.size,
            transcendentals=pieces.size,
        ),
        name="conv_select",
    )(place, seg_col, pieces, conv_weight, conv_bias, select_parts)


def normalise_kernel(rank, part_ref, out_ref):
    total = part_ref[0].astype(jnp.float32)
    for piece in range(1, part_ref.shape[0]):
        total = total + part_ref[piece].astype(jnp.float32)
    low = total[:, :rank]
    scale = lax.rsqrt(jnp.mean(low * low, axis=-1, keepdims=True) + 1e-06)
    out_ref[:, :rank] = (low * scale).astype(out_ref.dtype)
    out_ref[:, rank:] = total[:, rank:].astype(out_ref.dtype)


def normalise(parts, rank):
    return pl.pallas_call(
        functools.partial(normalise_kernel, rank),
        out_shape=jax.ShapeDtypeStruct(parts.shape[1:], jnp.bfloat16),
        name="normalise",
    )(parts)


def scan_kernel(rank, seg_ref, low_ref, weight_ref, bias_ref, decay_ref, gain_ref, conv_ref, out_ref,
                reset, maps, delta_rows, drive_rows, mixed_rows):
    toks = seg_ref.shape[0]
    states = decay_ref.shape[0]
    tiles = conv_ref.shape[0]
    per_shard = weight_ref.shape[2] // LANES
    ctx = out_ref.shape[0]
    rows = out_ref.shape[1]

    @pl.when(pl.program_id(0) == 0)
    def _():
        seg = jnp.broadcast_to(seg_ref[...], (toks, LANES)).astype(jnp.float32)
        reset[0:SUBLANES, :] = jnp.full((SUBLANES, LANES), -1.0, jnp.float32)
        reset[SUBLANES : SUBLANES + toks, :] = seg
        before = reset[SUBLANES - 1 : SUBLANES - 1 + toks, :]
        reset[0:toks, :] = jnp.where(before == seg, 0.0, FAR)
        for index in range(2 * states):
            column = low_ref[:, rank + index : rank + index + 1].astype(jnp.float32)
            maps[index] = jnp.broadcast_to(column, (toks, LANES))

    low = low_ref[:, 0:rank]
    for shard in range(tiles // per_shard):
        pre = jnp.dot(low, weight_ref[shard], preferred_element_type=jnp.float32)
        for part in range(per_shard):
            tile = shard * per_shard + part
            value = pre[:, part * LANES : (part + 1) * LANES] + bias_ref[tile : tile + 1, :]
            raised = jnp.exp(-jnp.abs(value))
            log_part = jnp.where(
                raised < 0.01,
                raised * (1.0 - raised * (0.5 - raised * (1.0 / 3.0))),
                jnp.log(1.0 + raised),
            )
            delta = (jnp.maximum(value, 0.0) + log_part).astype(jnp.bfloat16).astype(jnp.float32)
            delta_rows[tile * toks : (tile + 1) * toks, :] = delta
            drive_rows[tile * toks : (tile + 1) * toks, :] = delta * conv_ref[tile].astype(jnp.float32)

    rates = [-LOG2E * jnp.exp(decay_ref[n]) for n in range(states)]

    def block(index, held):
        held = list(held)
        for inner in range(SUBLANES):
            t = index * SUBLANES + inner
            delta = delta_rows[pl.ds(t, tiles, stride=toks), :]
            drive = drive_rows[pl.ds(t, tiles, stride=toks), :]
            far = delta + reset[pl.ds(t, 1), :]
            result = None
            for n in range(states):
                grow = jnp.exp2(far * rates[n])
                held[n] = grow * held[n] + drive * maps[n, pl.ds(t, 1), :]
                term = held[n] * maps[states + n, pl.ds(t, 1), :]
                result = term if result is None else result + term
            mixed_rows[pl.ds(t, tiles, stride=toks), :] = result
        return tuple(held)

    start = tuple(jnp.zeros((tiles, LANES), jnp.float32) for _ in range(states))
    lax.fori_loop(0, toks // SUBLANES, block, start)

    for tile in range(tiles):
        full = mixed_rows[tile * toks : (tile + 1) * toks, :] + gain_ref[tile : tile + 1, :] * conv_ref[tile].astype(
            jnp.float32
        )
        full = full.astype(out_ref.dtype)
        for piece in range(ctx):
            out_ref[piece, :, tile * LANES : (tile + 1) * LANES] = full[piece * rows : (piece + 1) * rows, :]


def state_scan(seg_col, low, delta_parts, bias, decay, gain, conv, ctx):
    toks = low.shape[0]
    shards, rank, width = delta_parts.shape
    states = decay.shape[0]
    tiles = SUBLANES
    groups = conv.shape[0] // tiles
    rows = toks // ctx
    steps = toks * conv.shape[0] * LANES * states
    return pl.pallas_call(
        functools.partial(scan_kernel, rank),
        grid=(groups,),
        in_specs=[
            pl.BlockSpec((toks, 1), lambda g: (0, 0)),
            pl.BlockSpec(low.shape, lambda g: (0, 0)),
            pl.BlockSpec((shards // groups, rank, width), lambda g: (g, 0, 0)),
            pl.BlockSpec((tiles, LANES), lambda g: (g, 0)),
            pl.BlockSpec((states, tiles, LANES), lambda g: (0, g, 0)),
            pl.BlockSpec((tiles, LANES), lambda g: (g, 0)),
            pl.BlockSpec((tiles, toks, LANES), lambda g: (g, 0, 0)),
        ],
        out_specs=pl.BlockSpec((ctx, rows, tiles * LANES), lambda g: (0, 0, g)),
        out_shape=jax.ShapeDtypeStruct((ctx, rows, conv.shape[0] * LANES), jnp.bfloat16),
        scratch_shapes=[
            pltpu.VMEM((toks + SUBLANES, LANES), jnp.float32),
            pltpu.VMEM((2 * states, toks, LANES), jnp.float32),
            pltpu.VMEM((tiles * toks, LANES), jnp.float32),
            pltpu.VMEM((tiles * toks, LANES), jnp.float32),
            pltpu.VMEM((tiles * toks, LANES), jnp.float32),
        ],
        compiler_params=pltpu.CompilerParams(vmem_limit_bytes=56 << 20),
        cost_estimate=pl.CostEstimate(
            flops=6 * steps, bytes_accessed=2 * delta_parts.size + 4 * conv.size, transcendentals=steps
        ),
        name="state_scan",
    )(seg_col, low, delta_parts, bias, decay, gain, conv)


def gate_kernel(fold, y_ref, gate_ref, out_ref):
    ctx, _, width = y_ref.shape
    for piece in range(ctx):
        place = piece % fold * (ctx // fold) + piece // fold
        lanes = slice(place * width, (place + 1) * width)
        gate = gate_ref[:, lanes].astype(jnp.float32)
        out_ref[:, lanes] = (y_ref[piece].astype(jnp.float32) * silu(gate)).astype(out_ref.dtype)


def apply_gate(pieces, gate, shards, fold):
    ctx, rows, total = pieces.shape
    width = total // shards
    return pl.pallas_call(
        functools.partial(gate_kernel, fold),
        grid=(shards,),
        in_specs=[
            pl.BlockSpec((ctx, rows, width), lambda s: (0, 0, s)),
            pl.BlockSpec((rows, ctx * width), lambda s: (0, s)),
        ],
        out_specs=pl.BlockSpec((rows, ctx * width), lambda s: (0, s)),
        out_shape=jax.ShapeDtypeStruct(gate.shape, jnp.bfloat16),
        cost_estimate=pl.CostEstimate(
            flops=4 * gate.size, bytes_accessed=6 * gate.size, transcendentals=gate.size
        ),
        name="gate",
    )(pieces, gate)


def shifted(value, axis, by):
    size = lax.axis_size(axis)
    pairs = [(i, i + by) for i in range(size) if 0 <= i + by < size]
    return lax.ppermute(value, axis, pairs)


def exchange(value):
    return lax.all_to_all(value, "ctx", 0, 0, tiled=True)


def local(
    queries,
    keys,
    values,
    mixer_input,
    gate_input,
    segment_ids,
    conv_weight,
    conv_bias,
    select_weight,
    delta_weight,
    delta_bias,
    decay_log,
    skip_gain,
):
    ctx = lax.axis_size("ctx")
    shards = lax.axis_size("rep")
    place = lax.axis_index("ctx")
    rows, channels = mixer_input.shape[1:]
    rank = delta_weight.shape[0]
    states = decay_log.shape[1]
    width = max(channels // (shards * ctx), LANES)
    fold = width * shards * ctx // channels
    tiles = channels // ctx // LANES
    seg = segment_ids[0]
    toks = seg.shape[0]
    seg_col = seg[:, None]
    back = min(ctx - 1, -(-(toks // 2 - 1) // rows))

    def own_part(array):
        cut = array.reshape(array.shape[:-1] + (shards // fold, fold, ctx // fold, width))
        cut = lax.dynamic_index_in_dim(cut, place // fold, cut.ndim - 2, keepdims=False)
        cut = lax.dynamic_index_in_dim(cut, place % fold, cut.ndim - 2, keepdims=False)
        return cut.reshape(array.shape[:-1] + (tiles, LANES))

    def gathered(weight):
        own = lax.dynamic_slice_in_dim(weight, place // fold * width, width, 1)
        parts = lax.all_gather(own, "rep", axis=0)
        if fold > 1:
            parts = parts.reshape((shards // fold, fold) + own.shape)
            parts = lax.dynamic_index_in_dim(parts, place % fold, 1, keepdims=False)
        return parts

    select_parts = gathered(select_weight)
    delta_parts = gathered(delta_weight)

    both = jnp.concatenate([keys[0], values[0]], axis=1)
    blocks = [shifted(both, "ctx", by) for by in range(back, 0, -1)] + [both]

    pieces = mixer_input[0].reshape(rows, shards // fold, fold, ctx // fold, width)
    pieces = jnp.transpose(pieces, (3, 2, 0, 1, 4)).reshape(ctx, rows, channels // ctx)
    pieces = exchange(pieces)

    seg_pad = jnp.concatenate([jnp.full((back * rows,), -1, jnp.int32), seg])
    seg_k = lax.dynamic_slice_in_dim(seg_pad, place * rows, (back + 1) * rows, 0)
    attended = attention(queries[0], blocks, seg_k[back * rows :, None], seg_k[None, :])

    lead = jnp.reshape(place % fold * (ctx // fold) + place // fold, (1,)).astype(jnp.int32)
    conv, parts = conv_select(lead, seg_col, pieces, conv_weight, conv_bias[None, :], select_parts)
    low_own = normalise(exchange(parts), rank)
    low = lax.all_gather(low_own, "ctx", axis=0, tiled=True)

    scanned = state_scan(
        seg_col,
        low,
        delta_parts,
        own_part(delta_bias),
        own_part(jnp.transpose(decay_log)),
        own_part(skip_gain),
        conv,
        ctx,
    )
    mixed = apply_gate(exchange(scanned), gate_input[0], shards // fold, fold)
    return (attended[None], mixed[None])


def solution(mesh):
    placed = (
        P("rep", "ctx", None),
        P("rep", "ctx", None),
        P("rep", "ctx", None),
        P("rep", "ctx", None),
        P("rep", "ctx", None),
        P("rep", None),
        P(),
        P(),
        P(None, "rep"),
        P(None, "rep"),
        P(),
        P(),
        P(),
    )
    return jax.shard_map(
        local,
        mesh=mesh,
        in_specs=placed,
        out_specs=(P("rep", "ctx", None), P("rep", "ctx", None)),
        check_vma=False,
    )
```

```python
import functools
import math

import jax
import jax.numpy as jnp
from jax import lax
from jax.experimental import pallas as pl
from jax.experimental.pallas import tpu as pltpu
from jax.sharding import PartitionSpec as P

QUERY_HEADS = 32
KEY_VALUE_HEADS = 4
HEAD_WIDTH = 128
LANES = 128
SUBLANES = 8
LOG2E = 1.0 / math.log(2.0)
FAR = 1e30


def silu(value):
    return 0.5 * value * (1.0 + jnp.tanh(0.5 * value))


def attention_kernel(begin, seg_q_ref, seg_k_ref, q_ref, *refs):
    out_ref = refs[-1]
    refs = refs[: -1 if begin == 0 else -2]
    rows = q_ref.shape[0]
    span = seg_k_ref.shape[1]
    groups = QUERY_HEADS // KEY_VALUE_HEADS
    row = lax.broadcasted_iota(jnp.int32, (rows, span), 0) + (span - rows)
    col = lax.broadcasted_iota(jnp.int32, (rows, span), 1)
    allowed = (col <= row) & (seg_q_ref[...] == seg_k_ref[...])
    shift = jnp.where(allowed, 0.0, -FAR)
    keys = jnp.concatenate([ref[...] for ref in refs[0::2]], axis=0)
    vals = jnp.concatenate([ref[...] for ref in refs[1::2]], axis=0)
    factor = LOG2E / math.sqrt(HEAD_WIDTH)
    batch = 4
    for first in range(0, groups, batch):
        cuts = [slice(head * HEAD_WIDTH, (head + 1) * HEAD_WIDTH) for head in range(first, first + batch)]
        scores = [
            lax.dot_general(q_ref[:, cut], keys, (((1,), (1,)), ((), ())), preferred_element_type=jnp.float32)
            for cut in cuts
        ]
        scores = [score + shift for score in scores]
        tops = [jnp.max(score, axis=-1, keepdims=True) for score in scores]
        weights = [jnp.exp2((score - top) * factor) for score, top in zip(scores, tops)]
        norms = [jnp.sum(weight, axis=-1, keepdims=True) for weight in weights]
        totals = [jnp.dot(weight.astype(jnp.bfloat16), vals, preferred_element_type=jnp.float32) for weight in weights]
        for cut, total, norm in zip(cuts, totals, norms):
            out_ref[:, cut] = (total / norm).astype(out_ref.dtype)


def attention(queries, blocks, seg_q, seg_k, begin, end, before=None):
    rows = queries.shape[0]
    span = seg_k.shape[1]
    group_width = QUERY_HEADS // KEY_VALUE_HEADS * HEAD_WIDTH
    key_spec = pl.BlockSpec((rows, HEAD_WIDTH), lambda h: (0, begin + h))
    value_spec = pl.BlockSpec((rows, HEAD_WIDTH), lambda h: (0, KEY_VALUE_HEADS + begin + h))
    wide = pl.BlockSpec((rows, group_width), lambda h: (0, begin + h))
    operands = [seg_q, seg_k, queries] + [block for block in blocks for _ in range(2)]
    in_specs = [
        pl.BlockSpec((rows, 1), lambda h: (0, 0)),
        pl.BlockSpec((1, span), lambda h: (0, 0)),
        wide,
        *([key_spec, value_spec] * len(blocks)),
    ]
    aliases = {}
    if before is not None:
        aliases = {len(operands): 0}
        operands.append(before)
        in_specs.append(pl.BlockSpec(memory_space=pl.ANY))
    return pl.pallas_call(
        functools.partial(attention_kernel, begin),
        grid=(end - begin,),
        in_specs=in_specs,
        out_specs=wide,
        out_shape=jax.ShapeDtypeStruct(queries.shape, jnp.bfloat16),
        input_output_aliases=aliases,
        compiler_params=pltpu.CompilerParams(vmem_limit_bytes=32 << 20),
        cost_estimate=pl.CostEstimate(
            flops=4 * rows * span * group_width * (end - begin),
            bytes_accessed=4 * rows * group_width * (end - begin),
            transcendentals=rows * span * group_width // HEAD_WIDTH * (end - begin),
        ),
        name=f"attention_{begin}",
    )(*operands)


def pack_kernel(order, fold, x_ref, out_ref):
    ctx, _, width = out_ref.shape
    for piece in range(ctx):
        place = piece % fold * (ctx // fold) + piece // fold
        out_ref[piece] = x_ref[:, place * width : (place + 1) * width]


def pack(value, ctx, shards, order, fold):
    rows, channels = value.shape
    width = channels // shards // ctx
    return pl.pallas_call(
        functools.partial(pack_kernel, order, fold),
        grid=(shards,),
        in_specs=[pl.BlockSpec((rows, ctx * width), lambda s: (0, order(s)))],
        out_specs=pl.BlockSpec((ctx, rows, width), lambda s: (0, 0, s)),
        out_shape=jax.ShapeDtypeStruct((ctx, rows, shards * width), value.dtype),
        name="pack",
    )(value)


def conv_select_kernel(lead_ref, seg_ref, x_ref, weight_ref, bias_ref, select_ref, conv_ref, part_ref, masks, padded, total):
    step = pl.program_id(0)
    toks = seg_ref.shape[0]
    width = x_ref.shape[2]
    pieces = x_ref.shape[0]
    rows = x_ref.shape[1]
    outputs = select_ref.shape[1]

    @pl.when(step == 0)
    def _():
        wide_seg = jnp.broadcast_to(seg_ref[...], (toks, LANES)).astype(jnp.float32)
        padded[0:SUBLANES, 0:LANES] = jnp.full((SUBLANES, LANES), -1.0, jnp.float32)
        padded[SUBLANES : SUBLANES + toks, 0:LANES] = wide_seg
        for tap in range(3):
            before = padded[SUBLANES - 3 + tap : SUBLANES - 3 + tap + toks, 0:LANES]
            masks[tap] = jnp.where(before == wide_seg, 1.0, 0.0)
        padded[0:SUBLANES, :] = jnp.zeros((SUBLANES, width), jnp.float32)
        total[...] = jnp.zeros_like(total)

    for piece in range(pieces):
        padded[SUBLANES + piece * rows : SUBLANES + (piece + 1) * rows, :] = x_ref[piece].astype(jnp.float32)
    outs = []
    for tile in range(width // LANES):
        lanes = slice(tile * LANES, (tile + 1) * LANES)
        running = jnp.broadcast_to(bias_ref[0:1, lanes], (toks, LANES))
        for tap in range(4):
            moved = padded[SUBLANES - 3 + tap : SUBLANES - 3 + tap + toks, lanes]
            term = weight_ref[tap : tap + 1, lanes] * moved
            running = running + (term * masks[tap] if tap < 3 else term)
        conv = silu(running).astype(jnp.bfloat16)
        conv_ref[:, lanes] = conv
        outs.append(conv)
    conv_all = jnp.concatenate(outs, axis=1) if len(outs) > 1 else outs[0]
    total[...] += lax.dot_general(
        conv_all, select_ref[0], (((1,), (1,)), ((), ())), preferred_element_type=jnp.float32
    )

    @pl.when(step == pl.num_programs(0) - 1)
    def _():
        spare = part_ref.shape[2] - outputs
        for piece in range(pieces):
            part_ref[piece, :, 0:outputs] = total[piece * rows : (piece + 1) * rows, :].astype(part_ref.dtype)
            part_ref[piece, :, outputs:] = jnp.zeros((rows, spare), part_ref.dtype)


def conv_select(lead, seg_col, pieces, conv_weight, conv_bias, select_parts, order):
    shards, outputs, width = select_parts.shape
    ctx, rows, _ = pieces.shape
    toks = ctx * rows
    padded_outputs = -(-outputs // LANES) * LANES
    return pl.pallas_call(
        conv_select_kernel,
        grid_spec=pltpu.PrefetchScalarGridSpec(
            num_scalar_prefetch=1,
            grid=(shards,),
            in_specs=[
                pl.BlockSpec((toks, 1), lambda s, p: (0, 0)),
                pl.BlockSpec((ctx, rows, width), lambda s, p: (0, 0, s)),
                pl.BlockSpec((4, width), lambda s, p: (0, order(s) * ctx + p[0])),
                pl.BlockSpec((1, width), lambda s, p: (0, order(s) * ctx + p[0])),
                pl.BlockSpec((1, outputs, width), lambda s, p: (s, 0, 0)),
            ],
            out_specs=[
                pl.BlockSpec((toks, width), lambda s, p: (0, s)),
                pl.BlockSpec((ctx, rows, padded_outputs), lambda s, p: (0, 0, 0)),
            ],
            scratch_shapes=[
                pltpu.VMEM((3, toks, LANES), jnp.float32),
                pltpu.VMEM((SUBLANES + toks, width), jnp.float32),
                pltpu.VMEM((toks, outputs), jnp.float32),
            ],
        ),
        out_shape=[
            jax.ShapeDtypeStruct((toks, shards * width), jnp.bfloat16),
            jax.ShapeDtypeStruct((ctx, rows, padded_outputs), jnp.bfloat16),
        ],
        compiler_params=pltpu.CompilerParams(vmem_limit_bytes=40 << 20),
        cost_estimate=pl.CostEstimate(
            flops=2 * toks * shards * width * outputs,
            bytes_accessed=2 * pieces.size * 2 + 2 * select_parts.size,
            transcendentals=pieces.size,
        ),
        name="conv_select",
    )(lead, seg_col, pieces, conv_weight, conv_bias, select_parts)


def normalise_kernel(rank, part_ref, out_ref):
    pieces = part_ref.shape[0]
    total = part_ref[0].astype(jnp.float32)
    for piece in range(1, pieces):
        total = total + part_ref[piece].astype(jnp.float32)
    low = total[:, :rank]
    scale = lax.rsqrt(jnp.mean(low * low, axis=-1, keepdims=True) + 1e-06)
    low = (low * scale).astype(out_ref.dtype)
    maps = total[:, rank:].astype(out_ref.dtype)
    for piece in range(pieces):
        out_ref[piece, :, :rank] = low
        out_ref[piece, :, rank:] = maps


def normalise(parts, rank):
    return pl.pallas_call(
        functools.partial(normalise_kernel, rank),
        out_shape=jax.ShapeDtypeStruct(parts.shape, jnp.bfloat16),
        name="normalise",
    )(parts)


def scan_kernel(rank, seg_ref, low_ref, weight_ref, bias_ref, decay_ref, gain_ref, conv_ref, out_ref,
                in_wide, out_diag, delta_rows, drive_rows, held_even, held_odd):
    toks = seg_ref.shape[0]
    states = decay_ref.shape[0]
    shards = weight_ref.shape[0]
    width = weight_ref.shape[2]
    tiles = shards * width // LANES
    rows = out_ref.shape[1]
    block = 16
    span = block * states

    for n in range(states):
        column = low_ref[:, rank + n : rank + n + 1].astype(jnp.float32)
        in_wide[:, n, :] = jnp.broadcast_to(column, (toks, LANES))
    lane = lax.broadcasted_iota(jnp.int32, (states, span), 1)
    spread = jnp.where(lane % states == lax.broadcasted_iota(jnp.int32, (states, span), 0), 1.0, 0.0)
    copies = jnp.dot(
        low_ref[:, rank + states : rank + 2 * states], spread.astype(jnp.bfloat16), preferred_element_type=jnp.float32
    )
    here = lax.broadcasted_iota(jnp.int32, (toks, span), 1) // states
    there = lax.broadcasted_iota(jnp.int32, (toks, span), 0) % block
    out_diag[...] = jnp.where(here == there, copies, 0.0).astype(jnp.bfloat16)

    seg = jnp.broadcast_to(seg_ref[...], (toks, LANES)).astype(jnp.float32)
    drive_rows[0, 0:SUBLANES, :] = jnp.full((SUBLANES, LANES), -1.0, jnp.float32)
    drive_rows[0, SUBLANES : SUBLANES + toks, :] = seg
    before = drive_rows[0, SUBLANES - 1 : SUBLANES - 1 + toks, :]
    reset = jnp.where(before == seg, 0.0, FAR)
    low = low_ref[:, 0:rank]
    for shard in range(shards):
        pre = jnp.dot(low, weight_ref[shard], preferred_element_type=jnp.float32)
        for part in range(width // LANES):
            tile = shard * (width // LANES) + part
            lanes = slice(tile * LANES, (tile + 1) * LANES)
            value = pre[:, part * LANES : (part + 1) * LANES] + bias_ref[:, lanes]
            raised = jnp.exp(-jnp.abs(value))
            log_part = jnp.where(
                raised < 0.01,
                raised * (1.0 - raised * (0.5 - raised * (1.0 / 3.0))),
                jnp.log(1.0 + raised),
            )
            delta = (jnp.maximum(value, 0.0) + log_part).astype(jnp.bfloat16).astype(jnp.float32)
            delta_rows[tile] = delta + reset
            drive_rows[tile, 0:toks, :] = delta * conv_ref[:, lanes].astype(jnp.float32)

    rates = [-LOG2E * jnp.exp(decay_ref[:, tile * LANES : (tile + 1) * LANES]) for tile in range(tiles)]

    def advance(index, held, history):
        held = list(held)
        for inner in range(block):
            t = index * block + inner
            into = in_wide[t]
            for tile in range(tiles):
                lanes = slice(tile * LANES, (tile + 1) * LANES)
                grow = jnp.exp2(delta_rows[tile, pl.ds(t, 1), :] * rates[tile])
                held[tile] = grow * held[tile] + into * drive_rows[tile, pl.ds(t, 1), :]
                history[inner * states : (inner + 1) * states, lanes] = held[tile].astype(jnp.bfloat16)
        return tuple(held)

    def finish(index, history):
        first = pl.multiple_of(index * block, block)
        mixed = jnp.dot(out_diag[pl.ds(first, block), :], history[...], preferred_element_type=jnp.float32)
        full = mixed + gain_ref[...] * conv_ref[pl.ds(first, block), :].astype(jnp.float32)
        place = pl.multiple_of(lax.rem(first, rows), block)
        out_ref[lax.div(first, rows), pl.ds(place, block), :] = full.astype(out_ref.dtype)

    held_odd[...] = jnp.zeros_like(held_odd)

    def pair(index, held):
        held = advance(2 * index, held, held_even)
        finish(jnp.maximum(2 * index - 1, 0), held_odd)
        held = advance(2 * index + 1, held, held_odd)
        finish(2 * index, held_even)
        return held

    start = tuple(jnp.zeros((states, LANES), jnp.float32) for _ in range(tiles))
    count = toks // block
    lax.fori_loop(0, count // 2, pair, start)
    finish(count - 1, held_odd)


def state_scan(seg_col, low, delta_parts, bias, decay, gain, conv, ctx, call, calls):
    toks = low.shape[0]
    shards, rank, width = delta_parts.shape
    shards = shards // calls
    states = decay.shape[0]
    rows = toks // ctx
    wide = shards * width
    steps = toks * wide * states
    return pl.pallas_call(
        functools.partial(scan_kernel, rank),
        grid=(1,),
        in_specs=[
            pl.BlockSpec((toks, 1), lambda g: (0, 0)),
            pl.BlockSpec(low.shape, lambda g: (0, 0)),
            pl.BlockSpec((shards, rank, width), lambda g: (call, 0, 0)),
            pl.BlockSpec((1, wide), lambda g: (0, call)),
            pl.BlockSpec((states, wide), lambda g: (0, call)),
            pl.BlockSpec((1, wide), lambda g: (0, call)),
            pl.BlockSpec((toks, wide), lambda g: (0, call)),
        ],
        out_specs=pl.BlockSpec((ctx, rows, wide), lambda g: (0, 0, 0)),
        out_shape=jax.ShapeDtypeStruct((ctx, rows, wide), jnp.bfloat16),
        scratch_shapes=[
            pltpu.VMEM((toks, states, LANES), jnp.float32),
            pltpu.VMEM((toks, 16 * states), jnp.bfloat16),
            pltpu.VMEM((wide // LANES, toks, LANES), jnp.float32),
            pltpu.VMEM((wide // LANES, toks + SUBLANES, LANES), jnp.float32),
            pltpu.VMEM((16 * states, wide), jnp.bfloat16),
            pltpu.VMEM((16 * states, wide), jnp.bfloat16),
        ],
        compiler_params=pltpu.CompilerParams(vmem_limit_bytes=56 << 20),
        cost_estimate=pl.CostEstimate(
            flops=6 * steps, bytes_accessed=2 * delta_parts.size // calls + 4 * toks * wide, transcendentals=steps
        ),
        name=f"state_scan_{call}",
    )(seg_col, low, delta_parts, bias, decay, gain, conv)


def gate_kernel(fold, y_ref, gate_ref, *refs):
    out_ref = refs[-1]
    ctx, _, width = y_ref.shape
    for piece in range(ctx):
        place = piece % fold * (ctx // fold) + piece // fold
        lanes = slice(place * width, (place + 1) * width)
        gate = gate_ref[:, lanes].astype(jnp.float32)
        out_ref[:, lanes] = (y_ref[piece].astype(jnp.float32) * silu(gate)).astype(out_ref.dtype)


def apply_gate(pieces, gate, width, order, fold, first, before=None):
    ctx, rows, total = pieces.shape
    wide = pl.BlockSpec((rows, ctx * width), lambda s: (0, order(first + s)))
    operands = [pieces, gate]
    in_specs = [pl.BlockSpec((ctx, rows, width), lambda s: (0, 0, s)), wide]
    aliases = {}
    if before is not None:
        aliases = {2: 0}
        operands.append(before)
        in_specs.append(pl.BlockSpec(memory_space=pl.ANY))
    return pl.pallas_call(
        functools.partial(gate_kernel, fold),
        grid=(total // width,),
        in_specs=in_specs,
        out_specs=wide,
        out_shape=jax.ShapeDtypeStruct(gate.shape, jnp.bfloat16),
        input_output_aliases=aliases,
        cost_estimate=pl.CostEstimate(
            flops=4 * pieces.size, bytes_accessed=6 * pieces.size, transcendentals=pieces.size
        ),
        name=f"gate_{first}",
    )(*operands)


def shifted(value, axis, by):
    size = lax.axis_size(axis)
    pairs = [(i, i + by) for i in range(size) if 0 <= i + by < size]
    return lax.ppermute(value, axis, pairs)


def exchange(value):
    return lax.all_to_all(value, "ctx", 0, 0, tiled=True)


def local(
    queries,
    keys,
    values,
    mixer_input,
    gate_input,
    segment_ids,
    conv_weight,
    conv_bias,
    select_weight,
    delta_weight,
    delta_bias,
    decay_log,
    skip_gain,
):
    ctx = lax.axis_size("ctx")
    shards = lax.axis_size("rep")
    place = lax.axis_index("ctx")
    rows, channels = mixer_input.shape[1:]
    rank = delta_weight.shape[0]
    states = decay_log.shape[1]
    width = max(channels // (shards * ctx), LANES)
    fold = width * shards * ctx // channels
    seg = segment_ids[0]
    toks = seg.shape[0]
    seg_col = seg[:, None]
    back = min(ctx - 1, -(-(toks // 2 - 1) // rows))

    slots = shards // fold
    half = slots // 2

    def order(slot):
        return slot % half * 2 + slot // half if fold == 1 else slot

    def own_part(array):
        cut = array.reshape(array.shape[:-1] + (slots, fold, ctx // fold, width))
        cut = lax.dynamic_index_in_dim(cut, place // fold, cut.ndim - 2, keepdims=False)
        cut = lax.dynamic_index_in_dim(cut, place % fold, cut.ndim - 2, keepdims=False)
        if fold == 1:
            cut = cut.reshape(array.shape[:-1] + (half, 2, width))
            cut = jnp.swapaxes(cut, -3, -2)
        return cut.reshape(array.shape[:-1] + (slots * width,))

    def gathered(weight):
        own = lax.dynamic_slice_in_dim(weight, place // fold * width, width, 1)
        if fold == 1:
            same_core = [list(range(core, shards, 2)) for core in range(2)]
            same_chip = [[chip, chip + 1] for chip in range(0, shards, 2)]
            parts = lax.all_gather(own, "rep", axis=0, axis_index_groups=same_core)
            return lax.all_gather(parts, "rep", axis=0, axis_index_groups=same_chip, tiled=True)
        parts = lax.all_gather(own, "rep", axis=0).reshape((slots, fold) + own.shape)
        return lax.dynamic_index_in_dim(parts, place % fold, 1, keepdims=False)

    select_parts = gathered(select_weight)
    delta_parts = gathered(delta_weight)

    both = jnp.concatenate([keys[0], values[0]], axis=1)
    blocks = [shifted(both, "ctx", by) for by in range(back, 0, -1)] + [both]

    pieces = exchange(pack(mixer_input[0], ctx, slots, order, fold))
    pieces, blocks = lax.optimization_barrier((pieces, blocks))

    lead = jnp.reshape(place % fold * (ctx // fold) + place // fold, (1,)).astype(jnp.int32)
    conv, parts = conv_select(lead, seg_col, pieces, conv_weight, conv_bias[None, :], select_parts, order)

    seg_pad = jnp.concatenate([jnp.full((back * rows,), -1, jnp.int32), seg])
    seg_k = lax.dynamic_slice_in_dim(seg_pad, place * rows, (back + 1) * rows, 0)
    seg_q = seg_k[back * rows :, None]
    parts, blocks = lax.optimization_barrier((parts, blocks))
    middle = KEY_VALUE_HEADS // 2
    attended = attention(queries[0], blocks, seg_q, seg_k[None, :], 0, middle)
    parts, attended = lax.optimization_barrier((exchange(parts), attended))
    low_own = normalise(parts, rank)
    low_own, attended = lax.optimization_barrier((low_own, attended))
    attended = attention(queries[0], blocks, seg_q, seg_k[None, :], middle, KEY_VALUE_HEADS, attended)
    low, attended = lax.optimization_barrier((exchange(low_own), attended))
    low = low.reshape(toks, low.shape[2])

    calls = 2
    bias = own_part(delta_bias)[None, :]
    gain = own_part(skip_gain)[None, :]
    decay = own_part(jnp.transpose(decay_log))
    scanned = [
        exchange(state_scan(seg_col, low, delta_parts, bias, decay, gain, conv, ctx, call, calls))
        for call in range(calls)
    ]
    mixed = None
    for call in range(calls):
        mixed = apply_gate(scanned[call], gate_input[0], width, order, fold, call * slots // calls, mixed)
    return (attended[None], mixed[None])


def solution(mesh):
    placed = (
        P("rep", "ctx", None),
        P("rep", "ctx", None),
        P("rep", "ctx", None),
        P("rep", "ctx", None),
        P("rep", "ctx", None),
        P("rep", None),
        P(),
        P(),
        P(None, "rep"),
        P(None, "rep"),
        P(),
        P(),
        P(),
    )
    return jax.shard_map(
        local,
        mesh=mesh,
        in_specs=placed,
        out_specs=(P("rep", "ctx", None), P("rep", "ctx", None)),
        check_vma=False,
    )
```

```python
import functools
import math

import jax
import jax.numpy as jnp
from jax import lax
from jax.experimental import pallas as pl
from jax.experimental.pallas import tpu as pltpu
from jax.sharding import PartitionSpec as P

QUERY_HEADS = 32
KEY_VALUE_HEADS = 4
HEAD_WIDTH = 128
LANES = 128
SUBLANES = 8
LOG2E = 1.0 / math.log(2.0)
FAR = 1e30


def silu(value):
    return 0.5 * value * (1.0 + jnp.tanh(0.5 * value))


def attention_kernel(begin, seg_q_ref, seg_k_ref, q_ref, *refs):
    out_ref = refs[-1]
    refs = refs[: -1 if begin == 0 else -2]
    rows = q_ref.shape[0]
    span = seg_k_ref.shape[1]
    groups = QUERY_HEADS // KEY_VALUE_HEADS
    row = lax.broadcasted_iota(jnp.int32, (rows, span), 0) + (span - rows)
    col = lax.broadcasted_iota(jnp.int32, (rows, span), 1)
    allowed = (col <= row) & (seg_q_ref[...] == seg_k_ref[...])
    shift = jnp.where(allowed, 0.0, -FAR)
    keys = jnp.concatenate([ref[...] for ref in refs[0::2]], axis=0)
    vals = jnp.concatenate([ref[...] for ref in refs[1::2]], axis=0)
    factor = LOG2E / math.sqrt(HEAD_WIDTH)
    batch = 4
    for first in range(0, groups, batch):
        cuts = [slice(head * HEAD_WIDTH, (head + 1) * HEAD_WIDTH) for head in range(first, first + batch)]
        scores = [
            lax.dot_general(q_ref[:, cut], keys, (((1,), (1,)), ((), ())), preferred_element_type=jnp.float32)
            for cut in cuts
        ]
        scores = [score + shift for score in scores]
        tops = [jnp.max(score, axis=-1, keepdims=True) for score in scores]
        weights = [jnp.exp2((score - top) * factor) for score, top in zip(scores, tops)]
        norms = [jnp.sum(weight, axis=-1, keepdims=True) for weight in weights]
        totals = [jnp.dot(weight.astype(jnp.bfloat16), vals, preferred_element_type=jnp.float32) for weight in weights]
        for cut, total, norm in zip(cuts, totals, norms):
            out_ref[:, cut] = (total / norm).astype(out_ref.dtype)


def attention(queries, blocks, seg_q, seg_k, begin, end, before=None):
    rows = queries.shape[0]
    span = seg_k.shape[1]
    group_width = QUERY_HEADS // KEY_VALUE_HEADS * HEAD_WIDTH
    key_spec = pl.BlockSpec((rows, HEAD_WIDTH), lambda h: (0, begin + h))
    value_spec = pl.BlockSpec((rows, HEAD_WIDTH), lambda h: (0, KEY_VALUE_HEADS + begin + h))
    wide = pl.BlockSpec((rows, group_width), lambda h: (0, begin + h))
    operands = [seg_q, seg_k, queries] + [block for block in blocks for _ in range(2)]
    in_specs = [
        pl.BlockSpec((rows, 1), lambda h: (0, 0)),
        pl.BlockSpec((1, span), lambda h: (0, 0)),
        wide,
        *([key_spec, value_spec] * len(blocks)),
    ]
    aliases = {}
    if before is not None:
        aliases = {len(operands): 0}
        operands.append(before)
        in_specs.append(pl.BlockSpec(memory_space=pl.ANY))
    return pl.pallas_call(
        functools.partial(attention_kernel, begin),
        grid=(end - begin,),
        in_specs=in_specs,
        out_specs=wide,
        out_shape=jax.ShapeDtypeStruct(queries.shape, jnp.bfloat16),
        input_output_aliases=aliases,
        compiler_params=pltpu.CompilerParams(vmem_limit_bytes=32 << 20),
        cost_estimate=pl.CostEstimate(
            flops=4 * rows * span * group_width * (end - begin),
            bytes_accessed=4 * rows * group_width * (end - begin),
            transcendentals=rows * span * group_width // HEAD_WIDTH * (end - begin),
        ),
        name=f"attention_{begin}",
    )(*operands)


def piece_lanes(slot, piece, ctx, fold, width):
    start = (slot * ctx + piece % fold * (ctx // fold) + piece // fold) * width
    return slice(start, start + width)


def pack_kernel(fold, width, x_ref, out_ref):
    ctx = out_ref.shape[0]
    for piece in range(ctx):
        for slot in range(out_ref.shape[2] // width):
            out_ref[piece, :, slot * width : (slot + 1) * width] = x_ref[:, piece_lanes(slot, piece, ctx, fold, width)]


def pack(value, ctx, fold, width):
    rows, channels = value.shape
    part = min(rows, 32)
    return pl.pallas_call(
        functools.partial(pack_kernel, fold, width),
        grid=(rows // part,),
        in_specs=[pl.BlockSpec((part, channels), lambda r: (r, 0))],
        out_specs=pl.BlockSpec((ctx, part, channels // ctx), lambda r: (0, r, 0)),
        out_shape=jax.ShapeDtypeStruct((ctx, rows, channels // ctx), value.dtype),
        name="pack",
    )(value)


def conv_select_kernel(seg_ref, x_ref, weight_ref, bias_ref, select_ref, conv_ref, part_ref, masks, padded, total):
    step = pl.program_id(0)
    toks = seg_ref.shape[0]
    pieces, rows, wide = x_ref.shape
    tiles = wide // LANES
    slots, outputs, width = select_ref.shape

    @pl.when(step == 0)
    def _():
        wide_seg = jnp.broadcast_to(seg_ref[...], (toks, LANES)).astype(jnp.float32)
        padded[0, 0:SUBLANES, :] = jnp.full((SUBLANES, LANES), -1.0, jnp.float32)
        padded[0, SUBLANES : SUBLANES + toks, :] = wide_seg
        for tap in range(3):
            before = padded[0, SUBLANES - 3 + tap : SUBLANES - 3 + tap + toks, :]
            masks[tap] = jnp.where(before == wide_seg, 1.0, 0.0)
        for tile in range(tiles):
            padded[tile, 0:SUBLANES, :] = jnp.zeros((SUBLANES, LANES), jnp.float32)
        total[...] = jnp.zeros_like(total)

    outs = []
    for tile in range(tiles):
        lanes = slice(tile * LANES, (tile + 1) * LANES)
        for piece in range(pieces):
            first = SUBLANES + piece * rows
            padded[tile, first : first + rows, :] = x_ref[piece, :, lanes].astype(jnp.float32)
        running = jnp.broadcast_to(bias_ref[0:1, lanes], (toks, LANES))
        for tap in range(4):
            moved = padded[tile, SUBLANES - 3 + tap : SUBLANES - 3 + tap + toks, :]
            term = weight_ref[tap : tap + 1, lanes] * moved
            running = running + (term * masks[tap] if tap < 3 else term)
        conv = silu(running).astype(jnp.bfloat16)
        conv_ref[:, lanes] = conv
        outs.append(conv)
    per_slot = width // LANES
    added = total[...]
    for slot in range(slots):
        conv = jnp.concatenate(outs[slot * per_slot : (slot + 1) * per_slot], axis=1) if per_slot > 1 else outs[slot]
        added = added + lax.dot_general(
            conv, select_ref[slot], (((1,), (1,)), ((), ())), preferred_element_type=jnp.float32
        )
    total[...] = added

    @pl.when(step == pl.num_programs(0) - 1)
    def _():
        spare = part_ref.shape[2] - outputs
        for piece in range(pieces):
            part_ref[piece, :, 0:outputs] = total[piece * rows : (piece + 1) * rows, :].astype(part_ref.dtype)
            part_ref[piece, :, outputs:] = jnp.zeros((rows, spare), part_ref.dtype)


def conv_select(seg_col, pieces, conv_weight, conv_bias, select_parts):
    slots, outputs, width = select_parts.shape
    ctx, rows, _ = pieces.shape
    toks = ctx * rows
    padded_outputs = -(-outputs // LANES) * LANES
    batch = 2
    wide = batch * width
    return pl.pallas_call(
        conv_select_kernel,
        grid=(slots // batch,),
        in_specs=[
            pl.BlockSpec((toks, 1), lambda s: (0, 0)),
            pl.BlockSpec((ctx, rows, wide), lambda s: (0, 0, s)),
            pl.BlockSpec((4, wide), lambda s: (0, s)),
            pl.BlockSpec((1, wide), lambda s: (0, s)),
            pl.BlockSpec((batch, outputs, width), lambda s: (s, 0, 0)),
        ],
        out_specs=[
            pl.BlockSpec((toks, wide), lambda s: (0, s)),
            pl.BlockSpec((ctx, rows, padded_outputs), lambda s: (0, 0, 0)),
        ],
        scratch_shapes=[
            pltpu.VMEM((3, toks, LANES), jnp.float32),
            pltpu.VMEM((wide // LANES, SUBLANES + toks, LANES), jnp.float32),
            pltpu.VMEM((toks, outputs), jnp.float32),
        ],
        out_shape=[
            jax.ShapeDtypeStruct((toks, slots * width), jnp.bfloat16),
            jax.ShapeDtypeStruct((ctx, rows, padded_outputs), jnp.bfloat16),
        ],
        compiler_params=pltpu.CompilerParams(vmem_limit_bytes=40 << 20),
        cost_estimate=pl.CostEstimate(
            flops=2 * toks * slots * width * outputs,
            bytes_accessed=2 * pieces.size * 2 + 2 * select_parts.size,
            transcendentals=pieces.size,
        ),
        name="conv_select",
    )(seg_col, pieces, conv_weight, conv_bias, select_parts)


def normalise_kernel(rank, part_ref, out_ref):
    pieces = part_ref.shape[0]
    total = part_ref[0].astype(jnp.float32)
    for piece in range(1, pieces):
        total = total + part_ref[piece].astype(jnp.float32)
    low = total[:, :rank]
    scale = lax.rsqrt(jnp.mean(low * low, axis=-1, keepdims=True) + 1e-06)
    low = (low * scale).astype(out_ref.dtype)
    maps = total[:, rank:].astype(out_ref.dtype)
    for piece in range(pieces):
        out_ref[piece, :, :rank] = low
        out_ref[piece, :, rank:] = maps


def normalise(parts, rank):
    return pl.pallas_call(
        functools.partial(normalise_kernel, rank),
        out_shape=jax.ShapeDtypeStruct(parts.shape, jnp.bfloat16),
        name="normalise",
    )(parts)


def scan_kernel(rank, reset_ref, low_ref, weight_ref, bias_ref, decay_ref, gain_ref, conv_ref, out_ref,
                in_cols, out_diag, delta_rows, drive_rows, held_even, held_odd):
    toks = reset_ref.shape[0]
    states = decay_ref.shape[0]
    shards = weight_ref.shape[0]
    width = weight_ref.shape[2]
    tiles = shards * width // LANES
    rows = out_ref.shape[1]
    block = 16
    span = block * states
    count = toks // block

    in_cols[...] = jnp.transpose(low_ref[:, rank : rank + LANES].astype(jnp.float32))[0:states, :]
    lane = lax.broadcasted_iota(jnp.int32, (states, span), 1)
    spread = jnp.where(lane % states == lax.broadcasted_iota(jnp.int32, (states, span), 0), 1.0, 0.0)
    copies = jnp.dot(
        low_ref[:, rank + states : rank + 2 * states], spread.astype(jnp.bfloat16), preferred_element_type=jnp.float32
    )
    here = lax.broadcasted_iota(jnp.int32, (toks, span), 1) // states
    there = lax.broadcasted_iota(jnp.int32, (toks, span), 0) % block
    out_diag[...] = jnp.where(here == there, copies, 0.0).astype(jnp.bfloat16)

    reset = jnp.broadcast_to(reset_ref[...], (toks, LANES))
    low = low_ref[:, 0:rank]
    for shard in range(shards):
        pre = jnp.dot(low, weight_ref[shard], preferred_element_type=jnp.float32)
        for part in range(width // LANES):
            tile = shard * (width // LANES) + part
            lanes = slice(tile * LANES, (tile + 1) * LANES)
            value = pre[:, part * LANES : (part + 1) * LANES] + bias_ref[:, lanes]
            raised = jnp.exp(-jnp.abs(value))
            log_part = jnp.where(
                raised < 0.01,
                raised * (1.0 - raised * (0.5 - raised * (1.0 / 3.0))),
                jnp.log(1.0 + raised),
            )
            delta = (jnp.maximum(value, 0.0) + log_part).astype(jnp.bfloat16).astype(jnp.float32)
            delta_rows[:, tile] = (delta + reset).reshape(count, block, LANES)
            drive_rows[:, tile] = (delta * conv_ref[:, lanes].astype(jnp.float32)).reshape(count, block, LANES)

    rates = [-LOG2E * jnp.exp(decay_ref[:, tile * LANES : (tile + 1) * LANES]) for tile in range(tiles)]

    def advance(index, held, history):
        held = list(held)
        per_row = LANES // block
        columns = in_cols[:, pl.ds(pl.multiple_of(lax.div(index, per_row) * LANES, LANES), LANES)]
        columns = pltpu.roll(columns, lax.rem(LANES - lax.rem(index, per_row) * block, LANES), 1)
        delta_now = delta_rows.at[index]
        drive_now = drive_rows.at[index]
        for inner in range(block):
            into = jnp.broadcast_to(columns[:, inner : inner + 1], (states, LANES))
            for tile in range(tiles):
                lanes = slice(tile * LANES, (tile + 1) * LANES)
                grow = jnp.exp2(delta_now[tile, inner : inner + 1, :] * rates[tile])
                held[tile] = grow * held[tile] + into * drive_now[tile, inner : inner + 1, :]
                history[inner * states : (inner + 1) * states, lanes] = held[tile].astype(jnp.bfloat16)
        return tuple(held)

    def finish(index, history):
        first = pl.multiple_of(index * block, block)
        mixed = jnp.dot(out_diag[pl.ds(first, block), :], history[...], preferred_element_type=jnp.float32)
        full = mixed + gain_ref[...] * conv_ref[pl.ds(first, block), :].astype(jnp.float32)
        place = pl.multiple_of(lax.rem(first, rows), block)
        out_ref[lax.div(first, rows), pl.ds(place, block), :] = full.astype(out_ref.dtype)

    held_odd[...] = jnp.zeros_like(held_odd)

    def pair(index, held):
        held = advance(2 * index, held, held_even)
        finish(jnp.maximum(2 * index - 1, 0), held_odd)
        held = advance(2 * index + 1, held, held_odd)
        finish(2 * index, held_even)
        return held

    start = tuple(jnp.zeros((states, LANES), jnp.float32) for _ in range(tiles))
    lax.fori_loop(0, count // 2, pair, start)
    finish(count - 1, held_odd)


def state_scan(reset_col, low, delta_parts, bias, decay, gain, conv, ctx, call, calls):
    toks = low.shape[0]
    shards, rank, width = delta_parts.shape
    shards = shards // calls
    states = decay.shape[0]
    rows = toks // ctx
    wide = shards * width
    steps = toks * wide * states
    return pl.pallas_call(
        functools.partial(scan_kernel, rank),
        grid=(1,),
        in_specs=[
            pl.BlockSpec((toks, 1), lambda g: (0, 0)),
            pl.BlockSpec(low.shape, lambda g: (0, 0)),
            pl.BlockSpec((shards, rank, width), lambda g: (call, 0, 0)),
            pl.BlockSpec((1, wide), lambda g: (0, call)),
            pl.BlockSpec((states, wide), lambda g: (0, call)),
            pl.BlockSpec((1, wide), lambda g: (0, call)),
            pl.BlockSpec((toks, wide), lambda g: (0, call)),
        ],
        out_specs=pl.BlockSpec((ctx, rows, wide), lambda g: (0, 0, 0)),
        out_shape=jax.ShapeDtypeStruct((ctx, rows, wide), jnp.bfloat16),
        scratch_shapes=[
            pltpu.VMEM((states, toks), jnp.float32),
            pltpu.VMEM((toks, 16 * states), jnp.bfloat16),
            pltpu.VMEM((toks // 16, wide // LANES, 16, LANES), jnp.float32),
            pltpu.VMEM((toks // 16, wide // LANES, 16, LANES), jnp.float32),
            pltpu.VMEM((16 * states, wide), jnp.bfloat16),
            pltpu.VMEM((16 * states, wide), jnp.bfloat16),
        ],
        compiler_params=pltpu.CompilerParams(vmem_limit_bytes=56 << 20),
        cost_estimate=pl.CostEstimate(
            flops=6 * steps, bytes_accessed=2 * delta_parts.size // calls + 4 * toks * wide, transcendentals=steps
        ),
        name=f"state_scan_{call}",
    )(reset_col, low, delta_parts, bias, decay, gain, conv)


def gate_kernel(fold, width, y_ref, gate_ref, *refs):
    out_ref = refs[-1]
    ctx, _, wide = y_ref.shape
    for slot in range(wide // width):
        for piece in range(ctx):
            lanes = piece_lanes(slot, piece, ctx, fold, width)
            value = y_ref[piece, :, slot * width : (slot + 1) * width].astype(jnp.float32)
            out_ref[:, lanes] = (value * silu(gate_ref[:, lanes].astype(jnp.float32))).astype(out_ref.dtype)


def apply_gate(pieces, gate, fold, width, call, before=None):
    ctx, rows, wide = pieces.shape
    part = min(rows, 32)
    columns = pl.BlockSpec((part, ctx * wide), lambda r: (r, call))
    operands = [pieces, gate]
    in_specs = [pl.BlockSpec((ctx, part, wide), lambda r: (0, r, 0)), columns]
    aliases = {}
    if before is not None:
        aliases = {2: 0}
        operands.append(before)
        in_specs.append(pl.BlockSpec(memory_space=pl.ANY))
    return pl.pallas_call(
        functools.partial(gate_kernel, fold, width),
        grid=(rows // part,),
        in_specs=in_specs,
        out_specs=columns,
        out_shape=jax.ShapeDtypeStruct(gate.shape, jnp.bfloat16),
        input_output_aliases=aliases,
        cost_estimate=pl.CostEstimate(
            flops=4 * pieces.size, bytes_accessed=6 * pieces.size, transcendentals=pieces.size
        ),
        name=f"gate_{call}",
    )(*operands)


def shifted(value, axis, by):
    size = lax.axis_size(axis)
    pairs = [(i, i + by) for i in range(size) if 0 <= i + by < size]
    return lax.ppermute(value, axis, pairs)


def exchange(value):
    return lax.all_to_all(value, "ctx", 0, 0, tiled=True)


def local(
    queries,
    keys,
    values,
    mixer_input,
    gate_input,
    segment_ids,
    conv_weight,
    conv_bias,
    select_weight,
    delta_weight,
    delta_bias,
    decay_log,
    skip_gain,
):
    ctx = lax.axis_size("ctx")
    shards = lax.axis_size("rep")
    place = lax.axis_index("ctx")
    rows, channels = mixer_input.shape[1:]
    rank = delta_weight.shape[0]
    states = decay_log.shape[1]
    width = max(channels // (shards * ctx), LANES)
    fold = width * shards * ctx // channels
    seg = segment_ids[0]
    toks = seg.shape[0]
    seg_col = seg[:, None]
    back = min(ctx - 1, -(-(toks // 2 - 1) // rows))

    slots = shards // fold

    def own_part(array):
        cut = array.reshape(array.shape[:-1] + (slots, fold, ctx // fold, width))
        cut = lax.dynamic_index_in_dim(cut, place // fold, cut.ndim - 2, keepdims=False)
        cut = lax.dynamic_index_in_dim(cut, place % fold, cut.ndim - 2, keepdims=False)
        return cut.reshape(array.shape[:-1] + (slots * width,))

    def gathered(weight):
        own = lax.dynamic_slice_in_dim(weight, place // fold * width, width, 1)
        parts = lax.all_gather(own, "rep", axis=0)
        if fold > 1:
            parts = parts.reshape((slots, fold) + own.shape)
            parts = lax.dynamic_index_in_dim(parts, place % fold, 1, keepdims=False)
        return parts

    select_parts = gathered(select_weight)
    delta_parts = gathered(delta_weight)

    both = jnp.concatenate([keys[0], values[0]], axis=1)
    blocks = [shifted(both, "ctx", by) for by in range(back, 0, -1)] + [both]

    pieces = exchange(pack(mixer_input[0], ctx, fold, width))
    pieces, blocks = lax.optimization_barrier((pieces, blocks))

    conv, parts = conv_select(seg_col, pieces, own_part(conv_weight), own_part(conv_bias)[None, :], select_parts)

    seg_pad = jnp.concatenate([jnp.full((back * rows,), -1, jnp.int32), seg])
    seg_k = lax.dynamic_slice_in_dim(seg_pad, place * rows, (back + 1) * rows, 0)
    seg_q = seg_k[back * rows :, None]
    parts, blocks = lax.optimization_barrier((parts, blocks))
    middle = KEY_VALUE_HEADS // 2
    attended = attention(queries[0], blocks, seg_q, seg_k[None, :], 0, middle)
    parts, attended = lax.optimization_barrier((exchange(parts), attended))
    low_own = normalise(parts, rank)
    low_own, attended = lax.optimization_barrier((low_own, attended))
    attended = attention(queries[0], blocks, seg_q, seg_k[None, :], middle, KEY_VALUE_HEADS, attended)
    low, attended = lax.optimization_barrier((exchange(low_own), attended))
    low = low.reshape(toks, low.shape[2])

    calls = 2
    bias = own_part(delta_bias)[None, :]
    gain = own_part(skip_gain)[None, :]
    decay = own_part(jnp.transpose(decay_log))
    same = jnp.concatenate([jnp.zeros((1,), bool), seg[1:] == seg[:-1]])
    reset_col = jnp.where(same, 0.0, FAR)[:, None]
    scanned = [
        exchange(state_scan(reset_col, low, delta_parts, bias, decay, gain, conv, ctx, call, calls))
        for call in range(calls)
    ]
    mixed = None
    for call in range(calls):
        mixed = apply_gate(scanned[call], gate_input[0], fold, width, call, mixed)
    return (attended[None], mixed[None])


def solution(mesh):
    placed = (
        P("rep", "ctx", None),
        P("rep", "ctx", None),
        P("rep", "ctx", None),
        P("rep", "ctx", None),
        P("rep", "ctx", None),
        P("rep", None),
        P(),
        P(),
        P(None, "rep"),
        P(None, "rep"),
        P(),
        P(),
        P(),
    )
    return jax.shard_map(
        local,
        mesh=mesh,
        in_specs=placed,
        out_specs=(P("rep", "ctx", None), P("rep", "ctx", None)),
        check_vma=False,
    )
```

```python
import functools
import math

import jax
import jax.numpy as jnp
from jax import lax
from jax.experimental import pallas as pl
from jax.experimental.pallas import tpu as pltpu
from jax.sharding import PartitionSpec as P

QUERY_HEADS = 32
KEY_VALUE_HEADS = 4
HEAD_WIDTH = 128
LANES = 128
SUBLANES = 8
LOG2E = 1.0 / math.log(2.0)
FAR = 1e30


def silu(value):
    return 0.5 * value * (1.0 + jnp.tanh(0.5 * value))


def attention_kernel(begin, seg_q_ref, seg_k_ref, q_ref, *refs):
    out_ref = refs[-1]
    refs = refs[: -1 if begin == 0 else -2]
    rows = q_ref.shape[0]
    span = seg_k_ref.shape[1]
    groups = QUERY_HEADS // KEY_VALUE_HEADS
    row = lax.broadcasted_iota(jnp.int32, (rows, span), 0) + (span - rows)
    col = lax.broadcasted_iota(jnp.int32, (rows, span), 1)
    allowed = (col <= row) & (seg_q_ref[...] == seg_k_ref[...])
    shift = jnp.where(allowed, 0.0, -FAR)
    keys = jnp.concatenate([ref[...] for ref in refs[0::2]], axis=0)
    vals = jnp.concatenate([ref[...] for ref in refs[1::2]], axis=0)
    factor = LOG2E / math.sqrt(HEAD_WIDTH)
    batch = 4
    for first in range(0, groups, batch):
        cuts = [slice(head * HEAD_WIDTH, (head + 1) * HEAD_WIDTH) for head in range(first, first + batch)]
        scores = [
            lax.dot_general(q_ref[:, cut], keys, (((1,), (1,)), ((), ())), preferred_element_type=jnp.float32)
            for cut in cuts
        ]
        scores = [score + shift for score in scores]
        tops = [jnp.max(score, axis=-1, keepdims=True) for score in scores]
        weights = [jnp.exp2((score - top) * factor) for score, top in zip(scores, tops)]
        norms = [jnp.sum(weight, axis=-1, keepdims=True) for weight in weights]
        totals = [jnp.dot(weight.astype(jnp.bfloat16), vals, preferred_element_type=jnp.float32) for weight in weights]
        for cut, total, norm in zip(cuts, totals, norms):
            out_ref[:, cut] = (total / norm).astype(out_ref.dtype)


def attention(queries, blocks, seg_q, seg_k, begin, end, before=None):
    rows = queries.shape[0]
    span = seg_k.shape[1]
    group_width = QUERY_HEADS // KEY_VALUE_HEADS * HEAD_WIDTH
    key_spec = pl.BlockSpec((rows, HEAD_WIDTH), lambda h: (0, begin + h))
    value_spec = pl.BlockSpec((rows, HEAD_WIDTH), lambda h: (0, KEY_VALUE_HEADS + begin + h))
    wide = pl.BlockSpec((rows, group_width), lambda h: (0, begin + h))
    operands = [seg_q, seg_k, queries] + [block for block in blocks for _ in range(2)]
    in_specs = [
        pl.BlockSpec((rows, 1), lambda h: (0, 0)),
        pl.BlockSpec((1, span), lambda h: (0, 0)),
        wide,
        *([key_spec, value_spec] * len(blocks)),
    ]
    aliases = {}
    if before is not None:
        aliases = {len(operands): 0}
        operands.append(before)
        in_specs.append(pl.BlockSpec(memory_space=pl.ANY))
    return pl.pallas_call(
        functools.partial(attention_kernel, begin),
        grid=(end - begin,),
        in_specs=in_specs,
        out_specs=wide,
        out_shape=jax.ShapeDtypeStruct(queries.shape, jnp.bfloat16),
        input_output_aliases=aliases,
        compiler_params=pltpu.CompilerParams(vmem_limit_bytes=16 << 20),
        cost_estimate=pl.CostEstimate(
            flops=4 * rows * span * group_width * (end - begin),
            bytes_accessed=4 * rows * group_width * (end - begin),
            transcendentals=rows * span * group_width // HEAD_WIDTH * (end - begin),
        ),
        name=f"attention_{begin}",
    )(*operands)


def piece_lanes(slot, piece, ctx, fold, width):
    start = (slot * ctx + piece % fold * (ctx // fold) + piece // fold) * width
    return slice(start, start + width)


def pack_kernel(fold, width, x_ref, out_ref):
    ctx = out_ref.shape[0]
    for piece in range(ctx):
        for slot in range(out_ref.shape[2] // width):
            out_ref[piece, :, slot * width : (slot + 1) * width] = x_ref[:, piece_lanes(slot, piece, ctx, fold, width)]


def pack(value, ctx, fold, width):
    rows, channels = value.shape
    part = min(rows, 32)
    return pl.pallas_call(
        functools.partial(pack_kernel, fold, width),
        grid=(rows // part,),
        in_specs=[pl.BlockSpec((part, channels), lambda r: (r, 0))],
        out_specs=pl.BlockSpec((ctx, part, channels // ctx), lambda r: (0, r, 0)),
        out_shape=jax.ShapeDtypeStruct((ctx, rows, channels // ctx), value.dtype),
        compiler_params=pltpu.CompilerParams(vmem_limit_bytes=12 << 20),
        name="pack",
    )(value)


def conv_select_kernel(seg_ref, x_ref, weight_ref, bias_ref, select_ref, conv_ref, part_ref, masks, padded, total):
    step = pl.program_id(0)
    toks = seg_ref.shape[0]
    pieces, rows, wide = x_ref.shape
    tiles = wide // LANES
    slots, outputs, width = select_ref.shape

    @pl.when(step == 0)
    def _():
        wide_seg = jnp.broadcast_to(seg_ref[...], (toks, LANES)).astype(jnp.float32)
        padded[0, 0:SUBLANES, :] = jnp.full((SUBLANES, LANES), -1.0, jnp.float32)
        padded[0, SUBLANES : SUBLANES + toks, :] = wide_seg
        for tap in range(3):
            before = padded[0, SUBLANES - 3 + tap : SUBLANES - 3 + tap + toks, :]
            masks[tap] = jnp.where(before == wide_seg, 1.0, 0.0)
        for tile in range(tiles):
            padded[tile, 0:SUBLANES, :] = jnp.zeros((SUBLANES, LANES), jnp.float32)
        total[...] = jnp.zeros_like(total)

    outs = []
    for tile in range(tiles):
        lanes = slice(tile * LANES, (tile + 1) * LANES)
        for piece in range(pieces):
            first = SUBLANES + piece * rows
            padded[tile, first : first + rows, :] = x_ref[piece, :, lanes].astype(jnp.float32)
        running = jnp.broadcast_to(bias_ref[0:1, lanes], (toks, LANES))
        for tap in range(4):
            moved = padded[tile, SUBLANES - 3 + tap : SUBLANES - 3 + tap + toks, :]
            term = weight_ref[tap : tap + 1, lanes] * moved
            running = running + (term * masks[tap] if tap < 3 else term)
        conv = silu(running).astype(jnp.bfloat16)
        conv_ref[:, lanes] = conv
        outs.append(conv)
    per_slot = width // LANES
    added = total[...]
    for slot in range(slots):
        conv = jnp.concatenate(outs[slot * per_slot : (slot + 1) * per_slot], axis=1) if per_slot > 1 else outs[slot]
        added = added + lax.dot_general(
            conv, select_ref[slot], (((1,), (1,)), ((), ())), preferred_element_type=jnp.float32
        )
    total[...] = added

    @pl.when(step == pl.num_programs(0) - 1)
    def _():
        spare = part_ref.shape[2] - outputs
        for piece in range(pieces):
            part_ref[piece, :, 0:outputs] = total[piece * rows : (piece + 1) * rows, :].astype(part_ref.dtype)
            part_ref[piece, :, outputs:] = jnp.zeros((rows, spare), part_ref.dtype)


def conv_select(seg_col, pieces, conv_weight, conv_bias, select_parts):
    slots, outputs, width = select_parts.shape
    ctx, rows, _ = pieces.shape
    toks = ctx * rows
    padded_outputs = -(-outputs // LANES) * LANES
    batch = 2
    wide = batch * width
    return pl.pallas_call(
        conv_select_kernel,
        grid=(slots // batch,),
        in_specs=[
            pl.BlockSpec((toks, 1), lambda s: (0, 0)),
            pl.BlockSpec((ctx, rows, wide), lambda s: (0, 0, s)),
            pl.BlockSpec((4, wide), lambda s: (0, s)),
            pl.BlockSpec((1, wide), lambda s: (0, s)),
            pl.BlockSpec((batch, outputs, width), lambda s: (s, 0, 0)),
        ],
        out_specs=[
            pl.BlockSpec((toks, wide), lambda s: (0, s)),
            pl.BlockSpec((ctx, rows, padded_outputs), lambda s: (0, 0, 0)),
        ],
        scratch_shapes=[
            pltpu.VMEM((3, toks, LANES), jnp.float32),
            pltpu.VMEM((wide // LANES, SUBLANES + toks, LANES), jnp.float32),
            pltpu.VMEM((toks, outputs), jnp.float32),
        ],
        out_shape=[
            jax.ShapeDtypeStruct((toks, slots * width), jnp.bfloat16),
            jax.ShapeDtypeStruct((ctx, rows, padded_outputs), jnp.bfloat16),
        ],
        compiler_params=pltpu.CompilerParams(vmem_limit_bytes=20 << 20),
        cost_estimate=pl.CostEstimate(
            flops=2 * toks * slots * width * outputs,
            bytes_accessed=2 * pieces.size * 2 + 2 * select_parts.size,
            transcendentals=pieces.size,
        ),
        name="conv_select",
    )(seg_col, pieces, conv_weight, conv_bias, select_parts)


def normalise_kernel(rank, part_ref, out_ref):
    pieces = part_ref.shape[0]
    total = part_ref[0].astype(jnp.float32)
    for piece in range(1, pieces):
        total = total + part_ref[piece].astype(jnp.float32)
    low = total[:, :rank]
    scale = lax.rsqrt(jnp.mean(low * low, axis=-1, keepdims=True) + 1e-06)
    low = (low * scale).astype(out_ref.dtype)
    maps = total[:, rank:].astype(out_ref.dtype)
    for piece in range(pieces):
        out_ref[piece, :, :rank] = low
        out_ref[piece, :, rank:] = maps


def normalise(parts, rank):
    return pl.pallas_call(
        functools.partial(normalise_kernel, rank),
        out_shape=jax.ShapeDtypeStruct(parts.shape, jnp.bfloat16),
        compiler_params=pltpu.CompilerParams(vmem_limit_bytes=12 << 20),
        name="normalise",
    )(parts)


def scan_kernel(rank, reset_ref, low_ref, weight_ref, bias_ref, decay_ref, gain_ref, conv_ref, out_ref,
                in_cols, out_diag, delta_rows, drive_rows, held_even, held_odd):
    toks = reset_ref.shape[0]
    states = decay_ref.shape[0]
    shards = weight_ref.shape[0]
    width = weight_ref.shape[2]
    tiles = shards * width // LANES
    rows = out_ref.shape[1]
    block = 16
    span = block * states
    count = toks // block

    in_cols[...] = jnp.transpose(low_ref[:, rank : rank + LANES].astype(jnp.float32))[0:states, :]
    lane = lax.broadcasted_iota(jnp.int32, (states, span), 1)
    spread = jnp.where(lane % states == lax.broadcasted_iota(jnp.int32, (states, span), 0), 1.0, 0.0)
    copies = jnp.dot(
        low_ref[:, rank + states : rank + 2 * states], spread.astype(jnp.bfloat16), preferred_element_type=jnp.float32
    )
    here = lax.broadcasted_iota(jnp.int32, (toks, span), 1) // states
    there = lax.broadcasted_iota(jnp.int32, (toks, span), 0) % block
    out_diag[...] = jnp.where(here == there, copies, 0.0).astype(jnp.bfloat16)

    reset = jnp.broadcast_to(reset_ref[...], (toks, LANES))
    low = low_ref[:, 0:rank]
    for shard in range(shards):
        pre = jnp.dot(low, weight_ref[shard], preferred_element_type=jnp.float32)
        for part in range(width // LANES):
            tile = shard * (width // LANES) + part
            lanes = slice(tile * LANES, (tile + 1) * LANES)
            value = pre[:, part * LANES : (part + 1) * LANES] + bias_ref[:, lanes]
            raised = jnp.exp(-jnp.abs(value))
            log_part = jnp.where(
                raised < 0.01,
                raised * (1.0 - raised * (0.5 - raised * (1.0 / 3.0))),
                jnp.log(1.0 + raised),
            )
            delta = (jnp.maximum(value, 0.0) + log_part).astype(jnp.bfloat16).astype(jnp.float32)
            delta_rows[:, tile] = (delta + reset).reshape(count, block, LANES)
            drive_rows[:, tile] = (delta * conv_ref[:, lanes].astype(jnp.float32)).reshape(count, block, LANES)

    rates = [-LOG2E * jnp.exp(decay_ref[:, tile * LANES : (tile + 1) * LANES]) for tile in range(tiles)]

    quarter = min(2 * LANES, tiles * LANES)
    quarters = tiles * LANES // quarter

    def finish(index, history, part):
        first = pl.multiple_of(index * block, block)
        lanes = slice(part * quarter, (part + 1) * quarter)
        mixed = jnp.dot(out_diag[pl.ds(first, block), :], history[:, lanes], preferred_element_type=jnp.float32)
        full = mixed + gain_ref[:, lanes] * conv_ref[pl.ds(first, block), lanes].astype(jnp.float32)
        place = pl.multiple_of(lax.rem(first, rows), block)
        out_ref[lax.div(first, rows), pl.ds(place, block), lanes] = full.astype(out_ref.dtype)

    def advance(index, held, history, before, before_history):
        held = list(held)
        per_row = LANES // block
        columns = in_cols[:, pl.ds(pl.multiple_of(lax.div(index, per_row) * LANES, LANES), LANES)]
        columns = pltpu.roll(columns, lax.rem(LANES - lax.rem(index, per_row) * block, LANES), 1)
        delta_now = delta_rows.at[index]
        drive_now = drive_rows.at[index]
        for inner in range(block):
            into = jnp.broadcast_to(columns[:, inner : inner + 1], (states, LANES))
            for tile in range(tiles):
                lanes = slice(tile * LANES, (tile + 1) * LANES)
                grow = jnp.exp2(delta_now[tile, inner : inner + 1, :] * rates[tile])
                held[tile] = grow * held[tile] + into * drive_now[tile, inner : inner + 1, :]
                history[inner * states : (inner + 1) * states, lanes] = held[tile].astype(jnp.bfloat16)
            if inner % (block // quarters) == 0:
                finish(before, before_history, inner // (block // quarters))
        return tuple(held)

    held_odd[...] = jnp.zeros_like(held_odd)

    def pair(index, held):
        held = advance(2 * index, held, held_even, jnp.maximum(2 * index - 1, 0), held_odd)
        return advance(2 * index + 1, held, held_odd, 2 * index, held_even)

    start = tuple(jnp.zeros((states, LANES), jnp.float32) for _ in range(tiles))
    lax.fori_loop(0, count // 2, pair, start)
    for part in range(quarters):
        finish(count - 1, held_odd, part)


def state_scan(reset_col, low, delta_parts, bias, decay, gain, conv, ctx, call, calls):
    toks = low.shape[0]
    shards, rank, width = delta_parts.shape
    shards = shards // calls
    states = decay.shape[0]
    rows = toks // ctx
    wide = shards * width
    steps = toks * wide * states
    return pl.pallas_call(
        functools.partial(scan_kernel, rank),
        grid=(1,),
        in_specs=[
            pl.BlockSpec((toks, 1), lambda g: (0, 0)),
            pl.BlockSpec(low.shape, lambda g: (0, 0)),
            pl.BlockSpec((shards, rank, width), lambda g: (call, 0, 0)),
            pl.BlockSpec((1, wide), lambda g: (0, call)),
            pl.BlockSpec((states, wide), lambda g: (0, call)),
            pl.BlockSpec((1, wide), lambda g: (0, call)),
            pl.BlockSpec((toks, wide), lambda g: (0, call)),
        ],
        out_specs=pl.BlockSpec((ctx, rows, wide), lambda g: (0, 0, 0)),
        out_shape=jax.ShapeDtypeStruct((ctx, rows, wide), jnp.bfloat16),
        scratch_shapes=[
            pltpu.VMEM((states, toks), jnp.float32),
            pltpu.VMEM((toks, 16 * states), jnp.bfloat16),
            pltpu.VMEM((toks // 16, wide // LANES, 16, LANES), jnp.float32),
            pltpu.VMEM((toks // 16, wide // LANES, 16, LANES), jnp.float32),
            pltpu.VMEM((16 * states, wide), jnp.bfloat16),
            pltpu.VMEM((16 * states, wide), jnp.bfloat16),
        ],
        compiler_params=pltpu.CompilerParams(vmem_limit_bytes=24 << 20),
        cost_estimate=pl.CostEstimate(
            flops=6 * steps, bytes_accessed=2 * delta_parts.size // calls + 4 * toks * wide, transcendentals=steps
        ),
        name=f"state_scan_{call}",
    )(reset_col, low, delta_parts, bias, decay, gain, conv)


def gate_kernel(fold, width, y_ref, gate_ref, *refs):
    out_ref = refs[-1]
    ctx, _, wide = y_ref.shape
    for slot in range(wide // width):
        for piece in range(ctx):
            lanes = piece_lanes(slot, piece, ctx, fold, width)
            value = y_ref[piece, :, slot * width : (slot + 1) * width].astype(jnp.float32)
            out_ref[:, lanes] = (value * silu(gate_ref[:, lanes].astype(jnp.float32))).astype(out_ref.dtype)


def apply_gate(pieces, gate, fold, width, call, before=None):
    ctx, rows, wide = pieces.shape
    part = min(rows, 32)
    columns = pl.BlockSpec((part, ctx * wide), lambda r: (r, call))
    operands = [pieces, gate]
    in_specs = [pl.BlockSpec((ctx, part, wide), lambda r: (0, r, 0)), columns]
    aliases = {}
    if before is not None:
        aliases = {2: 0}
        operands.append(before)
        in_specs.append(pl.BlockSpec(memory_space=pl.ANY))
    return pl.pallas_call(
        functools.partial(gate_kernel, fold, width),
        grid=(rows // part,),
        in_specs=in_specs,
        out_specs=columns,
        out_shape=jax.ShapeDtypeStruct(gate.shape, jnp.bfloat16),
        input_output_aliases=aliases,
        compiler_params=pltpu.CompilerParams(vmem_limit_bytes=12 << 20),
        cost_estimate=pl.CostEstimate(
            flops=4 * pieces.size, bytes_accessed=6 * pieces.size, transcendentals=pieces.size
        ),
        name=f"gate_{call}",
    )(*operands)


def shifted(value, axis, by):
    size = lax.axis_size(axis)
    pairs = [(i, i + by) for i in range(size) if 0 <= i + by < size]
    return lax.ppermute(value, axis, pairs)


def exchange(value):
    return lax.all_to_all(value, "ctx", 0, 0, tiled=True)


def local(
    queries,
    keys,
    values,
    mixer_input,
    gate_input,
    segment_ids,
    conv_weight,
    conv_bias,
    select_weight,
    delta_weight,
    delta_bias,
    decay_log,
    skip_gain,
):
    ctx = lax.axis_size("ctx")
    shards = lax.axis_size("rep")
    place = lax.axis_index("ctx")
    rows, channels = mixer_input.shape[1:]
    rank = delta_weight.shape[0]
    states = decay_log.shape[1]
    width = max(channels // (shards * ctx), LANES)
    fold = width * shards * ctx // channels
    seg = segment_ids[0]
    toks = seg.shape[0]
    seg_col = seg[:, None]
    back = min(ctx - 1, -(-(toks // 2 - 1) // rows))

    slots = shards // fold

    def own_part(array):
        cut = array.reshape(array.shape[:-1] + (slots, fold, ctx // fold, width))
        cut = lax.dynamic_index_in_dim(cut, place // fold, cut.ndim - 2, keepdims=False)
        cut = lax.dynamic_index_in_dim(cut, place % fold, cut.ndim - 2, keepdims=False)
        return cut.reshape(array.shape[:-1] + (slots * width,))

    def gathered(weight):
        own = lax.dynamic_slice_in_dim(weight, place // fold * width, width, 1)
        parts = lax.all_gather(own, "rep", axis=0)
        if fold > 1:
            parts = parts.reshape((slots, fold) + own.shape)
            parts = lax.dynamic_index_in_dim(parts, place % fold, 1, keepdims=False)
        return parts

    select_parts = gathered(select_weight)
    packed = pack(mixer_input[0], ctx, fold, width)
    packed, delta_weight = lax.optimization_barrier((packed, delta_weight))
    delta_parts = gathered(delta_weight)

    same = jnp.concatenate([jnp.zeros((1,), bool), seg[1:] == seg[:-1]])
    reset_col = jnp.where(same, 0.0, FAR)[:, None]
    seg_pad = jnp.concatenate([jnp.full((back * rows,), -1, jnp.int32), seg])
    seg_k = lax.dynamic_slice_in_dim(seg_pad, place * rows, (back + 1) * rows, 0)
    own = (
        own_part(delta_bias)[None, :],
        own_part(jnp.transpose(decay_log)),
        own_part(skip_gain)[None, :],
        reset_col,
        seg_k[back * rows :, None],
        seg_k[None, :],
        jnp.concatenate([keys[0], values[0]], axis=1),
    )
    pieces, own = lax.optimization_barrier((exchange(packed), own))
    bias, decay, gain, reset_col, seg_q, seg_k, both = own

    conv, parts = conv_select(seg_col, pieces, own_part(conv_weight), own_part(conv_bias)[None, :], select_parts)
    low = normalise(exchange(parts), rank)

    low, both = lax.optimization_barrier((low, both))
    blocks = [shifted(both, "ctx", by) for by in range(back, 0, -1)] + [both]
    low = exchange(low).reshape(toks, low.shape[2])

    calls = 2
    scanned = []
    for call in range(calls):
        scanned.append(state_scan(reset_col, low, delta_parts, bias, decay, gain, conv, ctx, call, calls))
    scanned[-1], blocks = lax.optimization_barrier((scanned[-1], blocks))
    attended = attention(queries[0], blocks, seg_q, seg_k, 0, KEY_VALUE_HEADS)
    scanned = [exchange(part) for part in scanned]
    scanned[-1], attended = lax.optimization_barrier((scanned[-1], attended))
    mixed = None
    for call in range(calls):
        mixed = apply_gate(scanned[call], gate_input[0], fold, width, call, mixed)
    return (attended[None], mixed[None])


def solution(mesh):
    placed = (
        P("rep", "ctx", None),
        P("rep", "ctx", None),
        P("rep", "ctx", None),
        P("rep", "ctx", None),
        P("rep", "ctx", None),
        P("rep", None),
        P(),
        P(),
        P(None, "rep"),
        P(None, "rep"),
        P(),
        P(),
        P(),
    )
    return jax.shard_map(
        local,
        mesh=mesh,
        in_specs=placed,
        out_specs=(P("rep", "ctx", None), P("rep", "ctx", None)),
        check_vma=False,
    )
```

```python
import functools
import math

import jax
import jax.numpy as jnp
from jax import lax
from jax.experimental import pallas as pl
from jax.experimental.pallas import tpu as pltpu
from jax.sharding import PartitionSpec as P

QUERY_HEADS = 32
KEY_VALUE_HEADS = 4
HEAD_WIDTH = 128
LANES = 128
SUBLANES = 8
LOG2E = 1.0 / math.log(2.0)
FAR = 1e30


def silu(value):
    half = 0.5 * value
    return half + half * jnp.tanh(half)


def attention_kernel(begin, seg_q_ref, seg_k_ref, q_ref, *refs):
    out_ref = refs[-1]
    refs = refs[: -1 if begin == 0 else -2]
    rows = q_ref.shape[0]
    span = seg_k_ref.shape[1]
    groups = QUERY_HEADS // KEY_VALUE_HEADS
    row = lax.broadcasted_iota(jnp.int32, (rows, span), 0) + (span - rows)
    col = lax.broadcasted_iota(jnp.int32, (rows, span), 1)
    allowed = (col <= row) & (seg_q_ref[...] == seg_k_ref[...])
    shift = jnp.where(allowed, 0.0, -FAR)
    keys = jnp.concatenate([ref[...] for ref in refs[0::2]], axis=0)
    vals = jnp.concatenate([ref[...] for ref in refs[1::2]], axis=0)
    factor = LOG2E / math.sqrt(HEAD_WIDTH)
    batch = 4
    for first in range(0, groups, batch):
        cuts = [slice(head * HEAD_WIDTH, (head + 1) * HEAD_WIDTH) for head in range(first, first + batch)]
        scores = [
            lax.dot_general(q_ref[:, cut], keys, (((1,), (1,)), ((), ())), preferred_element_type=jnp.float32)
            for cut in cuts
        ]
        scores = [score + shift for score in scores]
        tops = [jnp.max(score, axis=-1, keepdims=True) for score in scores]
        weights = [jnp.exp2((score - top) * factor) for score, top in zip(scores, tops)]
        norms = [jnp.sum(weight, axis=-1, keepdims=True) for weight in weights]
        totals = [jnp.dot(weight.astype(jnp.bfloat16), vals, preferred_element_type=jnp.float32) for weight in weights]
        for cut, total, norm in zip(cuts, totals, norms):
            out_ref[:, cut] = (total / norm).astype(out_ref.dtype)


def attention(queries, blocks, seg_q, seg_k, begin, end, before=None):
    rows = queries.shape[0]
    span = seg_k.shape[1]
    group_width = QUERY_HEADS // KEY_VALUE_HEADS * HEAD_WIDTH
    key_spec = pl.BlockSpec((rows, HEAD_WIDTH), lambda h: (0, begin + h))
    value_spec = pl.BlockSpec((rows, HEAD_WIDTH), lambda h: (0, KEY_VALUE_HEADS + begin + h))
    wide = pl.BlockSpec((rows, group_width), lambda h: (0, begin + h))
    operands = [seg_q, seg_k, queries] + [block for block in blocks for _ in range(2)]
    in_specs = [
        pl.BlockSpec((rows, 1), lambda h: (0, 0)),
        pl.BlockSpec((1, span), lambda h: (0, 0)),
        wide,
        *([key_spec, value_spec] * len(blocks)),
    ]
    aliases = {}
    if before is not None:
        aliases = {len(operands): 0}
        operands.append(before)
        in_specs.append(pl.BlockSpec(memory_space=pl.ANY))
    return pl.pallas_call(
        functools.partial(attention_kernel, begin),
        grid=(end - begin,),
        in_specs=in_specs,
        out_specs=wide,
        out_shape=jax.ShapeDtypeStruct(queries.shape, jnp.bfloat16),
        input_output_aliases=aliases,
        compiler_params=pltpu.CompilerParams(vmem_limit_bytes=48 << 20),
        cost_estimate=pl.CostEstimate(
            flops=4 * rows * span * group_width * (end - begin),
            bytes_accessed=4 * rows * group_width * (end - begin),
            transcendentals=rows * span * group_width // HEAD_WIDTH * (end - begin),
        ),
        name=f"attention_{begin}",
    )(*operands)


def piece_lanes(slot, piece, ctx, fold, width):
    start = (slot * ctx + piece % fold * (ctx // fold) + piece // fold) * width
    return slice(start, start + width)


def pack_kernel(fold, width, x_ref, out_ref):
    ctx = out_ref.shape[0]
    for piece in range(ctx):
        for slot in range(out_ref.shape[2] // width):
            out_ref[piece, :, slot * width : (slot + 1) * width] = x_ref[:, piece_lanes(slot, piece, ctx, fold, width)]


def pack(value, ctx, fold, width):
    rows, channels = value.shape
    part = min(rows, 32)
    return pl.pallas_call(
        functools.partial(pack_kernel, fold, width),
        grid=(rows // part,),
        in_specs=[pl.BlockSpec((part, channels), lambda r: (r, 0))],
        out_specs=pl.BlockSpec((ctx, part, channels // ctx), lambda r: (0, r, 0)),
        out_shape=jax.ShapeDtypeStruct((ctx, rows, channels // ctx), value.dtype),
        compiler_params=pltpu.CompilerParams(vmem_limit_bytes=12 << 20),
        name="pack",
    )(value)


def conv_select_kernel(seg_ref, x_ref, weight_ref, bias_ref, select_ref, conv_ref, part_ref, masks, padded, total):
    step = pl.program_id(0)
    toks = seg_ref.shape[0]
    pieces, rows, wide = x_ref.shape
    tiles = wide // LANES
    slots, outputs, width = select_ref.shape

    @pl.when(step == 0)
    def _():
        wide_seg = jnp.broadcast_to(seg_ref[...], (toks, LANES)).astype(jnp.float32)
        padded[0, 0:SUBLANES, :] = jnp.full((SUBLANES, LANES), -1.0, jnp.float32)
        padded[0, SUBLANES : SUBLANES + toks, :] = wide_seg
        for tap in range(3):
            before = padded[0, SUBLANES - 3 + tap : SUBLANES - 3 + tap + toks, :]
            masks[tap] = jnp.where(before == wide_seg, 1.0, 0.0)
        for tile in range(tiles):
            padded[tile, 0:SUBLANES, :] = jnp.zeros((SUBLANES, LANES), jnp.float32)
        total[...] = jnp.zeros_like(total)

    outs = []
    for tile in range(tiles):
        lanes = slice(tile * LANES, (tile + 1) * LANES)
        for piece in range(pieces):
            first = SUBLANES + piece * rows
            padded[tile, first : first + rows, :] = x_ref[piece, :, lanes].astype(jnp.float32)
        half = jnp.broadcast_to(0.5 * bias_ref[0:1, lanes], (toks, LANES))
        for tap in range(4):
            moved = padded[tile, SUBLANES - 3 + tap : SUBLANES - 3 + tap + toks, :]
            term = (0.5 * weight_ref[tap : tap + 1, lanes]) * moved
            half = half + (term * masks[tap] if tap < 3 else term)
        conv = (half + half * jnp.tanh(half)).astype(jnp.bfloat16)
        conv_ref[:, lanes] = conv
        outs.append(conv)
    conv = jnp.concatenate(outs, axis=1)
    select = jnp.concatenate([select_ref[slot] for slot in range(slots)], axis=1)
    total[...] += lax.dot_general(conv, select, (((1,), (1,)), ((), ())), preferred_element_type=jnp.float32)

    @pl.when(step == pl.num_programs(0) - 1)
    def _():
        spare = part_ref.shape[2] - outputs
        for piece in range(pieces):
            part_ref[piece, :, 0:outputs] = total[piece * rows : (piece + 1) * rows, :].astype(part_ref.dtype)
            part_ref[piece, :, outputs:] = jnp.zeros((rows, spare), part_ref.dtype)


def conv_select(seg_col, pieces, conv_weight, conv_bias, select_parts):
    slots, outputs, width = select_parts.shape
    ctx, rows, _ = pieces.shape
    toks = ctx * rows
    padded_outputs = -(-outputs // LANES) * LANES
    batch = 4
    wide = batch * width
    return pl.pallas_call(
        conv_select_kernel,
        grid=(slots // batch,),
        in_specs=[
            pl.BlockSpec((toks, 1), lambda s: (0, 0)),
            pl.BlockSpec((ctx, rows, wide), lambda s: (0, 0, s)),
            pl.BlockSpec((4, wide), lambda s: (0, s)),
            pl.BlockSpec((1, wide), lambda s: (0, s)),
            pl.BlockSpec((batch, outputs, width), lambda s: (s, 0, 0)),
        ],
        out_specs=[
            pl.BlockSpec((toks, wide), lambda s: (0, s)),
            pl.BlockSpec((ctx, rows, padded_outputs), lambda s: (0, 0, 0)),
        ],
        scratch_shapes=[
            pltpu.VMEM((3, toks, LANES), jnp.float32),
            pltpu.VMEM((wide // LANES, SUBLANES + toks, LANES), jnp.float32),
            pltpu.VMEM((toks, outputs), jnp.float32),
        ],
        out_shape=[
            jax.ShapeDtypeStruct((toks, slots * width), jnp.bfloat16),
            jax.ShapeDtypeStruct((ctx, rows, padded_outputs), jnp.bfloat16),
        ],
        compiler_params=pltpu.CompilerParams(vmem_limit_bytes=32 << 20),
        cost_estimate=pl.CostEstimate(
            flops=2 * toks * slots * width * outputs,
            bytes_accessed=2 * pieces.size * 2 + 2 * select_parts.size,
            transcendentals=pieces.size,
        ),
        name="conv_select",
    )(seg_col, pieces, conv_weight, conv_bias, select_parts)


def normalise_kernel(rank, part_ref, out_ref):
    pieces = part_ref.shape[0]
    total = part_ref[0].astype(jnp.float32)
    for piece in range(1, pieces):
        total = total + part_ref[piece].astype(jnp.float32)
    low = total[:, :rank]
    scale = lax.rsqrt(jnp.mean(low * low, axis=-1, keepdims=True) + 1e-06)
    low = (low * scale).astype(out_ref.dtype)
    maps = total[:, rank:].astype(out_ref.dtype)
    for piece in range(pieces):
        out_ref[piece, :, :rank] = low
        out_ref[piece, :, rank:] = maps


def normalise(parts, rank):
    return pl.pallas_call(
        functools.partial(normalise_kernel, rank),
        out_shape=jax.ShapeDtypeStruct(parts.shape, jnp.bfloat16),
        compiler_params=pltpu.CompilerParams(vmem_limit_bytes=12 << 20),
        name="normalise",
    )(parts)


def scan_kernel(rank, reset_ref, low_ref, weight_ref, bias_ref, decay_ref, gain_ref, conv_ref, out_ref,
                in_cols, out_diag, delta_rows, drive_rows, held_even, held_odd, into_even, into_odd):
    toks = reset_ref.shape[0]
    states = decay_ref.shape[0]
    shards = weight_ref.shape[0]
    width = weight_ref.shape[2]
    tiles = shards * width // LANES
    rows = out_ref.shape[1]
    block = 16
    span = block * states
    count = toks // block

    in_cols[...] = jnp.transpose(low_ref[:, rank : rank + LANES].astype(jnp.float32))[0:states, :]
    lane = lax.broadcasted_iota(jnp.int32, (states, span), 1)
    spread = jnp.where(lane % states == lax.broadcasted_iota(jnp.int32, (states, span), 0), 1.0, 0.0)
    copies = jnp.dot(
        low_ref[:, rank + states : rank + 2 * states], spread.astype(jnp.bfloat16), preferred_element_type=jnp.float32
    )
    here = lax.broadcasted_iota(jnp.int32, (toks, span), 1) // states
    there = lax.broadcasted_iota(jnp.int32, (toks, span), 0) % block
    out_diag[...] = jnp.where(here == there, copies, 0.0).astype(jnp.bfloat16)

    reset = jnp.broadcast_to(reset_ref[...], (toks, LANES))
    low = low_ref[:, 0:rank]
    for shard in range(shards):
        pre = jnp.dot(low, weight_ref[shard], preferred_element_type=jnp.float32)
        for part in range(width // LANES):
            tile = shard * (width // LANES) + part
            lanes = slice(tile * LANES, (tile + 1) * LANES)
            value = pre[:, part * LANES : (part + 1) * LANES] + bias_ref[:, lanes]
            raised = jnp.exp(-jnp.abs(value))
            log_part = jnp.where(
                raised < 0.01,
                raised * (1.0 - raised * (0.5 - raised * (1.0 / 3.0))),
                jnp.log(1.0 + raised),
            )
            delta = (jnp.maximum(value, 0.0) + log_part).astype(jnp.bfloat16).astype(jnp.float32)
            delta_rows[:, tile] = (delta + reset).reshape(count, block, LANES)
            drive = delta * conv_ref[:, lanes].astype(jnp.float32)
            drive_rows[:, :, lanes] = drive.astype(jnp.bfloat16).reshape(toks // LANES, LANES, LANES)

    rates = [-LOG2E * jnp.exp(decay_ref[:, tile * LANES : (tile + 1) * LANES]) for tile in range(tiles)]

    quarter = min(2 * LANES, tiles * LANES)
    quarters = tiles * LANES // quarter

    def finish(index, history, part):
        first = pl.multiple_of(index * block, block)
        lanes = slice(part * quarter, (part + 1) * quarter)
        mixed = jnp.dot(out_diag[pl.ds(first, block), :], history[:, lanes], preferred_element_type=jnp.float32)
        full = mixed + gain_ref[:, lanes] * conv_ref[pl.ds(first, block), lanes].astype(jnp.float32)
        place = pl.multiple_of(lax.rem(first, rows), block)
        out_ref[lax.div(first, rows), pl.ds(place, block), lanes] = full.astype(out_ref.dtype)

    lane_index = lax.broadcasted_iota(jnp.int32, (states, LANES), 1)
    per_row = LANES // block

    def one_hot(index):
        columns = in_cols[:, pl.ds(pl.multiple_of(lax.div(index, per_row) * LANES, LANES), LANES)]
        first = lax.rem(index, per_row) * block
        return jnp.concatenate(
            [jnp.where(lane_index == first + inner, columns, 0.0).astype(jnp.bfloat16) for inner in range(block)], axis=0
        )

    def inject(index, hot, into, part):
        lanes = slice(part * quarter, (part + 1) * quarter)
        drive = drive_rows[lax.div(index, per_row), :, lanes]
        into[:, lanes] = jnp.dot(hot, drive, preferred_element_type=jnp.float32)

    def advance(index, held, history, into, before, before_history, after, after_into):
        held = list(held)
        delta_now = delta_rows.at[index]
        hot = one_hot(after)
        stride = block // quarters
        for inner in range(block):
            at = slice(inner * states, (inner + 1) * states)
            for tile in range(tiles):
                lanes = slice(tile * LANES, (tile + 1) * LANES)
                grow = jnp.exp2(delta_now[tile, inner : inner + 1, :] * rates[tile])
                held[tile] = grow * held[tile] + into[at, lanes]
                history[at, lanes] = held[tile].astype(jnp.bfloat16)
            if inner % stride == 0:
                finish(before, before_history, inner // stride)
            if inner % stride == stride // 2:
                inject(after, hot, after_into, inner // stride)
        return tuple(held)

    held_odd[...] = jnp.zeros_like(held_odd)
    first_hot = one_hot(0)
    for part in range(quarters):
        inject(0, first_hot, into_even, part)

    def pair(index, held):
        even, odd = 2 * index, 2 * index + 1
        held = advance(even, held, held_even, into_even, jnp.maximum(even - 1, 0), held_odd, odd, into_odd)
        return advance(odd, held, held_odd, into_odd, even, held_even, jnp.minimum(odd + 1, count - 1), into_even)

    start = tuple(jnp.zeros((states, LANES), jnp.float32) for _ in range(tiles))
    lax.fori_loop(0, count // 2, pair, start)
    for part in range(quarters):
        finish(count - 1, held_odd, part)


def state_scan(reset_col, low, delta_parts, bias, decay, gain, conv, ctx, call, calls):
    toks = low.shape[0]
    shards, rank, width = delta_parts.shape
    shards = shards // calls
    states = decay.shape[0]
    rows = toks // ctx
    wide = shards * width
    steps = toks * wide * states
    return pl.pallas_call(
        functools.partial(scan_kernel, rank),
        grid=(1,),
        in_specs=[
            pl.BlockSpec((toks, 1), lambda g: (0, 0)),
            pl.BlockSpec(low.shape, lambda g: (0, 0)),
            pl.BlockSpec((shards, rank, width), lambda g: (call, 0, 0)),
            pl.BlockSpec((1, wide), lambda g: (0, call)),
            pl.BlockSpec((states, wide), lambda g: (0, call)),
            pl.BlockSpec((1, wide), lambda g: (0, call)),
            pl.BlockSpec((toks, wide), lambda g: (0, call)),
        ],
        out_specs=pl.BlockSpec((ctx, rows, wide), lambda g: (0, 0, 0)),
        out_shape=jax.ShapeDtypeStruct((ctx, rows, wide), jnp.bfloat16),
        scratch_shapes=[
            pltpu.VMEM((states, toks), jnp.float32),
            pltpu.VMEM((toks, 16 * states), jnp.bfloat16),
            pltpu.VMEM((toks // 16, wide // LANES, 16, LANES), jnp.float32),
            pltpu.VMEM((toks // LANES, LANES, wide), jnp.bfloat16),
            pltpu.VMEM((16 * states, wide), jnp.bfloat16),
            pltpu.VMEM((16 * states, wide), jnp.bfloat16),
            pltpu.VMEM((16 * states, wide), jnp.float32),
            pltpu.VMEM((16 * states, wide), jnp.float32),
        ],
        compiler_params=pltpu.CompilerParams(vmem_limit_bytes=60 << 20),
        cost_estimate=pl.CostEstimate(
            flops=6 * steps, bytes_accessed=2 * delta_parts.size // calls + 4 * toks * wide, transcendentals=steps
        ),
        name=f"state_scan_{call}",
    )(reset_col, low, delta_parts, bias, decay, gain, conv)


def gate_kernel(fold, width, y_ref, gate_ref, *refs):
    out_ref = refs[-1]
    ctx, _, wide = y_ref.shape
    for slot in range(wide // width):
        for piece in range(ctx):
            lanes = piece_lanes(slot, piece, ctx, fold, width)
            value = y_ref[piece, :, slot * width : (slot + 1) * width].astype(jnp.float32)
            out_ref[:, lanes] = (value * silu(gate_ref[:, lanes].astype(jnp.float32))).astype(out_ref.dtype)


def apply_gate(pieces, gate, fold, width, call, before=None):
    ctx, rows, wide = pieces.shape
    part = min(rows, 32)
    columns = pl.BlockSpec((part, ctx * wide), lambda r: (r, call))
    operands = [pieces, gate]
    in_specs = [pl.BlockSpec((ctx, part, wide), lambda r: (0, r, 0)), columns]
    aliases = {}
    if before is not None:
        aliases = {2: 0}
        operands.append(before)
        in_specs.append(pl.BlockSpec(memory_space=pl.ANY))
    return pl.pallas_call(
        functools.partial(gate_kernel, fold, width),
        grid=(rows // part,),
        in_specs=in_specs,
        out_specs=columns,
        out_shape=jax.ShapeDtypeStruct(gate.shape, jnp.bfloat16),
        input_output_aliases=aliases,
        compiler_params=pltpu.CompilerParams(vmem_limit_bytes=12 << 20),
        cost_estimate=pl.CostEstimate(
            flops=4 * pieces.size, bytes_accessed=6 * pieces.size, transcendentals=pieces.size
        ),
        name=f"gate_{call}",
    )(*operands)


def shifted(value, axis, by):
    size = lax.axis_size(axis)
    pairs = [(i, i + by) for i in range(size) if 0 <= i + by < size]
    return lax.ppermute(value, axis, pairs)


def exchange(value):
    return lax.all_to_all(value, "ctx", 0, 0, tiled=True)


def local(
    queries,
    keys,
    values,
    mixer_input,
    gate_input,
    segment_ids,
    conv_weight,
    conv_bias,
    select_weight,
    delta_weight,
    delta_bias,
    decay_log,
    skip_gain,
):
    ctx = lax.axis_size("ctx")
    shards = lax.axis_size("rep")
    place = lax.axis_index("ctx")
    rows, channels = mixer_input.shape[1:]
    rank = delta_weight.shape[0]
    states = decay_log.shape[1]
    width = max(channels // (shards * ctx), LANES)
    fold = width * shards * ctx // channels
    seg = segment_ids[0]
    toks = seg.shape[0]
    seg_col = seg[:, None]
    back = min(ctx - 1, -(-(toks // 2 - 1) // rows))

    slots = shards // fold

    def own_part(array):
        cut = array.reshape(array.shape[:-1] + (slots, fold, ctx // fold, width))
        cut = lax.dynamic_index_in_dim(cut, place // fold, cut.ndim - 2, keepdims=False)
        cut = lax.dynamic_index_in_dim(cut, place % fold, cut.ndim - 2, keepdims=False)
        return cut.reshape(array.shape[:-1] + (slots * width,))

    def gathered(weight):
        own = lax.dynamic_slice_in_dim(weight, place // fold * width, width, 1)
        parts = lax.all_gather(own, "rep", axis=0)
        if fold > 1:
            parts = parts.reshape((slots, fold) + own.shape)
            parts = lax.dynamic_index_in_dim(parts, place % fold, 1, keepdims=False)
        return parts

    select_parts = gathered(select_weight)
    packed = pack(mixer_input[0], ctx, fold, width)
    packed, delta_weight = lax.optimization_barrier((packed, delta_weight))
    delta_parts = gathered(delta_weight)

    same = jnp.concatenate([jnp.zeros((1,), bool), seg[1:] == seg[:-1]])
    reset_col = jnp.where(same, 0.0, FAR)[:, None]
    seg_pad = jnp.concatenate([jnp.full((back * rows,), -1, jnp.int32), seg])
    seg_k = lax.dynamic_slice_in_dim(seg_pad, place * rows, (back + 1) * rows, 0)
    own = (
        own_part(delta_bias)[None, :],
        own_part(jnp.transpose(decay_log)),
        own_part(skip_gain)[None, :],
        reset_col,
        seg_k[back * rows :, None],
        seg_k[None, :],
        jnp.concatenate([keys[0], values[0]], axis=1),
    )
    pieces, own = lax.optimization_barrier((exchange(packed), own))
    bias, decay, gain, reset_col, seg_q, seg_k, both = own

    conv, parts = conv_select(seg_col, pieces, own_part(conv_weight), own_part(conv_bias)[None, :], select_parts)

    parts, both = lax.optimization_barrier((parts, both))
    blocks = [shifted(both, "ctx", by) for by in range(back, 0, -1)] + [both]
    low = normalise(exchange(parts), rank)
    low, blocks = lax.optimization_barrier((low, blocks))
    attended = attention(queries[0], blocks, seg_q, seg_k, 0, KEY_VALUE_HEADS)
    low, attended = lax.optimization_barrier((exchange(low), attended))
    low = low.reshape(toks, low.shape[2])

    calls = 2
    scanned = []
    for call in range(calls):
        scanned.append(exchange(state_scan(reset_col, low, delta_parts, bias, decay, gain, conv, ctx, call, calls)))
    mixed = None
    for call in range(calls):
        if mixed is not None:
            scanned[call], mixed = lax.optimization_barrier((scanned[call], mixed))
        mixed = apply_gate(scanned[call], gate_input[0], fold, width, call, mixed)
    return (attended[None], mixed[None])


def solution(mesh):
    placed = (
        P("rep", "ctx", None),
        P("rep", "ctx", None),
        P("rep", "ctx", None),
        P("rep", "ctx", None),
        P("rep", "ctx", None),
        P("rep", None),
        P(),
        P(),
        P(None, "rep"),
        P(None, "rep"),
        P(),
        P(),
        P(),
    )
    return jax.shard_map(
        local,
        mesh=mesh,
        in_specs=placed,
        out_specs=(P("rep", "ctx", None), P("rep", "ctx", None)),
        check_vma=False,
    )
```

```python
import functools
import math

import jax
import jax.numpy as jnp
from jax import lax
from jax.experimental import pallas as pl
from jax.experimental.pallas import tpu as pltpu
from jax.sharding import PartitionSpec as P

QUERY_HEADS = 32
KEY_VALUE_HEADS = 4
HEAD_WIDTH = 128
LANES = 128
SUBLANES = 8
LOG2E = 1.0 / math.log(2.0)
FAR = 1e30


def silu(value):
    half = 0.5 * value
    return half + half * jnp.tanh(half)


def attention_kernel(begin, seg_q_ref, seg_k_ref, q_ref, *refs):
    out_ref = refs[-1]
    refs = refs[: -1 if begin == 0 else -2]
    rows = q_ref.shape[0]
    span = seg_k_ref.shape[1]
    groups = QUERY_HEADS // KEY_VALUE_HEADS
    row = lax.broadcasted_iota(jnp.int32, (rows, span), 0) + (span - rows)
    col = lax.broadcasted_iota(jnp.int32, (rows, span), 1)
    allowed = (col <= row) & (seg_q_ref[...] == seg_k_ref[...])
    shift = jnp.where(allowed, 0.0, -FAR)
    keys = jnp.concatenate([ref[...] for ref in refs[0::2]], axis=0)
    vals = jnp.concatenate([ref[...] for ref in refs[1::2]], axis=0)
    factor = LOG2E / math.sqrt(HEAD_WIDTH)
    batch = 4
    for first in range(0, groups, batch):
        cuts = [slice(head * HEAD_WIDTH, (head + 1) * HEAD_WIDTH) for head in range(first, first + batch)]
        scores = [
            lax.dot_general(q_ref[:, cut], keys, (((1,), (1,)), ((), ())), preferred_element_type=jnp.float32)
            for cut in cuts
        ]
        scores = [score + shift for score in scores]
        tops = [jnp.max(score, axis=-1, keepdims=True) for score in scores]
        weights = [jnp.exp2((score - top) * factor) for score, top in zip(scores, tops)]
        norms = [jnp.sum(weight, axis=-1, keepdims=True) for weight in weights]
        totals = [jnp.dot(weight.astype(jnp.bfloat16), vals, preferred_element_type=jnp.float32) for weight in weights]
        for cut, total, norm in zip(cuts, totals, norms):
            out_ref[:, cut] = (total / norm).astype(out_ref.dtype)


def attention(queries, blocks, seg_q, seg_k, begin, end, before=None):
    rows = queries.shape[0]
    span = seg_k.shape[1]
    group_width = QUERY_HEADS // KEY_VALUE_HEADS * HEAD_WIDTH
    key_spec = pl.BlockSpec((rows, HEAD_WIDTH), lambda h: (0, begin + h))
    value_spec = pl.BlockSpec((rows, HEAD_WIDTH), lambda h: (0, KEY_VALUE_HEADS + begin + h))
    wide = pl.BlockSpec((rows, group_width), lambda h: (0, begin + h))
    operands = [seg_q, seg_k, queries] + [block for block in blocks for _ in range(2)]
    in_specs = [
        pl.BlockSpec((rows, 1), lambda h: (0, 0)),
        pl.BlockSpec((1, span), lambda h: (0, 0)),
        wide,
        *([key_spec, value_spec] * len(blocks)),
    ]
    aliases = {}
    if before is not None:
        aliases = {len(operands): 0}
        operands.append(before)
        in_specs.append(pl.BlockSpec(memory_space=pl.ANY))
    return pl.pallas_call(
        functools.partial(attention_kernel, begin),
        grid=(end - begin,),
        in_specs=in_specs,
        out_specs=wide,
        out_shape=jax.ShapeDtypeStruct(queries.shape, jnp.bfloat16),
        input_output_aliases=aliases,
        compiler_params=pltpu.CompilerParams(vmem_limit_bytes=16 << 20),
        cost_estimate=pl.CostEstimate(
            flops=4 * rows * span * group_width * (end - begin),
            bytes_accessed=4 * rows * group_width * (end - begin),
            transcendentals=rows * span * group_width // HEAD_WIDTH * (end - begin),
        ),
        name=f"attention_{begin}",
    )(*operands)


def piece_lanes(slot, piece, ctx, fold, width):
    start = (slot * ctx + piece % fold * (ctx // fold) + piece // fold) * width
    return slice(start, start + width)


def pack_kernel(fold, width, x_ref, out_ref):
    ctx = out_ref.shape[0]
    for piece in range(ctx):
        for slot in range(out_ref.shape[2] // width):
            out_ref[piece, :, slot * width : (slot + 1) * width] = x_ref[:, piece_lanes(slot, piece, ctx, fold, width)]


def pack(value, ctx, fold, width):
    rows, channels = value.shape
    part = min(rows, 32)
    return pl.pallas_call(
        functools.partial(pack_kernel, fold, width),
        grid=(rows // part,),
        in_specs=[pl.BlockSpec((part, channels), lambda r: (r, 0))],
        out_specs=pl.BlockSpec((ctx, part, channels // ctx), lambda r: (0, r, 0)),
        out_shape=jax.ShapeDtypeStruct((ctx, rows, channels // ctx), value.dtype),
        compiler_params=pltpu.CompilerParams(vmem_limit_bytes=12 << 20),
        name="pack",
    )(value)


def conv_select_kernel(seg_ref, x_ref, weight_ref, bias_ref, select_ref, conv_ref, part_ref, masks, padded, total):
    step = pl.program_id(0)
    toks = seg_ref.shape[0]
    pieces, rows, wide = x_ref.shape
    tiles = wide // LANES
    slots, outputs, width = select_ref.shape

    @pl.when(step == 0)
    def _():
        wide_seg = jnp.broadcast_to(seg_ref[...], (toks, LANES)).astype(jnp.float32)
        padded[0, 0:SUBLANES, :] = jnp.full((SUBLANES, LANES), -1.0, jnp.float32)
        padded[0, SUBLANES : SUBLANES + toks, :] = wide_seg
        for tap in range(3):
            before = padded[0, SUBLANES - 3 + tap : SUBLANES - 3 + tap + toks, :]
            masks[tap] = jnp.where(before == wide_seg, 1.0, 0.0)
        for tile in range(tiles):
            padded[tile, 0:SUBLANES, :] = jnp.zeros((SUBLANES, LANES), jnp.float32)
        total[...] = jnp.zeros_like(total)

    outs = []
    for tile in range(tiles):
        lanes = slice(tile * LANES, (tile + 1) * LANES)
        for piece in range(pieces):
            first = SUBLANES + piece * rows
            padded[tile, first : first + rows, :] = x_ref[piece, :, lanes].astype(jnp.float32)
        half = jnp.broadcast_to(0.5 * bias_ref[0:1, lanes], (toks, LANES))
        for tap in range(4):
            moved = padded[tile, SUBLANES - 3 + tap : SUBLANES - 3 + tap + toks, :]
            term = (0.5 * weight_ref[tap : tap + 1, lanes]) * moved
            half = half + (term * masks[tap] if tap < 3 else term)
        conv = (half + half * jnp.tanh(half)).astype(jnp.bfloat16)
        conv_ref[:, lanes] = conv
        outs.append(conv)
    conv = jnp.concatenate(outs, axis=1)
    select = jnp.concatenate([select_ref[slot] for slot in range(slots)], axis=1)
    total[...] += lax.dot_general(conv, select, (((1,), (1,)), ((), ())), preferred_element_type=jnp.float32)

    @pl.when(step == pl.num_programs(0) - 1)
    def _():
        spare = part_ref.shape[2] - outputs
        for piece in range(pieces):
            part_ref[piece, :, 0:outputs] = total[piece * rows : (piece + 1) * rows, :].astype(part_ref.dtype)
            part_ref[piece, :, outputs:] = jnp.zeros((rows, spare), part_ref.dtype)


def conv_select(seg_col, pieces, conv_weight, conv_bias, select_parts):
    slots, outputs, width = select_parts.shape
    ctx, rows, _ = pieces.shape
    toks = ctx * rows
    padded_outputs = -(-outputs // LANES) * LANES
    batch = 4
    wide = batch * width
    return pl.pallas_call(
        conv_select_kernel,
        grid=(slots // batch,),
        in_specs=[
            pl.BlockSpec((toks, 1), lambda s: (0, 0)),
            pl.BlockSpec((ctx, rows, wide), lambda s: (0, 0, s)),
            pl.BlockSpec((4, wide), lambda s: (0, s)),
            pl.BlockSpec((1, wide), lambda s: (0, s)),
            pl.BlockSpec((batch, outputs, width), lambda s: (s, 0, 0)),
        ],
        out_specs=[
            pl.BlockSpec((toks, wide), lambda s: (0, s)),
            pl.BlockSpec((ctx, rows, padded_outputs), lambda s: (0, 0, 0)),
        ],
        scratch_shapes=[
            pltpu.VMEM((3, toks, LANES), jnp.float32),
            pltpu.VMEM((wide // LANES, SUBLANES + toks, LANES), jnp.float32),
            pltpu.VMEM((toks, outputs), jnp.float32),
        ],
        out_shape=[
            jax.ShapeDtypeStruct((toks, slots * width), jnp.bfloat16),
            jax.ShapeDtypeStruct((ctx, rows, padded_outputs), jnp.bfloat16),
        ],
        compiler_params=pltpu.CompilerParams(vmem_limit_bytes=32 << 20),
        cost_estimate=pl.CostEstimate(
            flops=2 * toks * slots * width * outputs,
            bytes_accessed=2 * pieces.size * 2 + 2 * select_parts.size,
            transcendentals=pieces.size,
        ),
        name="conv_select",
    )(seg_col, pieces, conv_weight, conv_bias, select_parts)


def normalise_kernel(rank, part_ref, out_ref):
    pieces = part_ref.shape[0]
    total = part_ref[0].astype(jnp.float32)
    for piece in range(1, pieces):
        total = total + part_ref[piece].astype(jnp.float32)
    low = total[:, :rank]
    scale = lax.rsqrt(jnp.mean(low * low, axis=-1, keepdims=True) + 1e-06)
    low = (low * scale).astype(out_ref.dtype)
    maps = total[:, rank:].astype(out_ref.dtype)
    for piece in range(pieces):
        out_ref[piece, :, :rank] = low
        out_ref[piece, :, rank:] = maps


def normalise(parts, rank):
    return pl.pallas_call(
        functools.partial(normalise_kernel, rank),
        out_shape=jax.ShapeDtypeStruct(parts.shape, jnp.bfloat16),
        compiler_params=pltpu.CompilerParams(vmem_limit_bytes=12 << 20),
        name="normalise",
    )(parts)


def scan_kernel(rank, first_shard, reset_ref, low_ref, weight_hbm, bias_ref, decay_ref, gain_ref, conv_hbm, out_ref,
                weight_ref, conv_ref, sems, in_cols, out_diag, delta_rows, drive_rows, held_even, held_odd):
    toks = reset_ref.shape[0]
    states = decay_ref.shape[0]
    shards = weight_ref.shape[0]
    width = weight_ref.shape[2]
    tiles = shards * width // LANES
    column = first_shard * width
    weight_copy = pltpu.make_async_copy(weight_hbm.at[pl.ds(first_shard, shards)], weight_ref, sems.at[0])
    conv_copy = pltpu.make_async_copy(conv_hbm.at[:, pl.ds(column, shards * width)], conv_ref, sems.at[1])
    weight_copy.start()
    conv_copy.start()
    rows = out_ref.shape[1]
    block = 16
    span = block * states
    count = toks // block

    in_cols[...] = jnp.transpose(low_ref[:, rank : rank + LANES].astype(jnp.float32))[0:states, :]
    lane = lax.broadcasted_iota(jnp.int32, (states, span), 1)
    spread = jnp.where(lane % states == lax.broadcasted_iota(jnp.int32, (states, span), 0), 1.0, 0.0)
    copies = jnp.dot(
        low_ref[:, rank + states : rank + 2 * states], spread.astype(jnp.bfloat16), preferred_element_type=jnp.float32
    )
    here = lax.broadcasted_iota(jnp.int32, (toks, span), 1) // states
    there = lax.broadcasted_iota(jnp.int32, (toks, span), 0) % block
    out_diag[...] = jnp.where(here == there, copies, 0.0).astype(jnp.bfloat16)

    reset = jnp.broadcast_to(reset_ref[...], (toks, LANES))
    low = low_ref[:, 0:rank]
    weight_copy.wait()
    conv_copy.wait()
    for shard in range(shards):
        pre = jnp.dot(low, weight_ref[shard], preferred_element_type=jnp.float32)
        for part in range(width // LANES):
            tile = shard * (width // LANES) + part
            lanes = slice(tile * LANES, (tile + 1) * LANES)
            value = pre[:, part * LANES : (part + 1) * LANES]
            value = value + bias_ref[:, column + tile * LANES : column + (tile + 1) * LANES]
            raised = jnp.exp(-jnp.abs(value))
            log_part = jnp.where(
                raised < 0.01,
                raised * (1.0 - raised * (0.5 - raised * (1.0 / 3.0))),
                jnp.log(1.0 + raised),
            )
            delta = (jnp.maximum(value, 0.0) + log_part).astype(jnp.bfloat16).astype(jnp.float32)
            delta_rows[:, tile] = (delta + reset).reshape(count, block, LANES)
            drive_rows[:, tile] = (delta * conv_ref[:, lanes].astype(jnp.float32)).reshape(count, block, LANES)

    rates = [
        -LOG2E * jnp.exp(decay_ref[:, column + tile * LANES : column + (tile + 1) * LANES]) for tile in range(tiles)
    ]

    wide = tiles * LANES
    cut = 2 * LANES
    cuts = -(-wide // cut)

    def finish(index, history, part):
        first = pl.multiple_of(index * block, block)
        lanes = slice(part * cut, min((part + 1) * cut, wide))
        mixed = jnp.dot(out_diag[pl.ds(first, block), :], history[:, lanes], preferred_element_type=jnp.float32)
        gain = gain_ref[:, column + lanes.start : column + lanes.stop]
        full = mixed + gain * conv_ref[pl.ds(first, block), lanes].astype(jnp.float32)
        place = pl.multiple_of(lax.rem(first, rows), block)
        out_ref[lax.div(first, rows), pl.ds(place, block), lanes] = full.astype(out_ref.dtype)

    def advance(index, held, history, before, before_history):
        held = list(held)
        per_row = LANES // block
        columns = in_cols[:, pl.ds(pl.multiple_of(lax.div(index, per_row) * LANES, LANES), LANES)]
        columns = pltpu.roll(columns, lax.rem(LANES - lax.rem(index, per_row) * block, LANES), 1)
        delta_now = delta_rows.at[index]
        drive_now = drive_rows.at[index]
        for inner in range(block):
            into = jnp.broadcast_to(columns[:, inner : inner + 1], (states, LANES))
            for tile in range(tiles):
                lanes = slice(tile * LANES, (tile + 1) * LANES)
                grow = jnp.exp2(delta_now[tile, inner : inner + 1, :] * rates[tile])
                held[tile] = grow * held[tile] + into * drive_now[tile, inner : inner + 1, :]
                history[inner * states : (inner + 1) * states, lanes] = held[tile].astype(jnp.bfloat16)
            if inner % (block // cuts) == 0 and inner // (block // cuts) < cuts:
                finish(before, before_history, inner // (block // cuts))
        return tuple(held)

    held_odd[...] = jnp.zeros_like(held_odd)

    def pair(index, held):
        held = advance(2 * index, held, held_even, jnp.maximum(2 * index - 1, 0), held_odd)
        return advance(2 * index + 1, held, held_odd, 2 * index, held_even)

    start = tuple(jnp.zeros((states, LANES), jnp.float32) for _ in range(tiles))
    lax.fori_loop(0, count // 2, pair, start)
    for part in range(cuts):
        finish(count - 1, held_odd, part)


def state_scan(reset_col, low, delta_parts, bias, decay, gain, conv, ctx, first_shard, shards):
    toks = low.shape[0]
    rank, width = delta_parts.shape[1:]
    states = decay.shape[0]
    rows = toks // ctx
    wide = shards * width
    steps = toks * wide * states
    whole = pl.BlockSpec(memory_space=pltpu.VMEM)
    return pl.pallas_call(
        functools.partial(scan_kernel, rank, first_shard),
        in_specs=[
            whole,
            whole,
            pl.BlockSpec(memory_space=pl.ANY),
            whole,
            whole,
            whole,
            pl.BlockSpec(memory_space=pl.ANY),
        ],
        out_specs=whole,
        out_shape=jax.ShapeDtypeStruct((ctx, rows, wide), jnp.bfloat16),
        scratch_shapes=[
            pltpu.VMEM((shards, rank, width), jnp.bfloat16),
            pltpu.VMEM((toks, wide), jnp.bfloat16),
            pltpu.SemaphoreType.DMA((2,)),
            pltpu.VMEM((states, toks), jnp.float32),
            pltpu.VMEM((toks, 16 * states), jnp.bfloat16),
            pltpu.VMEM((toks // 16, wide // LANES, 16, LANES), jnp.float32),
            pltpu.VMEM((toks // 16, wide // LANES, 16, LANES), jnp.float32),
            pltpu.VMEM((16 * states, wide), jnp.bfloat16),
            pltpu.VMEM((16 * states, wide), jnp.bfloat16),
        ],
        compiler_params=pltpu.CompilerParams(vmem_limit_bytes=60 << 20),
        cost_estimate=pl.CostEstimate(
            flops=6 * steps, bytes_accessed=2 * shards * rank * width + 4 * toks * wide, transcendentals=steps
        ),
        name=f"state_scan_{first_shard}",
    )(reset_col, low, delta_parts, bias, decay, gain, conv)


def gate_kernel(fold, width, gate_ref, *refs):
    out_ref = refs[-1]
    slot = 0
    for y_ref in refs[:-1]:
        ctx, _, wide = y_ref.shape
        for place in range(wide // width):
            for piece in range(ctx):
                lanes = piece_lanes(slot, piece, ctx, fold, width)
                value = y_ref[piece, :, place * width : (place + 1) * width].astype(jnp.float32)
                out_ref[:, lanes] = (value * silu(gate_ref[:, lanes].astype(jnp.float32))).astype(out_ref.dtype)
            slot += 1


def apply_gate(parts, gate, fold, width):
    rows, channels = gate.shape
    ctx = parts[0].shape[0]
    part = min(rows, 32)
    columns = pl.BlockSpec((part, channels), lambda r: (r, 0))
    return pl.pallas_call(
        functools.partial(gate_kernel, fold, width),
        grid=(rows // part,),
        in_specs=[columns] + [pl.BlockSpec((ctx, part, array.shape[2]), lambda r: (0, r, 0)) for array in parts],
        out_specs=columns,
        out_shape=jax.ShapeDtypeStruct(gate.shape, jnp.bfloat16),
        compiler_params=pltpu.CompilerParams(vmem_limit_bytes=16 << 20),
        cost_estimate=pl.CostEstimate(flops=4 * gate.size, bytes_accessed=6 * gate.size, transcendentals=gate.size),
        name="gate",
    )(gate, *parts)


def shifted(value, axis, by):
    size = lax.axis_size(axis)
    pairs = [(i, i + by) for i in range(size) if 0 <= i + by < size]
    return lax.ppermute(value, axis, pairs)


def exchange(value):
    return lax.all_to_all(value, "ctx", 0, 0, tiled=True)


def local(
    queries,
    keys,
    values,
    mixer_input,
    gate_input,
    segment_ids,
    conv_weight,
    conv_bias,
    select_weight,
    delta_weight,
    delta_bias,
    decay_log,
    skip_gain,
):
    ctx = lax.axis_size("ctx")
    shards = lax.axis_size("rep")
    place = lax.axis_index("ctx")
    rows, channels = mixer_input.shape[1:]
    rank = delta_weight.shape[0]
    states = decay_log.shape[1]
    width = max(channels // (shards * ctx), LANES)
    fold = width * shards * ctx // channels
    seg = segment_ids[0]
    toks = seg.shape[0]
    seg_col = seg[:, None]
    back = min(ctx - 1, -(-(toks // 2 - 1) // rows))

    slots = shards // fold

    def own_part(array):
        cut = array.reshape(array.shape[:-1] + (slots, fold, ctx // fold, width))
        cut = lax.dynamic_index_in_dim(cut, place // fold, cut.ndim - 2, keepdims=False)
        cut = lax.dynamic_index_in_dim(cut, place % fold, cut.ndim - 2, keepdims=False)
        return cut.reshape(array.shape[:-1] + (slots * width,))

    def gathered(weight):
        own = lax.dynamic_slice_in_dim(weight, place // fold * width, width, 1)
        parts = lax.all_gather(own, "rep", axis=0)
        if fold > 1:
            parts = parts.reshape((slots, fold) + own.shape)
            parts = lax.dynamic_index_in_dim(parts, place % fold, 1, keepdims=False)
        return parts

    select_parts = gathered(select_weight)
    packed = pack(mixer_input[0], ctx, fold, width)

    same = jnp.concatenate([jnp.zeros((1,), bool), seg[1:] == seg[:-1]])
    reset_col = jnp.where(same, 0.0, FAR)[:, None]
    seg_pad = jnp.concatenate([jnp.full((back * rows,), -1, jnp.int32), seg])
    seg_k = lax.dynamic_slice_in_dim(seg_pad, place * rows, (back + 1) * rows, 0)
    own = (
        own_part(delta_bias)[None, :],
        own_part(jnp.transpose(decay_log)),
        own_part(skip_gain)[None, :],
        reset_col,
        seg_k[back * rows :, None],
        seg_k[None, :],
        jnp.concatenate([keys[0], values[0]], axis=1),
    )
    pieces, own, delta_weight = lax.optimization_barrier((exchange(packed), own, delta_weight))
    delta_parts = gathered(delta_weight)
    bias, decay, gain, reset_col, seg_q, seg_k, both = own

    conv, parts = conv_select(seg_col, pieces, own_part(conv_weight), own_part(conv_bias)[None, :], select_parts)
    low = normalise(exchange(parts), rank)

    low, both = lax.optimization_barrier((low, both))
    blocks = [shifted(both, "ctx", by) for by in range(back, 0, -1)] + [both]
    low = exchange(low).reshape(toks, low.shape[2])

    early = slots * 5 // 8
    scanned = []
    for first, count in ((0, early), (early, slots - early)):
        scanned.append(state_scan(reset_col, low, delta_parts, bias, decay, gain, conv, ctx, first, count))
    scanned[-1], blocks = lax.optimization_barrier((scanned[-1], blocks))
    attended = attention(queries[0], blocks, seg_q, seg_k, 0, KEY_VALUE_HEADS)
    scanned = [exchange(part) for part in scanned]
    scanned[-1], attended = lax.optimization_barrier((scanned[-1], attended))
    mixed = apply_gate(scanned, gate_input[0], fold, width)
    return (attended[None], mixed[None])


def solution(mesh):
    placed = (
        P("rep", "ctx", None),
        P("rep", "ctx", None),
        P("rep", "ctx", None),
        P("rep", "ctx", None),
        P("rep", "ctx", None),
        P("rep", None),
        P(),
        P(),
        P(None, "rep"),
        P(None, "rep"),
        P(),
        P(),
        P(),
    )
    return jax.shard_map(
        local,
        mesh=mesh,
        in_specs=placed,
        out_specs=(P("rep", "ctx", None), P("rep", "ctx", None)),
        check_vma=False,
    )
```

```python
import functools
import math

import jax
import jax.numpy as jnp
from jax import lax
from jax.experimental import pallas as pl
from jax.experimental.pallas import tpu as pltpu
from jax.sharding import PartitionSpec as P

QUERY_HEADS = 32
KEY_VALUE_HEADS = 4
HEAD_WIDTH = 128
LANES = 128
SUBLANES = 8
LOG2E = 1.0 / math.log(2.0)
FAR = 1e30


def silu(value):
    half = 0.5 * value
    return half + half * jnp.tanh(half)


def attention_kernel(begin, seg_q_ref, seg_k_ref, q_ref, *refs):
    out_ref = refs[-1]
    refs = refs[: -1 if begin == 0 else -2]
    rows = q_ref.shape[0]
    span = seg_k_ref.shape[1]
    groups = QUERY_HEADS // KEY_VALUE_HEADS
    row = lax.broadcasted_iota(jnp.int32, (rows, span), 0) + (span - rows)
    col = lax.broadcasted_iota(jnp.int32, (rows, span), 1)
    allowed = (col <= row) & (seg_q_ref[...] == seg_k_ref[...])
    shift = jnp.where(allowed, 0.0, -FAR)
    keys = jnp.concatenate([ref[...] for ref in refs[0::2]], axis=0)
    vals = jnp.concatenate([ref[...] for ref in refs[1::2]], axis=0)
    factor = LOG2E / math.sqrt(HEAD_WIDTH)
    batch = 4
    for first in range(0, groups, batch):
        cuts = [slice(head * HEAD_WIDTH, (head + 1) * HEAD_WIDTH) for head in range(first, first + batch)]
        scores = [
            lax.dot_general(q_ref[:, cut], keys, (((1,), (1,)), ((), ())), preferred_element_type=jnp.float32)
            for cut in cuts
        ]
        scores = [score + shift for score in scores]
        tops = [jnp.max(score, axis=-1, keepdims=True) for score in scores]
        weights = [jnp.exp2((score - top) * factor) for score, top in zip(scores, tops)]
        norms = [jnp.sum(weight, axis=-1, keepdims=True) for weight in weights]
        totals = [jnp.dot(weight.astype(jnp.bfloat16), vals, preferred_element_type=jnp.float32) for weight in weights]
        for cut, total, norm in zip(cuts, totals, norms):
            out_ref[:, cut] = (total / norm).astype(out_ref.dtype)


def attention(queries, blocks, seg_q, seg_k, begin, end, before=None):
    rows = queries.shape[0]
    span = seg_k.shape[1]
    group_width = QUERY_HEADS // KEY_VALUE_HEADS * HEAD_WIDTH
    key_spec = pl.BlockSpec((rows, HEAD_WIDTH), lambda h: (0, begin + h))
    value_spec = pl.BlockSpec((rows, HEAD_WIDTH), lambda h: (0, KEY_VALUE_HEADS + begin + h))
    wide = pl.BlockSpec((rows, group_width), lambda h: (0, begin + h))
    operands = [seg_q, seg_k, queries] + [block for block in blocks for _ in range(2)]
    in_specs = [
        pl.BlockSpec((rows, 1), lambda h: (0, 0)),
        pl.BlockSpec((1, span), lambda h: (0, 0)),
        wide,
        *([key_spec, value_spec] * len(blocks)),
    ]
    aliases = {}
    if before is not None:
        aliases = {len(operands): 0}
        operands.append(before)
        in_specs.append(pl.BlockSpec(memory_space=pl.ANY))
    return pl.pallas_call(
        functools.partial(attention_kernel, begin),
        grid=(end - begin,),
        in_specs=in_specs,
        out_specs=wide,
        out_shape=jax.ShapeDtypeStruct(queries.shape, jnp.bfloat16),
        input_output_aliases=aliases,
        compiler_params=pltpu.CompilerParams(vmem_limit_bytes=16 << 20),
        cost_estimate=pl.CostEstimate(
            flops=4 * rows * span * group_width * (end - begin),
            bytes_accessed=4 * rows * group_width * (end - begin),
            transcendentals=rows * span * group_width // HEAD_WIDTH * (end - begin),
        ),
        name=f"attention_{begin}",
    )(*operands)


def piece_lanes(slot, piece, ctx, fold, width):
    start = (slot * ctx + piece % fold * (ctx // fold) + piece // fold) * width
    return slice(start, start + width)


def pack_kernel(fold, width, x_ref, out_ref):
    ctx = out_ref.shape[0]
    for piece in range(ctx):
        for slot in range(out_ref.shape[2] // width):
            out_ref[piece, :, slot * width : (slot + 1) * width] = x_ref[:, piece_lanes(slot, piece, ctx, fold, width)]


def pack(value, ctx, fold, width):
    rows, channels = value.shape
    part = min(rows, 32)
    return pl.pallas_call(
        functools.partial(pack_kernel, fold, width),
        grid=(rows // part,),
        in_specs=[pl.BlockSpec((part, channels), lambda r: (r, 0))],
        out_specs=pl.BlockSpec((ctx, part, channels // ctx), lambda r: (0, r, 0)),
        out_shape=jax.ShapeDtypeStruct((ctx, rows, channels // ctx), value.dtype),
        compiler_params=pltpu.CompilerParams(vmem_limit_bytes=12 << 20),
        name="pack",
    )(value)


def conv_select_kernel(seg_ref, x_ref, weight_ref, bias_ref, select_ref, conv_ref, part_ref, masks, padded, total):
    step = pl.program_id(0)
    toks = seg_ref.shape[0]
    pieces, rows, wide = x_ref.shape
    tiles = wide // LANES
    slots, outputs, width = select_ref.shape

    @pl.when(step == 0)
    def _():
        wide_seg = jnp.broadcast_to(seg_ref[...], (toks, LANES)).astype(jnp.float32)
        padded[0, 0:SUBLANES, :] = jnp.full((SUBLANES, LANES), -1.0, jnp.float32)
        padded[0, SUBLANES : SUBLANES + toks, :] = wide_seg
        for tap in range(3):
            before = padded[0, SUBLANES - 3 + tap : SUBLANES - 3 + tap + toks, :]
            masks[tap] = jnp.where(before == wide_seg, 1.0, 0.0)
        for tile in range(tiles):
            padded[tile, 0:SUBLANES, :] = jnp.zeros((SUBLANES, LANES), jnp.float32)
        total[...] = jnp.zeros_like(total)

    outs = []
    for tile in range(tiles):
        lanes = slice(tile * LANES, (tile + 1) * LANES)
        for piece in range(pieces):
            first = SUBLANES + piece * rows
            padded[tile, first : first + rows, :] = x_ref[piece, :, lanes].astype(jnp.float32)
        half = jnp.broadcast_to(0.5 * bias_ref[0:1, lanes], (toks, LANES))
        for tap in range(4):
            moved = padded[tile, SUBLANES - 3 + tap : SUBLANES - 3 + tap + toks, :]
            term = (0.5 * weight_ref[tap : tap + 1, lanes]) * moved
            half = half + (term * masks[tap] if tap < 3 else term)
        conv = (half + half * jnp.tanh(half)).astype(jnp.bfloat16)
        conv_ref[:, lanes] = conv
        outs.append(conv)
    conv = jnp.concatenate(outs, axis=1)
    select = jnp.concatenate([select_ref[slot] for slot in range(slots)], axis=1)
    total[...] += lax.dot_general(conv, select, (((1,), (1,)), ((), ())), preferred_element_type=jnp.float32)

    @pl.when(step == pl.num_programs(0) - 1)
    def _():
        spare = part_ref.shape[2] - outputs
        for piece in range(pieces):
            part_ref[piece, :, 0:outputs] = total[piece * rows : (piece + 1) * rows, :].astype(part_ref.dtype)
            part_ref[piece, :, outputs:] = jnp.zeros((rows, spare), part_ref.dtype)


def conv_select(seg_col, pieces, conv_weight, conv_bias, select_parts):
    slots, outputs, width = select_parts.shape
    ctx, rows, _ = pieces.shape
    toks = ctx * rows
    padded_outputs = -(-outputs // LANES) * LANES
    batch = 4
    wide = batch * width
    return pl.pallas_call(
        conv_select_kernel,
        grid=(slots // batch,),
        in_specs=[
            pl.BlockSpec((toks, 1), lambda s: (0, 0)),
            pl.BlockSpec((ctx, rows, wide), lambda s: (0, 0, s)),
            pl.BlockSpec((4, wide), lambda s: (0, s)),
            pl.BlockSpec((1, wide), lambda s: (0, s)),
            pl.BlockSpec((batch, outputs, width), lambda s: (s, 0, 0)),
        ],
        out_specs=[
            pl.BlockSpec((toks, wide), lambda s: (0, s)),
            pl.BlockSpec((ctx, rows, padded_outputs), lambda s: (0, 0, 0)),
        ],
        scratch_shapes=[
            pltpu.VMEM((3, toks, LANES), jnp.float32),
            pltpu.VMEM((wide // LANES, SUBLANES + toks, LANES), jnp.float32),
            pltpu.VMEM((toks, outputs), jnp.float32),
        ],
        out_shape=[
            jax.ShapeDtypeStruct((toks, slots * width), jnp.bfloat16),
            jax.ShapeDtypeStruct((ctx, rows, padded_outputs), jnp.bfloat16),
        ],
        compiler_params=pltpu.CompilerParams(vmem_limit_bytes=32 << 20),
        cost_estimate=pl.CostEstimate(
            flops=2 * toks * slots * width * outputs,
            bytes_accessed=2 * pieces.size * 2 + 2 * select_parts.size,
            transcendentals=pieces.size,
        ),
        name="conv_select",
    )(seg_col, pieces, conv_weight, conv_bias, select_parts)


def normalise_kernel(rank, part_ref, out_ref):
    pieces = part_ref.shape[0]
    total = part_ref[0].astype(jnp.float32)
    for piece in range(1, pieces):
        total = total + part_ref[piece].astype(jnp.float32)
    low = total[:, :rank]
    scale = lax.rsqrt(jnp.mean(low * low, axis=-1, keepdims=True) + 1e-06)
    low = (low * scale).astype(out_ref.dtype)
    maps = total[:, rank:].astype(out_ref.dtype)
    for piece in range(pieces):
        out_ref[piece, :, :rank] = low
        out_ref[piece, :, rank:] = maps


def normalise(parts, rank):
    return pl.pallas_call(
        functools.partial(normalise_kernel, rank),
        out_shape=jax.ShapeDtypeStruct(parts.shape, jnp.bfloat16),
        compiler_params=pltpu.CompilerParams(vmem_limit_bytes=12 << 20),
        name="normalise",
    )(parts)


def scan_kernel(rank, first_shard, reset_ref, low_ref, weight_hbm, bias_ref, decay_ref, gain_ref, conv_hbm, out_ref,
                weight_ref, conv_ref, sems, in_cols, out_diag, delta_rows, drive_rows, held_even, held_odd):
    toks = reset_ref.shape[0]
    states = decay_ref.shape[0]
    shards = weight_ref.shape[0]
    width = weight_ref.shape[2]
    tiles = shards * width // LANES
    column = first_shard * width
    weight_copy = pltpu.make_async_copy(weight_hbm.at[pl.ds(first_shard, shards)], weight_ref, sems.at[0])
    conv_copy = pltpu.make_async_copy(conv_hbm.at[:, pl.ds(column, shards * width)], conv_ref, sems.at[1])
    weight_copy.start()
    conv_copy.start()
    rows = out_ref.shape[1]
    block = 16
    span = block * states
    count = toks // block

    in_cols[...] = jnp.transpose(low_ref[:, rank : rank + LANES].astype(jnp.float32))[0:states, :]
    bits = states.bit_length() - 1
    lane = lax.broadcasted_iota(jnp.int32, (states, span), 1)
    spread = jnp.where((lane & (states - 1)) == lax.broadcasted_iota(jnp.int32, (states, span), 0), 1.0, 0.0)
    copies = jnp.dot(
        low_ref[:, rank + states : rank + 2 * states], spread.astype(jnp.bfloat16), preferred_element_type=jnp.float32
    )
    here = lax.shift_right_logical(lax.broadcasted_iota(jnp.int32, (block, span), 1), bits)
    there = lax.broadcasted_iota(jnp.int32, (block, span), 0)
    keep = jnp.where(here == there, 1.0, 0.0)
    out_diag[...] = (copies.reshape(count, block, span) * keep[None]).reshape(toks, span).astype(jnp.bfloat16)

    reset = jnp.broadcast_to(reset_ref[...], (toks, LANES))
    low = low_ref[:, 0:rank]
    weight_copy.wait()
    conv_copy.wait()
    for shard in range(shards):
        pre = jnp.dot(low, weight_ref[shard], preferred_element_type=jnp.float32)
        for part in range(width // LANES):
            tile = shard * (width // LANES) + part
            lanes = slice(tile * LANES, (tile + 1) * LANES)
            value = pre[:, part * LANES : (part + 1) * LANES]
            value = value + bias_ref[:, column + tile * LANES : column + (tile + 1) * LANES]
            raised = jnp.exp2(jnp.minimum(value, 80.0) * LOG2E)
            small = raised - 0.5 * raised * raised
            delta = jnp.maximum(value, jnp.where(raised < 0.01, small, jnp.log(1.0 + raised)))
            delta_rows[:, tile] = (delta + reset).reshape(count, block, LANES)
            drive_rows[:, tile] = (delta * conv_ref[:, lanes].astype(jnp.float32)).reshape(count, block, LANES)

    rates = [
        -LOG2E * jnp.exp(decay_ref[:, column + tile * LANES : column + (tile + 1) * LANES]) for tile in range(tiles)
    ]

    wide = tiles * LANES
    cut = 2 * LANES
    cuts = -(-wide // cut)

    def finish(index, history, part):
        first = pl.multiple_of(index * block, block)
        lanes = slice(part * cut, min((part + 1) * cut, wide))
        mixed = jnp.dot(out_diag[pl.ds(first, block), :], history[:, lanes], preferred_element_type=jnp.float32)
        gain = gain_ref[:, column + lanes.start : column + lanes.stop]
        full = mixed + gain * conv_ref[pl.ds(first, block), lanes].astype(jnp.float32)
        place = pl.multiple_of(lax.rem(first, rows), block)
        out_ref[lax.div(first, rows), pl.ds(place, block), lanes] = full.astype(out_ref.dtype)

    def advance(index, held, history, before, before_history):
        held = list(held)
        per_row = LANES // block
        columns = in_cols[:, pl.ds(pl.multiple_of(lax.div(index, per_row) * LANES, LANES), LANES)]
        columns = pltpu.roll(columns, lax.rem(LANES - lax.rem(index, per_row) * block, LANES), 1)
        delta_now = delta_rows.at[index]
        drive_now = drive_rows.at[index]
        for inner in range(block):
            into = jnp.broadcast_to(columns[:, inner : inner + 1], (states, LANES))
            for tile in range(tiles):
                lanes = slice(tile * LANES, (tile + 1) * LANES)
                grow = jnp.exp2(delta_now[tile, inner : inner + 1, :] * rates[tile])
                held[tile] = grow * held[tile] + into * drive_now[tile, inner : inner + 1, :]
                history[inner * states : (inner + 1) * states, lanes] = held[tile].astype(jnp.bfloat16)
            if inner % (block // cuts) == 0 and inner // (block // cuts) < cuts:
                finish(before, before_history, inner // (block // cuts))
        return tuple(held)

    held_odd[...] = jnp.zeros_like(held_odd)

    def pair(index, held):
        held = advance(2 * index, held, held_even, jnp.maximum(2 * index - 1, 0), held_odd)
        return advance(2 * index + 1, held, held_odd, 2 * index, held_even)

    start = tuple(jnp.zeros((states, LANES), jnp.float32) for _ in range(tiles))
    lax.fori_loop(0, count // 2, pair, start)
    for part in range(cuts):
        finish(count - 1, held_odd, part)


def state_scan(reset_col, low, delta_parts, bias, decay, gain, conv, ctx, first_shard, shards):
    toks = low.shape[0]
    rank, width = delta_parts.shape[1:]
    states = decay.shape[0]
    rows = toks // ctx
    wide = shards * width
    steps = toks * wide * states
    whole = pl.BlockSpec(memory_space=pltpu.VMEM)
    return pl.pallas_call(
        functools.partial(scan_kernel, rank, first_shard),
        in_specs=[
            whole,
            whole,
            pl.BlockSpec(memory_space=pl.ANY),
            whole,
            whole,
            whole,
            pl.BlockSpec(memory_space=pl.ANY),
        ],
        out_specs=whole,
        out_shape=jax.ShapeDtypeStruct((ctx, rows, wide), jnp.bfloat16),
        scratch_shapes=[
            pltpu.VMEM((shards, rank, width), jnp.bfloat16),
            pltpu.VMEM((toks, wide), jnp.bfloat16),
            pltpu.SemaphoreType.DMA((2,)),
            pltpu.VMEM((states, toks), jnp.float32),
            pltpu.VMEM((toks, 16 * states), jnp.bfloat16),
            pltpu.VMEM((toks // 16, wide // LANES, 16, LANES), jnp.float32),
            pltpu.VMEM((toks // 16, wide // LANES, 16, LANES), jnp.float32),
            pltpu.VMEM((16 * states, wide), jnp.bfloat16),
            pltpu.VMEM((16 * states, wide), jnp.bfloat16),
        ],
        compiler_params=pltpu.CompilerParams(vmem_limit_bytes=60 << 20),
        cost_estimate=pl.CostEstimate(
            flops=6 * steps, bytes_accessed=2 * shards * rank * width + 4 * toks * wide, transcendentals=steps
        ),
        name=f"state_scan_{first_shard}",
    )(reset_col, low, delta_parts, bias, decay, gain, conv)


def gate_kernel(fold, width, gate_ref, *refs):
    out_ref = refs[-1]
    slot = 0
    for y_ref in refs[:-1]:
        ctx, _, wide = y_ref.shape
        for place in range(wide // width):
            for piece in range(ctx):
                lanes = piece_lanes(slot, piece, ctx, fold, width)
                value = y_ref[piece, :, place * width : (place + 1) * width].astype(jnp.float32)
                out_ref[:, lanes] = (value * silu(gate_ref[:, lanes].astype(jnp.float32))).astype(out_ref.dtype)
            slot += 1


def apply_gate(parts, gate, fold, width):
    rows, channels = gate.shape
    ctx = parts[0].shape[0]
    part = min(rows, 32)
    columns = pl.BlockSpec((part, channels), lambda r: (r, 0))
    return pl.pallas_call(
        functools.partial(gate_kernel, fold, width),
        grid=(rows // part,),
        in_specs=[columns] + [pl.BlockSpec((ctx, part, array.shape[2]), lambda r: (0, r, 0)) for array in parts],
        out_specs=columns,
        out_shape=jax.ShapeDtypeStruct(gate.shape, jnp.bfloat16),
        compiler_params=pltpu.CompilerParams(vmem_limit_bytes=16 << 20),
        cost_estimate=pl.CostEstimate(flops=4 * gate.size, bytes_accessed=6 * gate.size, transcendentals=gate.size),
        name="gate",
    )(gate, *parts)


def shifted(value, axis, by):
    size = lax.axis_size(axis)
    pairs = [(i, i + by) for i in range(size) if 0 <= i + by < size]
    return lax.ppermute(value, axis, pairs)


def exchange(value):
    return lax.all_to_all(value, "ctx", 0, 0, tiled=True)


def local(
    queries,
    keys,
    values,
    mixer_input,
    gate_input,
    segment_ids,
    conv_weight,
    conv_bias,
    select_weight,
    delta_weight,
    delta_bias,
    decay_log,
    skip_gain,
):
    ctx = lax.axis_size("ctx")
    shards = lax.axis_size("rep")
    place = lax.axis_index("ctx")
    rows, channels = mixer_input.shape[1:]
    rank = delta_weight.shape[0]
    states = decay_log.shape[1]
    width = max(channels // (shards * ctx), LANES)
    fold = width * shards * ctx // channels
    seg = segment_ids[0]
    toks = seg.shape[0]
    seg_col = seg[:, None]
    back = min(ctx - 1, -(-(toks // 2 - 1) // rows))

    slots = shards // fold

    def own_part(array):
        cut = array.reshape(array.shape[:-1] + (slots, fold, ctx // fold, width))
        cut = lax.dynamic_index_in_dim(cut, place // fold, cut.ndim - 2, keepdims=False)
        cut = lax.dynamic_index_in_dim(cut, place % fold, cut.ndim - 2, keepdims=False)
        return cut.reshape(array.shape[:-1] + (slots * width,))

    def own_columns(weight):
        return lax.dynamic_slice_in_dim(weight, place // fold * width, width, 1)

    def gathered(own):
        parts = lax.all_gather(own, "rep", axis=0)
        if fold > 1:
            parts = parts.reshape((slots, fold) + own.shape)
            parts = lax.dynamic_index_in_dim(parts, place % fold, 1, keepdims=False)
        return parts

    select_parts = gathered(own_columns(select_weight))
    packed = pack(mixer_input[0], ctx, fold, width)

    same = jnp.concatenate([jnp.zeros((1,), bool), seg[1:] == seg[:-1]])
    reset_col = jnp.where(same, 0.0, FAR)[:, None]
    seg_pad = jnp.concatenate([jnp.full((back * rows,), -1, jnp.int32), seg])
    seg_k = lax.dynamic_slice_in_dim(seg_pad, place * rows, (back + 1) * rows, 0)
    own = (
        own_part(delta_bias)[None, :],
        own_part(jnp.transpose(decay_log)),
        own_part(skip_gain)[None, :],
        reset_col,
        seg_k[back * rows :, None],
        seg_k[None, :],
        jnp.concatenate([keys[0], values[0]], axis=1),
        own_part(conv_weight),
        own_part(conv_bias)[None, :],
        seg_col,
        own_columns(delta_weight),
    )
    pieces, own = lax.optimization_barrier((exchange(packed), own))
    bias, decay, gain, reset_col, seg_q, seg_k, both, conv_weight, conv_bias, seg_col, delta_own = own
    delta_parts = gathered(delta_own)

    conv, parts = conv_select(seg_col, pieces, conv_weight, conv_bias, select_parts)
    low = normalise(exchange(parts), rank)

    low, both = lax.optimization_barrier((low, both))
    blocks = [shifted(both, "ctx", by) for by in range(back, 0, -1)] + [both]
    low = exchange(low).reshape(toks, low.shape[2])

    early = slots * 5 // 8
    scanned = []
    for first, count in ((0, early), (early, slots - early)):
        if scanned:
            low, scanned[-1] = lax.optimization_barrier((low, scanned[-1]))
        scanned.append(state_scan(reset_col, low, delta_parts, bias, decay, gain, conv, ctx, first, count))
    scanned[-1], blocks = lax.optimization_barrier((scanned[-1], blocks))
    attended = attention(queries[0], blocks, seg_q, seg_k, 0, KEY_VALUE_HEADS)
    scanned = [exchange(part) for part in scanned]
    scanned[-1], attended = lax.optimization_barrier((scanned[-1], attended))
    mixed = apply_gate(scanned, gate_input[0], fold, width)
    return (attended[None], mixed[None])


def solution(mesh):
    placed = (
        P("rep", "ctx", None),
        P("rep", "ctx", None),
        P("rep", "ctx", None),
        P("rep", "ctx", None),
        P("rep", "ctx", None),
        P("rep", None),
        P(),
        P(),
        P(None, "rep"),
        P(None, "rep"),
        P(),
        P(),
        P(),
    )
    return jax.shard_map(
        local,
        mesh=mesh,
        in_specs=placed,
        out_specs=(P("rep", "ctx", None), P("rep", "ctx", None)),
        check_vma=False,
    )
```

```python
import functools
import math

import jax
import jax.numpy as jnp
from jax import lax
from jax.experimental import pallas as pl
from jax.experimental.pallas import tpu as pltpu
from jax.sharding import PartitionSpec as P

QUERY_HEADS = 32
KEY_VALUE_HEADS = 4
HEAD_WIDTH = 128
LANES = 128
SUBLANES = 8
LOG2E = 1.0 / math.log(2.0)
FAR = 1e30


def silu(value):
    half = 0.5 * value
    return half + half * jnp.tanh(half)


def attention_kernel(begin, seg_q_ref, seg_k_ref, q_ref, *refs):
    out_ref = refs[-1]
    refs = refs[: -1 if begin == 0 else -2]
    rows = q_ref.shape[0]
    span = seg_k_ref.shape[1]
    groups = QUERY_HEADS // KEY_VALUE_HEADS
    row = lax.broadcasted_iota(jnp.int32, (rows, span), 0) + (span - rows)
    col = lax.broadcasted_iota(jnp.int32, (rows, span), 1)
    allowed = (col <= row) & (seg_q_ref[...] == seg_k_ref[...])
    shift = jnp.where(allowed, 0.0, -FAR)
    keys = jnp.concatenate([ref[...] for ref in refs[0::2]], axis=0)
    vals = jnp.concatenate([ref[...] for ref in refs[1::2]], axis=0)
    factor = LOG2E / math.sqrt(HEAD_WIDTH)
    batch = 4
    for first in range(0, groups, batch):
        cuts = [slice(head * HEAD_WIDTH, (head + 1) * HEAD_WIDTH) for head in range(first, first + batch)]
        scores = [
            lax.dot_general(q_ref[:, cut], keys, (((1,), (1,)), ((), ())), preferred_element_type=jnp.float32)
            for cut in cuts
        ]
        scores = [score + shift for score in scores]
        tops = [jnp.max(score, axis=-1, keepdims=True) for score in scores]
        weights = [jnp.exp2((score - top) * factor) for score, top in zip(scores, tops)]
        norms = [jnp.sum(weight, axis=-1, keepdims=True) for weight in weights]
        totals = [jnp.dot(weight.astype(jnp.bfloat16), vals, preferred_element_type=jnp.float32) for weight in weights]
        for cut, total, norm in zip(cuts, totals, norms):
            out_ref[:, cut] = (total / norm).astype(out_ref.dtype)


def attention(queries, blocks, seg_q, seg_k, begin, end, before=None):
    rows = queries.shape[0]
    span = seg_k.shape[1]
    group_width = QUERY_HEADS // KEY_VALUE_HEADS * HEAD_WIDTH
    key_spec = pl.BlockSpec((rows, HEAD_WIDTH), lambda h: (0, begin + h))
    value_spec = pl.BlockSpec((rows, HEAD_WIDTH), lambda h: (0, KEY_VALUE_HEADS + begin + h))
    wide = pl.BlockSpec((rows, group_width), lambda h: (0, begin + h))
    operands = [seg_q, seg_k, queries] + [block for block in blocks for _ in range(2)]
    in_specs = [
        pl.BlockSpec((rows, 1), lambda h: (0, 0)),
        pl.BlockSpec((1, span), lambda h: (0, 0)),
        wide,
        *([key_spec, value_spec] * len(blocks)),
    ]
    aliases = {}
    if before is not None:
        aliases = {len(operands): 0}
        operands.append(before)
        in_specs.append(pl.BlockSpec(memory_space=pl.ANY))
    return pl.pallas_call(
        functools.partial(attention_kernel, begin),
        grid=(end - begin,),
        in_specs=in_specs,
        out_specs=wide,
        out_shape=jax.ShapeDtypeStruct(queries.shape, jnp.bfloat16),
        input_output_aliases=aliases,
        compiler_params=pltpu.CompilerParams(vmem_limit_bytes=16 << 20),
        cost_estimate=pl.CostEstimate(
            flops=4 * rows * span * group_width * (end - begin),
            bytes_accessed=4 * rows * group_width * (end - begin),
            transcendentals=rows * span * group_width // HEAD_WIDTH * (end - begin),
        ),
        name=f"attention_{begin}",
    )(*operands)


def piece_lanes(slot, piece, ctx, fold, width):
    start = (slot * ctx + piece % fold * (ctx // fold) + piece // fold) * width
    return slice(start, start + width)


def pack_kernel(fold, width, x_ref, out_ref):
    ctx = out_ref.shape[0]
    for piece in range(ctx):
        for slot in range(out_ref.shape[2] // width):
            out_ref[piece, :, slot * width : (slot + 1) * width] = x_ref[:, piece_lanes(slot, piece, ctx, fold, width)]


def pack(value, ctx, fold, width, half):
    rows, channels = value.shape
    channels = channels // 2
    part = min(rows, 64)
    return pl.pallas_call(
        functools.partial(pack_kernel, fold, width),
        grid=(rows // part,),
        in_specs=[pl.BlockSpec((part, channels), lambda r: (r, half))],
        out_specs=pl.BlockSpec((ctx, part, channels // ctx), lambda r: (0, r, 0)),
        out_shape=jax.ShapeDtypeStruct((ctx, rows, channels // ctx), value.dtype),
        compiler_params=pltpu.CompilerParams(vmem_limit_bytes=12 << 20),
        name=f"pack_{half}",
    )(value)


def convolve(seg_ref, x_ref, weight_ref, bias_ref, masks, padded):
    toks = seg_ref.shape[0]
    pieces, rows, wide = x_ref.shape
    tiles = wide // LANES

    @pl.when(pl.program_id(0) == 0)
    def _():
        wide_seg = jnp.broadcast_to(seg_ref[...], (toks, LANES)).astype(jnp.float32)
        padded[0, 0:SUBLANES, :] = jnp.full((SUBLANES, LANES), -1.0, jnp.float32)
        padded[0, SUBLANES : SUBLANES + toks, :] = wide_seg
        for tap in range(3):
            before = padded[0, SUBLANES - 3 + tap : SUBLANES - 3 + tap + toks, :]
            masks[tap] = jnp.where(before == wide_seg, 1.0, 0.0)
        for tile in range(tiles):
            padded[tile, 0:SUBLANES, :] = jnp.zeros((SUBLANES, LANES), jnp.float32)

    outs = []
    for tile in range(tiles):
        lanes = slice(tile * LANES, (tile + 1) * LANES)
        for piece in range(pieces):
            first = SUBLANES + piece * rows
            padded[tile, first : first + rows, :] = x_ref[piece, :, lanes].astype(jnp.float32)
        half = jnp.broadcast_to(0.5 * bias_ref[0:1, lanes], (toks, LANES))
        for tap in range(4):
            moved = padded[tile, SUBLANES - 3 + tap : SUBLANES - 3 + tap + toks, :]
            term = (0.5 * weight_ref[tap : tap + 1, lanes]) * moved
            half = half + (term * masks[tap] if tap < 3 else term)
        outs.append((half + half * jnp.tanh(half)).astype(jnp.bfloat16))
    return outs


def conv_kernel(seg_ref, x_ref, weight_ref, bias_ref, conv_ref, masks, padded):
    for tile, conv in enumerate(convolve(seg_ref, x_ref, weight_ref, bias_ref, masks, padded)):
        conv_ref[:, tile * LANES : (tile + 1) * LANES] = conv


def conv_select_kernel(seg_ref, x_ref, weight_ref, bias_ref, early_ref, early_select_ref, select_ref,
                       conv_ref, part_ref, masks, padded, total):
    step = pl.program_id(0)
    pieces, rows, _ = x_ref.shape
    slots, outputs, _ = select_ref.shape

    def product(conv, select_ref):
        select = jnp.concatenate([select_ref[slot] for slot in range(slots)], axis=1)
        return lax.dot_general(conv, select, (((1,), (1,)), ((), ())), preferred_element_type=jnp.float32)

    early = product(early_ref[...], early_select_ref)

    @pl.when(step == 0)
    def _():
        total[...] = early

    @pl.when(step > 0)
    def _():
        total[...] += early

    outs = convolve(seg_ref, x_ref, weight_ref, bias_ref, masks, padded)
    for tile, conv in enumerate(outs):
        conv_ref[:, tile * LANES : (tile + 1) * LANES] = conv
    total[...] += product(jnp.concatenate(outs, axis=1), select_ref)

    @pl.when(step == pl.num_programs(0) - 1)
    def _():
        spare = part_ref.shape[2] - outputs
        for piece in range(pieces):
            part_ref[piece, :, 0:outputs] = total[piece * rows : (piece + 1) * rows, :].astype(part_ref.dtype)
            part_ref[piece, :, outputs:] = jnp.zeros((rows, spare), part_ref.dtype)


CONV_BATCH = 2


def conv_specs(seg_col, pieces, width, half, steps):
    ctx, rows, _ = pieces.shape
    wide = CONV_BATCH * width
    toks = ctx * rows
    in_specs = [
        pl.BlockSpec(seg_col.shape, lambda s: (0, 0)),
        pl.BlockSpec((ctx, rows, wide), lambda s: (0, 0, s)),
        pl.BlockSpec((4, wide), lambda s: (0, half * steps + s)),
        pl.BlockSpec((1, wide), lambda s: (0, half * steps + s)),
    ]
    scratch = [
        pltpu.VMEM((3, toks, LANES), jnp.float32),
        pltpu.VMEM((wide // LANES, SUBLANES + toks, LANES), jnp.float32),
    ]
    return in_specs, pl.BlockSpec((toks, wide), lambda s: (0, s)), scratch


def conv_early(seg_col, pieces, conv_weight, conv_bias, width):
    toks = seg_col.shape[0]
    columns = pieces.shape[2]
    steps = columns // (CONV_BATCH * width)
    in_specs, out_spec, scratch = conv_specs(seg_col, pieces, width, 0, steps)
    return pl.pallas_call(
        conv_kernel,
        grid=(steps,),
        in_specs=in_specs,
        out_specs=out_spec,
        scratch_shapes=scratch,
        out_shape=jax.ShapeDtypeStruct((toks, columns), jnp.bfloat16),
        compiler_params=pltpu.CompilerParams(vmem_limit_bytes=24 << 20),
        cost_estimate=pl.CostEstimate(
            flops=16 * pieces.size, bytes_accessed=4 * pieces.size, transcendentals=pieces.size
        ),
        name="conv_early",
    )(seg_col, pieces, conv_weight, conv_bias)


def conv_select(seg_col, pieces, conv_weight, conv_bias, early, select_parts):
    slots, outputs, width = select_parts.shape
    ctx, rows, columns = pieces.shape
    toks = ctx * rows
    padded_outputs = -(-outputs // LANES) * LANES
    steps = columns // (CONV_BATCH * width)
    in_specs, out_spec, scratch = conv_specs(seg_col, pieces, width, 1, steps)
    return pl.pallas_call(
        conv_select_kernel,
        grid=(steps,),
        in_specs=in_specs
        + [
            pl.BlockSpec((toks, CONV_BATCH * width), lambda s: (0, s)),
            pl.BlockSpec((CONV_BATCH, outputs, width), lambda s: (s, 0, 0)),
            pl.BlockSpec((CONV_BATCH, outputs, width), lambda s: (steps + s, 0, 0)),
        ],
        out_specs=[out_spec, pl.BlockSpec((ctx, rows, padded_outputs), lambda s: (0, 0, 0))],
        scratch_shapes=scratch + [pltpu.VMEM((toks, outputs), jnp.float32)],
        out_shape=[
            jax.ShapeDtypeStruct((toks, columns), jnp.bfloat16),
            jax.ShapeDtypeStruct((ctx, rows, padded_outputs), jnp.bfloat16),
        ],
        compiler_params=pltpu.CompilerParams(vmem_limit_bytes=24 << 20),
        cost_estimate=pl.CostEstimate(
            flops=2 * toks * slots * width * outputs,
            bytes_accessed=6 * pieces.size + 2 * select_parts.size,
            transcendentals=pieces.size,
        ),
        name="conv_select",
    )(seg_col, pieces, conv_weight, conv_bias, early, select_parts, select_parts)


def normalise_kernel(rank, part_ref, out_ref):
    pieces = part_ref.shape[0]
    total = part_ref[0].astype(jnp.float32)
    for piece in range(1, pieces):
        total = total + part_ref[piece].astype(jnp.float32)
    low = total[:, :rank]
    scale = lax.rsqrt(jnp.mean(low * low, axis=-1, keepdims=True) + 1e-06)
    low = (low * scale).astype(out_ref.dtype)
    maps = total[:, rank:].astype(out_ref.dtype)
    for piece in range(pieces):
        out_ref[piece, :, :rank] = low
        out_ref[piece, :, rank:] = maps


def normalise(parts, rank):
    return pl.pallas_call(
        functools.partial(normalise_kernel, rank),
        out_shape=jax.ShapeDtypeStruct(parts.shape, jnp.bfloat16),
        compiler_params=pltpu.CompilerParams(vmem_limit_bytes=12 << 20),
        name="normalise",
    )(parts)


def scan_kernel(rank, first_shard, reset_hbm, low_hbm, weight_hbm, bias_ref, decay_ref, gain_ref,
                conv_early_hbm, conv_late_hbm, out_ref, reset_ref, low_ref, weight_ref, conv_ref, sems, in_cols, out_diag, delta_rows, drive_rows, held_even, held_odd):
    toks = low_ref.shape[0]
    states = decay_ref.shape[0]
    shards = weight_ref.shape[0]
    width = weight_ref.shape[2]
    tiles = shards * width // LANES
    column = first_shard * width
    low_copy = pltpu.make_async_copy(low_hbm, low_ref, sems.at[0])
    low_copy.start()
    copies = [
        pltpu.make_async_copy(weight_hbm.at[pl.ds(first_shard, shards)], weight_ref, sems.at[1]),
        pltpu.make_async_copy(reset_hbm, reset_ref, sems.at[2]),
    ]
    middle = conv_early_hbm.shape[1]
    end = column + shards * width
    for source, start, low_end, high_end in (
        (conv_early_hbm, 0, column, min(end, middle)),
        (conv_late_hbm, middle, max(column, middle), end),
    ):
        if low_end < high_end:
            size = high_end - low_end
            copies.append(
                pltpu.make_async_copy(
                    source.at[:, pl.ds(low_end - start, size)],
                    conv_ref.at[:, pl.ds(low_end - column, size)],
                    sems.at[1 + len(copies)],
                )
            )
    for copy in copies:
        copy.start()
    low_copy.wait()
    rows = out_ref.shape[1]
    block = 16
    span = block * states
    count = toks // block

    in_cols[...] = jnp.transpose(low_ref[:, rank : rank + LANES].astype(jnp.float32))[0:states, :]
    bits = states.bit_length() - 1
    lane = lax.broadcasted_iota(jnp.int32, (states, span), 1)
    spread = jnp.where((lane & (states - 1)) == lax.broadcasted_iota(jnp.int32, (states, span), 0), 1.0, 0.0)
    spread_out = jnp.dot(
        low_ref[:, rank + states : rank + 2 * states], spread.astype(jnp.bfloat16), preferred_element_type=jnp.float32
    )
    here = lax.shift_right_logical(lax.broadcasted_iota(jnp.int32, (block, span), 1), bits)
    there = lax.broadcasted_iota(jnp.int32, (block, span), 0)
    keep = jnp.where(here == there, 1.0, 0.0)
    out_diag[...] = (spread_out.reshape(count, block, span) * keep[None]).reshape(toks, span).astype(jnp.bfloat16)

    for copy in copies:
        copy.wait()
    reset = jnp.broadcast_to(reset_ref[...], (toks, LANES))
    low = low_ref[:, 0:rank]
    for shard in range(shards):
        pre = jnp.dot(low, weight_ref[shard], preferred_element_type=jnp.float32)
        for part in range(width // LANES):
            tile = shard * (width // LANES) + part
            lanes = slice(tile * LANES, (tile + 1) * LANES)
            value = pre[:, part * LANES : (part + 1) * LANES]
            value = value + bias_ref[:, column + tile * LANES : column + (tile + 1) * LANES]
            raised = jnp.exp2(jnp.minimum(value, 80.0) * LOG2E)
            small = raised - 0.5 * raised * raised
            delta = jnp.maximum(value, jnp.where(raised < 0.01, small, jnp.log(1.0 + raised)))
            delta_rows[:, tile] = (delta + reset).reshape(count, block, LANES)
            drive_rows[:, tile] = (delta * conv_ref[:, lanes].astype(jnp.float32)).reshape(count, block, LANES)

    rates = [
        -LOG2E * jnp.exp(decay_ref[:, column + tile * LANES : column + (tile + 1) * LANES]) for tile in range(tiles)
    ]

    wide = tiles * LANES
    cut = 2 * LANES
    cuts = -(-wide // cut)

    def finish(index, history, part):
        first = pl.multiple_of(index * block, block)
        lanes = slice(part * cut, min((part + 1) * cut, wide))
        mixed = jnp.dot(out_diag[pl.ds(first, block), :], history[:, lanes], preferred_element_type=jnp.float32)
        gain = gain_ref[:, column + lanes.start : column + lanes.stop]
        full = mixed + gain * conv_ref[pl.ds(first, block), lanes].astype(jnp.float32)
        place = pl.multiple_of(lax.rem(first, rows), block)
        out_ref[lax.div(first, rows), pl.ds(place, block), lanes] = full.astype(out_ref.dtype)

    def advance(index, held, history, before, before_history):
        held = list(held)
        per_row = LANES // block
        columns = in_cols[:, pl.ds(pl.multiple_of(lax.div(index, per_row) * LANES, LANES), LANES)]
        columns = pltpu.roll(columns, lax.rem(LANES - lax.rem(index, per_row) * block, LANES), 1)
        delta_now = delta_rows.at[index]
        drive_now = drive_rows.at[index]
        for inner in range(block):
            into = jnp.broadcast_to(columns[:, inner : inner + 1], (states, LANES))
            for tile in range(tiles):
                lanes = slice(tile * LANES, (tile + 1) * LANES)
                grow = jnp.exp2(delta_now[tile, inner : inner + 1, :] * rates[tile])
                held[tile] = grow * held[tile] + into * drive_now[tile, inner : inner + 1, :]
                history[inner * states : (inner + 1) * states, lanes] = held[tile].astype(jnp.bfloat16)
            if inner % (block // cuts) == 0 and inner // (block // cuts) < cuts:
                finish(before, before_history, inner // (block // cuts))
        return tuple(held)

    held_odd[...] = jnp.zeros_like(held_odd)

    def pair(index, held):
        held = advance(2 * index, held, held_even, jnp.maximum(2 * index - 1, 0), held_odd)
        return advance(2 * index + 1, held, held_odd, 2 * index, held_even)

    start = tuple(jnp.zeros((states, LANES), jnp.float32) for _ in range(tiles))
    lax.fori_loop(0, count // 2, pair, start)
    for part in range(cuts):
        finish(count - 1, held_odd, part)


def state_scan(reset_col, low, delta_parts, bias, decay, gain, convs, ctx, first_shard, shards):
    toks = low.shape[0]
    rank, width = delta_parts.shape[1:]
    states = decay.shape[0]
    rows = toks // ctx
    wide = shards * width
    steps = toks * wide * states
    whole = pl.BlockSpec(memory_space=pltpu.VMEM)
    left = pl.BlockSpec(memory_space=pl.ANY)
    return pl.pallas_call(
        functools.partial(scan_kernel, rank, first_shard),
        in_specs=[left, left, left, whole, whole, whole, left, left],
        out_specs=whole,
        out_shape=jax.ShapeDtypeStruct((ctx, rows, wide), jnp.bfloat16),
        scratch_shapes=[
            pltpu.VMEM(reset_col.shape, reset_col.dtype),
            pltpu.VMEM(low.shape, low.dtype),
            pltpu.VMEM((shards, rank, width), jnp.bfloat16),
            pltpu.VMEM((toks, wide), jnp.bfloat16),
            pltpu.SemaphoreType.DMA((5,)),
            pltpu.VMEM((states, toks), jnp.float32),
            pltpu.VMEM((toks, 16 * states), jnp.bfloat16),
            pltpu.VMEM((toks // 16, wide // LANES, 16, LANES), jnp.float32),
            pltpu.VMEM((toks // 16, wide // LANES, 16, LANES), jnp.float32),
            pltpu.VMEM((16 * states, wide), jnp.bfloat16),
            pltpu.VMEM((16 * states, wide), jnp.bfloat16),
        ],
        compiler_params=pltpu.CompilerParams(vmem_limit_bytes=60 << 20),
        cost_estimate=pl.CostEstimate(
            flops=6 * steps, bytes_accessed=2 * shards * rank * width + 4 * toks * wide, transcendentals=steps
        ),
        name=f"state_scan_{first_shard}",
    )(reset_col, low, delta_parts, bias, decay, gain, *convs)


def gate_kernel(fold, width, gate_ref, *refs):
    out_ref = refs[-1]
    slot = 0
    for y_ref in refs[:-1]:
        ctx, _, wide = y_ref.shape
        for place in range(wide // width):
            for piece in range(ctx):
                lanes = piece_lanes(slot, piece, ctx, fold, width)
                value = y_ref[piece, :, place * width : (place + 1) * width].astype(jnp.float32)
                out_ref[:, lanes] = (value * silu(gate_ref[:, lanes].astype(jnp.float32))).astype(out_ref.dtype)
            slot += 1


def apply_gate(parts, gate, fold, width):
    rows, channels = gate.shape
    ctx = parts[0].shape[0]
    part = min(rows, 32)
    columns = pl.BlockSpec((part, channels), lambda r: (r, 0))
    return pl.pallas_call(
        functools.partial(gate_kernel, fold, width),
        grid=(rows // part,),
        in_specs=[columns] + [pl.BlockSpec((ctx, part, array.shape[2]), lambda r: (0, r, 0)) for array in parts],
        out_specs=columns,
        out_shape=jax.ShapeDtypeStruct(gate.shape, jnp.bfloat16),
        compiler_params=pltpu.CompilerParams(vmem_limit_bytes=16 << 20),
        cost_estimate=pl.CostEstimate(flops=4 * gate.size, bytes_accessed=6 * gate.size, transcendentals=gate.size),
        name="gate",
    )(gate, *parts)


def shifted(value, axis, by):
    size = lax.axis_size(axis)
    pairs = [(i, i + by) for i in range(size) if 0 <= i + by < size]
    return lax.ppermute(value, axis, pairs)


def exchange(value):
    return lax.all_to_all(value, "ctx", 0, 0, tiled=True)


def local(
    queries,
    keys,
    values,
    mixer_input,
    gate_input,
    segment_ids,
    conv_weight,
    conv_bias,
    select_weight,
    delta_weight,
    delta_bias,
    decay_log,
    skip_gain,
):
    ctx = lax.axis_size("ctx")
    shards = lax.axis_size("rep")
    place = lax.axis_index("ctx")
    rows, channels = mixer_input.shape[1:]
    rank = delta_weight.shape[0]
    states = decay_log.shape[1]
    width = max(channels // (shards * ctx), LANES)
    fold = width * shards * ctx // channels
    seg = segment_ids[0]
    toks = seg.shape[0]
    seg_col = seg[:, None]
    back = min(ctx - 1, -(-(toks // 2 - 1) // rows))

    slots = shards // fold

    def own_part(array):
        cut = array.reshape(array.shape[:-1] + (slots, fold, ctx // fold, width))
        cut = lax.dynamic_index_in_dim(cut, place // fold, cut.ndim - 2, keepdims=False)
        cut = lax.dynamic_index_in_dim(cut, place % fold, cut.ndim - 2, keepdims=False)
        return cut.reshape(array.shape[:-1] + (slots * width,))

    def own_columns(weight):
        return lax.dynamic_slice_in_dim(weight, place // fold * width, width, 1)

    def gathered(own):
        parts = lax.all_gather(own, "rep", axis=0)
        if fold > 1:
            parts = parts.reshape((slots, fold) + own.shape)
            parts = lax.dynamic_index_in_dim(parts, place % fold, 1, keepdims=False)
        return parts

    select_parts = gathered(own_columns(select_weight))
    packed = [pack(mixer_input[0], ctx, fold, width, half) for half in range(2)]

    same = jnp.concatenate([jnp.zeros((1,), bool), seg[1:] == seg[:-1]])
    reset_col = jnp.where(same, 0.0, FAR)[:, None]
    seg_pad = jnp.concatenate([jnp.full((back * rows,), -1, jnp.int32), seg])
    seg_k = lax.dynamic_slice_in_dim(seg_pad, place * rows, (back + 1) * rows, 0)
    own = (
        own_part(delta_bias)[None, :],
        own_part(jnp.transpose(decay_log)),
        own_part(skip_gain)[None, :],
        reset_col,
        seg_k[back * rows :, None],
        seg_k[None, :],
        jnp.concatenate([keys[0], values[0]], axis=1),
        own_part(conv_weight),
        own_part(conv_bias)[None, :],
        seg_col,
        own_columns(delta_weight),
    )
    early_pieces, own = lax.optimization_barrier((exchange(packed[0]), own))
    late_pieces = exchange(packed[1])
    bias, decay, gain, reset_col, seg_q, seg_k, both, conv_weight, conv_bias, seg_col, delta_own = own
    delta_parts = gathered(delta_own)

    early = conv_early(seg_col, early_pieces, conv_weight, conv_bias, width)
    late, parts = conv_select(seg_col, late_pieces, conv_weight, conv_bias, early, select_parts)
    low = normalise(exchange(parts), rank)

    low, both = lax.optimization_barrier((low, both))
    blocks = [shifted(both, "ctx", by) for by in range(back, 0, -1)] + [both]
    low = exchange(low).reshape(toks, low.shape[2])

    split = slots * 5 // 8
    scanned = [
        state_scan(reset_col, low, delta_parts, bias, decay, gain, (early, late), ctx, first, count)
        for first, count in ((0, split), (split, slots - split))
    ]
    scanned[0], blocks = lax.optimization_barrier((scanned[0], blocks))
    attended = attention(queries[0], blocks, seg_q, seg_k, 0, KEY_VALUE_HEADS)
    scanned = [exchange(part) for part in scanned]
    scanned[0], attended = lax.optimization_barrier((scanned[0], attended))
    mixed = apply_gate(scanned, gate_input[0], fold, width)
    return (attended[None], mixed[None])


def solution(mesh):
    placed = (
        P("rep", "ctx", None),
        P("rep", "ctx", None),
        P("rep", "ctx", None),
        P("rep", "ctx", None),
        P("rep", "ctx", None),
        P("rep", None),
        P(),
        P(),
        P(None, "rep"),
        P(None, "rep"),
        P(),
        P(),
        P(),
    )
    return jax.shard_map(
        local,
        mesh=mesh,
        in_specs=placed,
        out_specs=(P("rep", "ctx", None), P("rep", "ctx", None)),
        check_vma=False,
    )
```

```python
import functools
import math

import jax
import jax.numpy as jnp
from jax import lax
from jax.experimental import pallas as pl
from jax.experimental.pallas import tpu as pltpu
from jax.sharding import PartitionSpec as P

QUERY_HEADS = 32
KEY_VALUE_HEADS = 4
HEAD_WIDTH = 128
LANES = 128
SUBLANES = 8
LOG2E = 1.0 / math.log(2.0)
FAR = 1e30


def silu(value):
    half = 0.5 * value
    return half + half * jnp.tanh(half)


def attention_kernel(begin, seg_q_ref, seg_k_ref, q_ref, *refs):
    out_ref = refs[-1]
    refs = refs[: -1 if begin == 0 else -2]
    rows = q_ref.shape[0]
    span = seg_k_ref.shape[1]
    groups = QUERY_HEADS // KEY_VALUE_HEADS
    row = lax.broadcasted_iota(jnp.int32, (rows, span), 0) + (span - rows)
    col = lax.broadcasted_iota(jnp.int32, (rows, span), 1)
    allowed = (col <= row) & (seg_q_ref[...] == seg_k_ref[...])
    shift = jnp.where(allowed, 0.0, -FAR)
    keys = jnp.concatenate([ref[...] for ref in refs[0::2]], axis=0)
    vals = jnp.concatenate([ref[...] for ref in refs[1::2]], axis=0)
    factor = LOG2E / math.sqrt(HEAD_WIDTH)
    batch = 4
    for first in range(0, groups, batch):
        cuts = [slice(head * HEAD_WIDTH, (head + 1) * HEAD_WIDTH) for head in range(first, first + batch)]
        scores = [
            lax.dot_general(q_ref[:, cut], keys, (((1,), (1,)), ((), ())), preferred_element_type=jnp.float32)
            for cut in cuts
        ]
        scores = [score + shift for score in scores]
        tops = [jnp.max(score, axis=-1, keepdims=True) for score in scores]
        weights = [jnp.exp2((score - top) * factor) for score, top in zip(scores, tops)]
        norms = [jnp.sum(weight, axis=-1, keepdims=True) for weight in weights]
        totals = [jnp.dot(weight.astype(jnp.bfloat16), vals, preferred_element_type=jnp.float32) for weight in weights]
        for cut, total, norm in zip(cuts, totals, norms):
            out_ref[:, cut] = (total / norm).astype(out_ref.dtype)


def attention(queries, blocks, seg_q, seg_k, begin, end, before=None):
    rows = queries.shape[0]
    span = seg_k.shape[1]
    group_width = QUERY_HEADS // KEY_VALUE_HEADS * HEAD_WIDTH
    key_spec = pl.BlockSpec((rows, HEAD_WIDTH), lambda h: (0, begin + h))
    value_spec = pl.BlockSpec((rows, HEAD_WIDTH), lambda h: (0, KEY_VALUE_HEADS + begin + h))
    wide = pl.BlockSpec((rows, group_width), lambda h: (0, begin + h))
    operands = [seg_q, seg_k, queries] + [block for block in blocks for _ in range(2)]
    in_specs = [
        pl.BlockSpec((rows, 1), lambda h: (0, 0)),
        pl.BlockSpec((1, span), lambda h: (0, 0)),
        wide,
        *([key_spec, value_spec] * len(blocks)),
    ]
    aliases = {}
    if before is not None:
        aliases = {len(operands): 0}
        operands.append(before)
        in_specs.append(pl.BlockSpec(memory_space=pl.ANY))
    return pl.pallas_call(
        functools.partial(attention_kernel, begin),
        grid=(end - begin,),
        in_specs=in_specs,
        out_specs=wide,
        out_shape=jax.ShapeDtypeStruct(queries.shape, jnp.bfloat16),
        input_output_aliases=aliases,
        compiler_params=pltpu.CompilerParams(vmem_limit_bytes=40 << 20),
        cost_estimate=pl.CostEstimate(
            flops=4 * rows * span * group_width * (end - begin),
            bytes_accessed=4 * rows * group_width * (end - begin),
            transcendentals=rows * span * group_width // HEAD_WIDTH * (end - begin),
        ),
        name=f"attention_{begin}",
    )(*operands)


def piece_lanes(slot, piece, ctx, fold, width):
    start = (slot * ctx + piece % fold * (ctx // fold) + piece // fold) * width
    return slice(start, start + width)


def pack_kernel(fold, width, x_ref, out_ref):
    ctx = out_ref.shape[0]
    for piece in range(ctx):
        for slot in range(out_ref.shape[2] // width):
            out_ref[piece, :, slot * width : (slot + 1) * width] = x_ref[:, piece_lanes(slot, piece, ctx, fold, width)]


def pack(value, ctx, fold, width):
    rows, channels = value.shape
    part = min(rows, 32)
    return pl.pallas_call(
        functools.partial(pack_kernel, fold, width),
        grid=(rows // part,),
        in_specs=[pl.BlockSpec((part, channels), lambda r: (r, 0))],
        out_specs=pl.BlockSpec((ctx, part, channels // ctx), lambda r: (0, r, 0)),
        out_shape=jax.ShapeDtypeStruct((ctx, rows, channels // ctx), value.dtype),
        compiler_params=pltpu.CompilerParams(vmem_limit_bytes=12 << 20),
        name="pack",
    )(value)


def conv_select_kernel(seg_ref, x_ref, weight_ref, bias_ref, select_ref, conv_ref, part_ref, masks, padded, total):
    step = pl.program_id(0)
    toks = seg_ref.shape[0]
    pieces, rows, wide = x_ref.shape
    tiles = wide // LANES
    slots, outputs, width = select_ref.shape

    @pl.when(step == 0)
    def _():
        wide_seg = jnp.broadcast_to(seg_ref[...], (toks, LANES)).astype(jnp.float32)
        padded[0, 0:SUBLANES, :] = jnp.full((SUBLANES, LANES), -1.0, jnp.float32)
        padded[0, SUBLANES : SUBLANES + toks, :] = wide_seg
        for tap in range(3):
            before = padded[0, SUBLANES - 3 + tap : SUBLANES - 3 + tap + toks, :]
            masks[tap] = jnp.where(before == wide_seg, 1.0, 0.0)
        for tile in range(tiles):
            padded[tile, 0:SUBLANES, :] = jnp.zeros((SUBLANES, LANES), jnp.float32)
        total[...] = jnp.zeros_like(total)

    outs = []
    for tile in range(tiles):
        lanes = slice(tile * LANES, (tile + 1) * LANES)
        for piece in range(pieces):
            first = SUBLANES + piece * rows
            padded[tile, first : first + rows, :] = x_ref[piece, :, lanes].astype(jnp.float32)
        half = jnp.broadcast_to(0.5 * bias_ref[0:1, lanes], (toks, LANES))
        for tap in range(4):
            moved = padded[tile, SUBLANES - 3 + tap : SUBLANES - 3 + tap + toks, :]
            term = (0.5 * weight_ref[tap : tap + 1, lanes]) * moved
            half = half + (term * masks[tap] if tap < 3 else term)
        conv = (half + half * jnp.tanh(half)).astype(jnp.bfloat16)
        conv_ref[:, lanes] = conv
        outs.append(conv)
    conv = jnp.concatenate(outs, axis=1)
    select = jnp.concatenate([select_ref[slot] for slot in range(slots)], axis=1)
    total[...] += lax.dot_general(conv, select, (((1,), (1,)), ((), ())), preferred_element_type=jnp.float32)

    @pl.when(step == pl.num_programs(0) - 1)
    def _():
        spare = part_ref.shape[2] - outputs
        for piece in range(pieces):
            part_ref[piece, :, 0:outputs] = total[piece * rows : (piece + 1) * rows, :].astype(part_ref.dtype)
            part_ref[piece, :, outputs:] = jnp.zeros((rows, spare), part_ref.dtype)


def conv_select(seg_col, pieces, conv_weight, conv_bias, select_parts):
    slots, outputs, width = select_parts.shape
    ctx, rows, _ = pieces.shape
    toks = ctx * rows
    padded_outputs = -(-outputs // LANES) * LANES
    batch = 4
    wide = batch * width
    return pl.pallas_call(
        conv_select_kernel,
        grid=(slots // batch,),
        in_specs=[
            pl.BlockSpec((toks, 1), lambda s: (0, 0)),
            pl.BlockSpec((ctx, rows, wide), lambda s: (0, 0, s)),
            pl.BlockSpec((4, wide), lambda s: (0, s)),
            pl.BlockSpec((1, wide), lambda s: (0, s)),
            pl.BlockSpec((batch, outputs, width), lambda s: (s, 0, 0)),
        ],
        out_specs=[
            pl.BlockSpec((toks, wide), lambda s: (0, s)),
            pl.BlockSpec((ctx, rows, padded_outputs), lambda s: (0, 0, 0)),
        ],
        scratch_shapes=[
            pltpu.VMEM((3, toks, LANES), jnp.float32),
            pltpu.VMEM((wide // LANES, SUBLANES + toks, LANES), jnp.float32),
            pltpu.VMEM((toks, outputs), jnp.float32),
        ],
        out_shape=[
            jax.ShapeDtypeStruct((toks, slots * width), jnp.bfloat16),
            jax.ShapeDtypeStruct((ctx, rows, padded_outputs), jnp.bfloat16),
        ],
        compiler_params=pltpu.CompilerParams(vmem_limit_bytes=32 << 20),
        cost_estimate=pl.CostEstimate(
            flops=2 * toks * slots * width * outputs,
            bytes_accessed=2 * pieces.size * 2 + 2 * select_parts.size,
            transcendentals=pieces.size,
        ),
        name="conv_select",
    )(seg_col, pieces, conv_weight, conv_bias, select_parts)


def normalise_kernel(rank, part_ref, out_ref):
    pieces = part_ref.shape[0]
    total = part_ref[0].astype(jnp.float32)
    for piece in range(1, pieces):
        total = total + part_ref[piece].astype(jnp.float32)
    low = total[:, :rank]
    scale = lax.rsqrt(jnp.mean(low * low, axis=-1, keepdims=True) + 1e-06)
    low = (low * scale).astype(out_ref.dtype)
    maps = total[:, rank:].astype(out_ref.dtype)
    for piece in range(pieces):
        out_ref[piece, :, :rank] = low
        out_ref[piece, :, rank:] = maps


def normalise(parts, rank):
    return pl.pallas_call(
        functools.partial(normalise_kernel, rank),
        out_shape=jax.ShapeDtypeStruct(parts.shape, jnp.bfloat16),
        compiler_params=pltpu.CompilerParams(vmem_limit_bytes=12 << 20),
        name="normalise",
    )(parts)


def scan_kernel(rank, first_shard, reset_hbm, low_hbm, weight_hbm, bias_ref, decay_ref, gain_ref,
                conv_hbm, out_ref, reset_ref, low_ref, weight_ref, conv_ref, sems, in_cols, out_diag, delta_rows, drive_rows, held_even, held_odd):
    toks = low_ref.shape[0]
    states = decay_ref.shape[0]
    shards = weight_ref.shape[0]
    width = weight_ref.shape[2]
    tiles = shards * width // LANES
    column = first_shard * width
    low_copy = pltpu.make_async_copy(low_hbm, low_ref, sems.at[0])
    reset_copy = pltpu.make_async_copy(reset_hbm, reset_ref, sems.at[1])
    low_copy.start()
    reset_copy.start()
    shard_copies = []
    for shard in range(shards):
        at = shard * width
        shard_copies += [
            pltpu.make_async_copy(weight_hbm.at[first_shard + shard], weight_ref.at[shard], sems.at[2 + 2 * shard]),
            pltpu.make_async_copy(
                conv_hbm.at[:, pl.ds(column + at, width)], conv_ref.at[:, pl.ds(at, width)], sems.at[3 + 2 * shard]
            ),
        ]
    for copy in shard_copies:
        copy.start()
    low_copy.wait()
    rows = out_ref.shape[1]
    block = 16
    span = block * states
    count = toks // block

    in_cols[...] = jnp.transpose(low_ref[:, rank : rank + LANES].astype(jnp.float32))[0:states, :]
    bits = states.bit_length() - 1
    lane = lax.broadcasted_iota(jnp.int32, (states, span), 1)
    spread = jnp.where((lane & (states - 1)) == lax.broadcasted_iota(jnp.int32, (states, span), 0), 1.0, 0.0)
    spread_out = jnp.dot(
        low_ref[:, rank + states : rank + 2 * states], spread.astype(jnp.bfloat16), preferred_element_type=jnp.float32
    )
    here = lax.shift_right_logical(lax.broadcasted_iota(jnp.int32, (block, span), 1), bits)
    there = lax.broadcasted_iota(jnp.int32, (block, span), 0)
    keep = jnp.where(here == there, 1.0, 0.0)
    out_diag[...] = (spread_out.reshape(count, block, span) * keep[None]).reshape(toks, span).astype(jnp.bfloat16)

    reset_copy.wait()
    reset = jnp.broadcast_to(reset_ref[...], (toks, LANES))
    low = low_ref[:, 0:rank]
    for shard in range(shards):
        shard_copies[2 * shard].wait()
        shard_copies[2 * shard + 1].wait()
        pre = jnp.dot(low, weight_ref[shard], preferred_element_type=jnp.float32)
        for part in range(width // LANES):
            tile = shard * (width // LANES) + part
            lanes = slice(tile * LANES, (tile + 1) * LANES)
            value = pre[:, part * LANES : (part + 1) * LANES]
            value = value + bias_ref[:, column + tile * LANES : column + (tile + 1) * LANES]
            raised = jnp.exp2(jnp.minimum(value, 80.0) * LOG2E)
            small = raised - 0.5 * raised * raised
            delta = jnp.maximum(value, jnp.where(raised < 0.01, small, jnp.log(1.0 + raised)))
            delta_rows[:, tile] = (delta + reset).reshape(count, block, LANES)
            drive_rows[:, tile] = (delta * conv_ref[:, lanes].astype(jnp.float32)).reshape(count, block, LANES)

    rates = [
        -LOG2E * jnp.exp(decay_ref[:, column + tile * LANES : column + (tile + 1) * LANES]) for tile in range(tiles)
    ]

    wide = tiles * LANES
    cut = 2 * LANES
    cuts = -(-wide // cut)

    def finish(index, history, part):
        first = pl.multiple_of(index * block, block)
        lanes = slice(part * cut, min((part + 1) * cut, wide))
        mixed = jnp.dot(out_diag[pl.ds(first, block), :], history[:, lanes], preferred_element_type=jnp.float32)
        gain = gain_ref[:, column + lanes.start : column + lanes.stop]
        full = mixed + gain * conv_ref[pl.ds(first, block), lanes].astype(jnp.float32)
        place = pl.multiple_of(lax.rem(first, rows), block)
        out_ref[lax.div(first, rows), pl.ds(place, block), lanes] = full.astype(out_ref.dtype)

    def advance(index, held, history, before, before_history):
        held = list(held)
        per_row = LANES // block
        columns = in_cols[:, pl.ds(pl.multiple_of(lax.div(index, per_row) * LANES, LANES), LANES)]
        columns = pltpu.roll(columns, lax.rem(LANES - lax.rem(index, per_row) * block, LANES), 1)
        delta_now = delta_rows.at[index]
        drive_now = drive_rows.at[index]
        for inner in range(block):
            into = jnp.broadcast_to(columns[:, inner : inner + 1], (states, LANES))
            for tile in range(tiles):
                lanes = slice(tile * LANES, (tile + 1) * LANES)
                grow = jnp.exp2(delta_now[tile, inner : inner + 1, :] * rates[tile])
                held[tile] = grow * held[tile] + into * drive_now[tile, inner : inner + 1, :]
                history[inner * states : (inner + 1) * states, lanes] = held[tile].astype(jnp.bfloat16)
            if inner % (block // cuts) == 0 and inner // (block // cuts) < cuts:
                finish(before, before_history, inner // (block // cuts))
        return tuple(held)

    held_odd[...] = jnp.zeros_like(held_odd)

    def pair(index, held):
        held = advance(2 * index, held, held_even, jnp.maximum(2 * index - 1, 0), held_odd)
        return advance(2 * index + 1, held, held_odd, 2 * index, held_even)

    start = tuple(jnp.zeros((states, LANES), jnp.float32) for _ in range(tiles))
    lax.fori_loop(0, count // 2, pair, start)
    for part in range(cuts):
        finish(count - 1, held_odd, part)


def state_scan(reset_col, low, delta_parts, bias, decay, gain, conv, ctx, first_shard, shards):
    toks = low.shape[0]
    rank, width = delta_parts.shape[1:]
    states = decay.shape[0]
    rows = toks // ctx
    wide = shards * width
    steps = toks * wide * states
    whole = pl.BlockSpec(memory_space=pltpu.VMEM)
    left = pl.BlockSpec(memory_space=pl.ANY)
    return pl.pallas_call(
        functools.partial(scan_kernel, rank, first_shard),
        in_specs=[left, left, left, whole, whole, whole, left],
        out_specs=whole,
        out_shape=jax.ShapeDtypeStruct((ctx, rows, wide), jnp.bfloat16),
        scratch_shapes=[
            pltpu.VMEM(reset_col.shape, reset_col.dtype),
            pltpu.VMEM(low.shape, low.dtype),
            pltpu.VMEM((shards, rank, width), jnp.bfloat16),
            pltpu.VMEM((toks, wide), jnp.bfloat16),
            pltpu.SemaphoreType.DMA((2 + 2 * shards,)),
            pltpu.VMEM((states, toks), jnp.float32),
            pltpu.VMEM((toks, 16 * states), jnp.bfloat16),
            pltpu.VMEM((toks // 16, wide // LANES, 16, LANES), jnp.float32),
            pltpu.VMEM((toks // 16, wide // LANES, 16, LANES), jnp.float32),
            pltpu.VMEM((16 * states, wide), jnp.bfloat16),
            pltpu.VMEM((16 * states, wide), jnp.bfloat16),
        ],
        compiler_params=pltpu.CompilerParams(vmem_limit_bytes=60 << 20),
        cost_estimate=pl.CostEstimate(
            flops=6 * steps, bytes_accessed=2 * shards * rank * width + 4 * toks * wide, transcendentals=steps
        ),
        name=f"state_scan_{first_shard}",
    )(reset_col, low, delta_parts, bias, decay, gain, conv)


def gate_kernel(fold, width, gate_ref, *refs):
    out_ref = refs[-1]
    slot = 0
    for y_ref in refs[:-1]:
        ctx, _, wide = y_ref.shape
        for place in range(wide // width):
            for piece in range(ctx):
                lanes = piece_lanes(slot, piece, ctx, fold, width)
                value = y_ref[piece, :, place * width : (place + 1) * width].astype(jnp.float32)
                out_ref[:, lanes] = (value * silu(gate_ref[:, lanes].astype(jnp.float32))).astype(out_ref.dtype)
            slot += 1


def apply_gate(parts, gate, fold, width):
    rows, channels = gate.shape
    ctx = parts[0].shape[0]
    part = min(rows, 32)
    columns = pl.BlockSpec((part, channels), lambda r: (r, 0))
    return pl.pallas_call(
        functools.partial(gate_kernel, fold, width),
        grid=(rows // part,),
        in_specs=[columns] + [pl.BlockSpec((ctx, part, array.shape[2]), lambda r: (0, r, 0)) for array in parts],
        out_specs=columns,
        out_shape=jax.ShapeDtypeStruct(gate.shape, jnp.bfloat16),
        compiler_params=pltpu.CompilerParams(vmem_limit_bytes=16 << 20),
        cost_estimate=pl.CostEstimate(flops=4 * gate.size, bytes_accessed=6 * gate.size, transcendentals=gate.size),
        name="gate",
    )(gate, *parts)


def shifted(value, axis, by):
    size = lax.axis_size(axis)
    pairs = [(i, i + by) for i in range(size) if 0 <= i + by < size]
    return lax.ppermute(value, axis, pairs)


def exchange(value):
    return lax.all_to_all(value, "ctx", 0, 0, tiled=True)


def local(
    queries,
    keys,
    values,
    mixer_input,
    gate_input,
    segment_ids,
    conv_weight,
    conv_bias,
    select_weight,
    delta_weight,
    delta_bias,
    decay_log,
    skip_gain,
):
    ctx = lax.axis_size("ctx")
    shards = lax.axis_size("rep")
    place = lax.axis_index("ctx")
    rows, channels = mixer_input.shape[1:]
    rank = delta_weight.shape[0]
    states = decay_log.shape[1]
    width = max(channels // (shards * ctx), LANES)
    fold = width * shards * ctx // channels
    seg = segment_ids[0]
    toks = seg.shape[0]
    seg_col = seg[:, None]
    back = min(ctx - 1, -(-(toks // 2 - 1) // rows))

    slots = shards // fold

    def own_part(array):
        cut = array.reshape(array.shape[:-1] + (slots, fold, ctx // fold, width))
        cut = lax.dynamic_index_in_dim(cut, place // fold, cut.ndim - 2, keepdims=False)
        cut = lax.dynamic_index_in_dim(cut, place % fold, cut.ndim - 2, keepdims=False)
        return cut.reshape(array.shape[:-1] + (slots * width,))

    def own_columns(weight):
        return lax.dynamic_slice_in_dim(weight, place // fold * width, width, 1)

    def gathered(own):
        parts = lax.all_gather(own, "rep", axis=0)
        if fold > 1:
            parts = parts.reshape((slots, fold) + own.shape)
            parts = lax.dynamic_index_in_dim(parts, place % fold, 1, keepdims=False)
        return parts

    select_parts = gathered(own_columns(select_weight))
    packed = pack(mixer_input[0], ctx, fold, width)

    same = jnp.concatenate([jnp.zeros((1,), bool), seg[1:] == seg[:-1]])
    reset_col = jnp.where(same, 0.0, FAR)[:, None]
    seg_pad = jnp.concatenate([jnp.full((back * rows,), -1, jnp.int32), seg])
    seg_k = lax.dynamic_slice_in_dim(seg_pad, place * rows, (back + 1) * rows, 0)
    own = (
        own_part(delta_bias)[None, :],
        own_part(jnp.transpose(decay_log)),
        own_part(skip_gain)[None, :],
        reset_col,
        seg_k[back * rows :, None],
        seg_k[None, :],
        jnp.concatenate([keys[0], values[0]], axis=1),
        own_part(conv_weight),
        own_part(conv_bias)[None, :],
        seg_col,
        own_columns(delta_weight),
    )
    pieces, own = lax.optimization_barrier((exchange(packed), own))
    bias, decay, gain, reset_col, seg_q, seg_k, both, conv_weight, conv_bias, seg_col, delta_own = own
    delta_parts = gathered(delta_own)

    conv, parts = conv_select(seg_col, pieces, conv_weight, conv_bias, select_parts)
    low = normalise(exchange(parts), rank)

    low, both = lax.optimization_barrier((low, both))
    blocks = [shifted(both, "ctx", by) for by in range(back, 0, -1)] + [both]
    low, blocks = lax.optimization_barrier((exchange(low), blocks))
    low = low.reshape(toks, low.shape[2])

    split = slots * 3 // 4
    scanned = [
        state_scan(reset_col, low, delta_parts, bias, decay, gain, conv, ctx, first, count)
        for first, count in ((0, split), (split, slots - split))
    ]
    scanned[0], blocks = lax.optimization_barrier((scanned[0], blocks))
    attended = attention(queries[0], blocks, seg_q, seg_k, 0, KEY_VALUE_HEADS)
    scanned = [exchange(part) for part in scanned]
    scanned[0], attended = lax.optimization_barrier((scanned[0], attended))
    mixed = apply_gate(scanned, gate_input[0], fold, width)
    return (attended[None], mixed[None])


def solution(mesh):
    placed = (
        P("rep", "ctx", None),
        P("rep", "ctx", None),
        P("rep", "ctx", None),
        P("rep", "ctx", None),
        P("rep", "ctx", None),
        P("rep", None),
        P(),
        P(),
        P(None, "rep"),
        P(None, "rep"),
        P(),
        P(),
        P(),
    )
    return jax.shard_map(
        local,
        mesh=mesh,
        in_specs=placed,
        out_specs=(P("rep", "ctx", None), P("rep", "ctx", None)),
        check_vma=False,
    )
```

```python
import functools
import math

import jax
import jax.numpy as jnp
from jax import lax
from jax.experimental import pallas as pl
from jax.experimental.pallas import tpu as pltpu
from jax.sharding import PartitionSpec as P

QUERY_HEADS = 32
KEY_VALUE_HEADS = 4
HEAD_WIDTH = 128
LANES = 128
SUBLANES = 8
LOG2E = 1.0 / math.log(2.0)
FAR = 1e30


def silu(value):
    half = 0.5 * value
    return half + half * jnp.tanh(half)


def attention_kernel(begin, seg_q_ref, seg_k_ref, q_ref, *refs):
    out_ref = refs[-1]
    refs = refs[: -1 if begin == 0 else -2]
    rows = q_ref.shape[0]
    span = seg_k_ref.shape[1]
    groups = QUERY_HEADS // KEY_VALUE_HEADS
    row = lax.broadcasted_iota(jnp.int32, (rows, span), 0) + (span - rows)
    col = lax.broadcasted_iota(jnp.int32, (rows, span), 1)
    allowed = (col <= row) & (seg_q_ref[...] == seg_k_ref[...])
    shift = jnp.where(allowed, 0.0, -FAR)
    keys = jnp.concatenate([ref[...] for ref in refs[0::2]], axis=0)
    vals = jnp.concatenate([ref[...] for ref in refs[1::2]], axis=0)
    factor = LOG2E / math.sqrt(HEAD_WIDTH)
    batch = 4
    for first in range(0, groups, batch):
        cuts = [slice(head * HEAD_WIDTH, (head + 1) * HEAD_WIDTH) for head in range(first, first + batch)]
        scores = [
            lax.dot_general(q_ref[:, cut], keys, (((1,), (1,)), ((), ())), preferred_element_type=jnp.float32)
            for cut in cuts
        ]
        scores = [score + shift for score in scores]
        tops = [jnp.max(score, axis=-1, keepdims=True) for score in scores]
        weights = [jnp.exp2((score - top) * factor) for score, top in zip(scores, tops)]
        norms = [jnp.sum(weight, axis=-1, keepdims=True) for weight in weights]
        totals = [jnp.dot(weight.astype(jnp.bfloat16), vals, preferred_element_type=jnp.float32) for weight in weights]
        for cut, total, norm in zip(cuts, totals, norms):
            out_ref[:, cut] = (total / norm).astype(out_ref.dtype)


def attention(queries, blocks, seg_q, seg_k, begin, end, before=None):
    rows = queries.shape[0]
    span = seg_k.shape[1]
    group_width = QUERY_HEADS // KEY_VALUE_HEADS * HEAD_WIDTH
    key_spec = pl.BlockSpec((rows, HEAD_WIDTH), lambda h: (0, begin + h))
    value_spec = pl.BlockSpec((rows, HEAD_WIDTH), lambda h: (0, KEY_VALUE_HEADS + begin + h))
    wide = pl.BlockSpec((rows, group_width), lambda h: (0, begin + h))
    operands = [seg_q, seg_k, queries] + [block for block in blocks for _ in range(2)]
    in_specs = [
        pl.BlockSpec((rows, 1), lambda h: (0, 0)),
        pl.BlockSpec((1, span), lambda h: (0, 0)),
        wide,
        *([key_spec, value_spec] * len(blocks)),
    ]
    aliases = {}
    if before is not None:
        aliases = {len(operands): 0}
        operands.append(before)
        in_specs.append(pl.BlockSpec(memory_space=pl.ANY))
    return pl.pallas_call(
        functools.partial(attention_kernel, begin),
        grid=(end - begin,),
        in_specs=in_specs,
        out_specs=wide,
        out_shape=jax.ShapeDtypeStruct(queries.shape, jnp.bfloat16),
        input_output_aliases=aliases,
        compiler_params=pltpu.CompilerParams(vmem_limit_bytes=54 << 20),
        cost_estimate=pl.CostEstimate(
            flops=4 * rows * span * group_width * (end - begin),
            bytes_accessed=4 * rows * group_width * (end - begin),
            transcendentals=rows * span * group_width // HEAD_WIDTH * (end - begin),
        ),
        name=f"attention_{begin}",
    )(*operands)


def piece_lanes(slot, piece, ctx, fold, width):
    start = (slot * ctx + piece % fold * (ctx // fold) + piece // fold) * width
    return slice(start, start + width)


def pack_kernel(fold, width, x_ref, out_ref):
    ctx = out_ref.shape[0]
    for piece in range(ctx):
        for slot in range(out_ref.shape[2] // width):
            out_ref[piece, :, slot * width : (slot + 1) * width] = x_ref[:, piece_lanes(slot, piece, ctx, fold, width)]


def pack(value, ctx, fold, width):
    rows, channels = value.shape
    part = min(rows, 32)
    return pl.pallas_call(
        functools.partial(pack_kernel, fold, width),
        grid=(rows // part,),
        in_specs=[pl.BlockSpec((part, channels), lambda r: (r, 0))],
        out_specs=pl.BlockSpec((ctx, part, channels // ctx), lambda r: (0, r, 0)),
        out_shape=jax.ShapeDtypeStruct((ctx, rows, channels // ctx), value.dtype),
        compiler_params=pltpu.CompilerParams(vmem_limit_bytes=12 << 20),
        name="pack",
    )(value)


def conv_select_kernel(match_ref, x_ref, weight_ref, bias_ref, select_ref, early_ref, late_ref, part_ref, masks, padded, total):
    step = pl.program_id(0)
    pieces, rows, wide = x_ref.shape
    toks = pieces * rows
    tiles = wide // LANES
    slots, outputs, _ = select_ref.shape

    @pl.when(step == 0)
    def _():
        for tap in range(3):
            masks[tap] = jnp.broadcast_to(match_ref[:, tap : tap + 1], (toks, LANES))
        for tile in range(tiles):
            padded[tile, 0:SUBLANES, :] = jnp.zeros((SUBLANES, LANES), jnp.float32)

    outs = []
    for tile in range(tiles):
        lanes = slice(tile * LANES, (tile + 1) * LANES)
        for piece in range(pieces):
            first = SUBLANES + piece * rows
            padded[tile, first : first + rows, :] = x_ref[piece, :, lanes].astype(jnp.float32)
        half = jnp.broadcast_to(0.5 * bias_ref[0:1, lanes], (toks, LANES))
        for tap in range(4):
            moved = padded[tile, SUBLANES - 3 + tap : SUBLANES - 3 + tap + toks, :]
            term = (0.5 * weight_ref[tap : tap + 1, lanes]) * moved
            half = half + (term * masks[tap] if tap < 3 else term)
        outs.append((half + half * jnp.tanh(half)).astype(jnp.bfloat16))
    conv = jnp.concatenate(outs, axis=1)
    select = jnp.concatenate([select_ref[slot] for slot in range(slots)], axis=1)
    added = lax.dot_general(conv, select, (((1,), (1,)), ((), ())), preferred_element_type=jnp.float32)

    @pl.when(step == 0)
    def _():
        early_ref[...] = conv
        total[...] = added

    @pl.when(step == 1)
    def _():
        late_ref[...] = conv
        spare = part_ref.shape[2] - outputs
        full = (total[...] + added).astype(part_ref.dtype)
        for piece in range(pieces):
            part_ref[piece, :, 0:outputs] = full[piece * rows : (piece + 1) * rows, :]
            part_ref[piece, :, outputs:] = jnp.zeros((rows, spare), part_ref.dtype)


def conv_select(match, pieces, conv_weight, conv_bias, select_parts):
    slots, outputs, width = select_parts.shape
    ctx, rows, columns = pieces.shape
    toks = ctx * rows
    padded_outputs = -(-outputs // LANES) * LANES
    wide = columns // 2
    half = pl.BlockSpec((toks, wide), lambda s: (0, 0))
    return pl.pallas_call(
        conv_select_kernel,
        grid=(2,),
        in_specs=[
            pl.BlockSpec(match.shape, lambda s: (0, 0)),
            pl.BlockSpec((ctx, rows, wide), lambda s: (0, 0, s)),
            pl.BlockSpec((4, wide), lambda s: (0, s)),
            pl.BlockSpec((1, wide), lambda s: (0, s)),
            pl.BlockSpec((slots // 2, outputs, width), lambda s: (s, 0, 0)),
        ],
        out_specs=[half, half, pl.BlockSpec((ctx, rows, padded_outputs), lambda s: (0, 0, 0))],
        scratch_shapes=[
            pltpu.VMEM((3, toks, LANES), jnp.float32),
            pltpu.VMEM((wide // LANES, SUBLANES + toks, LANES), jnp.float32),
            pltpu.VMEM((toks, outputs), jnp.float32),
        ],
        out_shape=[
            jax.ShapeDtypeStruct((toks, wide), jnp.bfloat16),
            jax.ShapeDtypeStruct((toks, wide), jnp.bfloat16),
            jax.ShapeDtypeStruct((ctx, rows, padded_outputs), jnp.bfloat16),
        ],
        compiler_params=pltpu.CompilerParams(vmem_limit_bytes=32 << 20),
        cost_estimate=pl.CostEstimate(
            flops=2 * toks * slots * width * outputs,
            bytes_accessed=2 * pieces.size * 2 + 2 * select_parts.size,
            transcendentals=pieces.size,
        ),
        name="conv_select",
    )(match, pieces, conv_weight, conv_bias, select_parts)


def normalise_kernel(rank, part_ref, out_ref):
    pieces = part_ref.shape[0]
    total = part_ref[0].astype(jnp.float32)
    for piece in range(1, pieces):
        total = total + part_ref[piece].astype(jnp.float32)
    low = total[:, :rank]
    scale = lax.rsqrt(jnp.mean(low * low, axis=-1, keepdims=True) + 1e-06)
    low = (low * scale).astype(out_ref.dtype)
    maps = total[:, rank:].astype(out_ref.dtype)
    for piece in range(pieces):
        out_ref[piece, :, :rank] = low
        out_ref[piece, :, rank:] = maps


def normalise(parts, rank):
    return pl.pallas_call(
        functools.partial(normalise_kernel, rank),
        out_shape=jax.ShapeDtypeStruct(parts.shape, jnp.bfloat16),
        compiler_params=pltpu.CompilerParams(vmem_limit_bytes=12 << 20),
        name="normalise",
    )(parts)


def scan_kernel(rank, first_shard, reset_hbm, low_hbm, weight_hbm, bias_ref, decay_ref, gain_ref,
                early_hbm, late_hbm, out_ref, reset_ref, low_ref, weight_ref, conv_ref, sems, in_cols, out_diag, delta_rows, drive_rows, held_even, held_odd):
    toks = low_ref.shape[0]
    states = decay_ref.shape[0]
    shards = weight_ref.shape[0]
    width = weight_ref.shape[2]
    tiles = shards * width // LANES
    column = first_shard * width
    low_copy = pltpu.make_async_copy(low_hbm, low_ref, sems.at[0])
    reset_copy = pltpu.make_async_copy(reset_hbm, reset_ref, sems.at[1])
    low_copy.start()
    reset_copy.start()
    shard_copies = []
    for shard in range(shards):
        at = shard * width
        start = column + at
        middle = early_hbm.shape[1]
        source = early_hbm.at[:, pl.ds(start, width)] if start < middle else late_hbm.at[:, pl.ds(start - middle, width)]
        shard_copies += [
            pltpu.make_async_copy(weight_hbm.at[first_shard + shard], weight_ref.at[shard], sems.at[2 + 2 * shard]),
            pltpu.make_async_copy(source, conv_ref.at[:, pl.ds(at, width)], sems.at[3 + 2 * shard]),
        ]
    for copy in shard_copies:
        copy.start()
    low_copy.wait()
    rows = out_ref.shape[1]
    block = 16
    span = block * states
    count = toks // block

    in_cols[...] = jnp.transpose(low_ref[:, rank : rank + LANES].astype(jnp.float32))[0:states, :]
    bits = states.bit_length() - 1
    lane = lax.broadcasted_iota(jnp.int32, (states, span), 1)
    spread = jnp.where((lane & (states - 1)) == lax.broadcasted_iota(jnp.int32, (states, span), 0), 1.0, 0.0)
    spread_out = jnp.dot(
        low_ref[:, rank + states : rank + 2 * states], spread.astype(jnp.bfloat16), preferred_element_type=jnp.float32
    )
    here = lax.shift_right_logical(lax.broadcasted_iota(jnp.int32, (block, span), 1), bits)
    there = lax.broadcasted_iota(jnp.int32, (block, span), 0)
    keep = jnp.where(here == there, 1.0, 0.0)
    out_diag[...] = (spread_out.reshape(count, block, span) * keep[None]).reshape(toks, span).astype(jnp.bfloat16)

    reset_copy.wait()
    reset = jnp.broadcast_to(reset_ref[...], (toks, LANES))
    low = low_ref[:, 0:rank]
    for shard in range(shards):
        shard_copies[2 * shard].wait()
        shard_copies[2 * shard + 1].wait()
        pre = jnp.dot(low, weight_ref[shard], preferred_element_type=jnp.float32)
        for part in range(width // LANES):
            tile = shard * (width // LANES) + part
            lanes = slice(tile * LANES, (tile + 1) * LANES)
            value = pre[:, part * LANES : (part + 1) * LANES]
            value = value + bias_ref[:, column + tile * LANES : column + (tile + 1) * LANES]
            raised = jnp.exp2(jnp.minimum(value, 80.0) * LOG2E)
            small = raised - 0.5 * raised * raised
            delta = jnp.maximum(value, jnp.where(raised < 0.01, small, jnp.log(1.0 + raised)))
            delta_rows[:, tile] = (delta + reset).reshape(count, block, LANES)
            drive_rows[:, tile] = (delta * conv_ref[:, lanes].astype(jnp.float32)).reshape(count, block, LANES)

    rates = [
        -LOG2E * jnp.exp(decay_ref[:, column + tile * LANES : column + (tile + 1) * LANES]) for tile in range(tiles)
    ]

    wide = tiles * LANES
    cut = 2 * LANES
    cuts = -(-wide // cut)

    def finish(index, history, part):
        first = pl.multiple_of(index * block, block)
        lanes = slice(part * cut, min((part + 1) * cut, wide))
        mixed = jnp.dot(out_diag[pl.ds(first, block), :], history[:, lanes], preferred_element_type=jnp.float32)
        gain = gain_ref[:, column + lanes.start : column + lanes.stop]
        full = mixed + gain * conv_ref[pl.ds(first, block), lanes].astype(jnp.float32)
        place = pl.multiple_of(lax.rem(first, rows), block)
        out_ref[lax.div(first, rows), pl.ds(place, block), lanes] = full.astype(out_ref.dtype)

    def advance(index, held, history, before, before_history):
        held = list(held)
        per_row = LANES // block
        columns = in_cols[:, pl.ds(pl.multiple_of(lax.div(index, per_row) * LANES, LANES), LANES)]
        columns = pltpu.roll(columns, lax.rem(LANES - lax.rem(index, per_row) * block, LANES), 1)
        delta_now = delta_rows.at[index]
        drive_now = drive_rows.at[index]
        for inner in range(block):
            into = jnp.broadcast_to(columns[:, inner : inner + 1], (states, LANES))
            for tile in range(tiles):
                lanes = slice(tile * LANES, (tile + 1) * LANES)
                grow = jnp.exp2(delta_now[tile, inner : inner + 1, :] * rates[tile])
                held[tile] = grow * held[tile] + into * drive_now[tile, inner : inner + 1, :]
                history[inner * states : (inner + 1) * states, lanes] = held[tile].astype(jnp.bfloat16)
            if inner % (block // cuts) == 0 and inner // (block // cuts) < cuts:
                finish(before, before_history, inner // (block // cuts))
        return tuple(held)

    held_odd[...] = jnp.zeros_like(held_odd)

    def pair(index, held):
        held = advance(2 * index, held, held_even, jnp.maximum(2 * index - 1, 0), held_odd)
        return advance(2 * index + 1, held, held_odd, 2 * index, held_even)

    start = tuple(jnp.zeros((states, LANES), jnp.float32) for _ in range(tiles))
    lax.fori_loop(0, count // 2, pair, start)
    for part in range(cuts):
        finish(count - 1, held_odd, part)


def state_scan(reset_col, low, delta_parts, bias, decay, gain, convs, ctx, first_shard, shards):
    toks = low.shape[0]
    rank, width = delta_parts.shape[1:]
    states = decay.shape[0]
    rows = toks // ctx
    wide = shards * width
    steps = toks * wide * states
    whole = pl.BlockSpec(memory_space=pltpu.VMEM)
    left = pl.BlockSpec(memory_space=pl.ANY)
    return pl.pallas_call(
        functools.partial(scan_kernel, rank, first_shard),
        in_specs=[left, left, left, whole, whole, whole, left, left],
        out_specs=whole,
        out_shape=jax.ShapeDtypeStruct((ctx, rows, wide), jnp.bfloat16),
        scratch_shapes=[
            pltpu.VMEM(reset_col.shape, reset_col.dtype),
            pltpu.VMEM(low.shape, low.dtype),
            pltpu.VMEM((shards, rank, width), jnp.bfloat16),
            pltpu.VMEM((toks, wide), jnp.bfloat16),
            pltpu.SemaphoreType.DMA((2 + 2 * shards,)),
            pltpu.VMEM((states, toks), jnp.float32),
            pltpu.VMEM((toks, 16 * states), jnp.bfloat16),
            pltpu.VMEM((toks // 16, wide // LANES, 16, LANES), jnp.float32),
            pltpu.VMEM((toks // 16, wide // LANES, 16, LANES), jnp.float32),
            pltpu.VMEM((16 * states, wide), jnp.bfloat16),
            pltpu.VMEM((16 * states, wide), jnp.bfloat16),
        ],
        compiler_params=pltpu.CompilerParams(vmem_limit_bytes=54 << 20),
        cost_estimate=pl.CostEstimate(
            flops=6 * steps, bytes_accessed=2 * shards * rank * width + 4 * toks * wide, transcendentals=steps
        ),
        name=f"state_scan_{first_shard}",
    )(reset_col, low, delta_parts, bias, decay, gain, *convs)


def gate_kernel(fold, width, gate_ref, *refs):
    out_ref = refs[-1]
    slot = 0
    for y_ref in refs[:-1]:
        ctx, _, wide = y_ref.shape
        for place in range(wide // width):
            for piece in range(ctx):
                lanes = piece_lanes(slot, piece, ctx, fold, width)
                value = y_ref[piece, :, place * width : (place + 1) * width].astype(jnp.float32)
                out_ref[:, lanes] = (value * silu(gate_ref[:, lanes].astype(jnp.float32))).astype(out_ref.dtype)
            slot += 1


def apply_gate(parts, gate, fold, width):
    rows, channels = gate.shape
    ctx = parts[0].shape[0]
    part = min(rows, 32)
    columns = pl.BlockSpec((part, channels), lambda r: (r, 0))
    return pl.pallas_call(
        functools.partial(gate_kernel, fold, width),
        grid=(rows // part,),
        in_specs=[columns] + [pl.BlockSpec((ctx, part, array.shape[2]), lambda r: (0, r, 0)) for array in parts],
        out_specs=columns,
        out_shape=jax.ShapeDtypeStruct(gate.shape, jnp.bfloat16),
        compiler_params=pltpu.CompilerParams(vmem_limit_bytes=16 << 20),
        cost_estimate=pl.CostEstimate(flops=4 * gate.size, bytes_accessed=6 * gate.size, transcendentals=gate.size),
        name="gate",
    )(gate, *parts)


def shifted(value, axis, by):
    size = lax.axis_size(axis)
    pairs = [(i, i + by) for i in range(size) if 0 <= i + by < size]
    return lax.ppermute(value, axis, pairs)


def exchange(value):
    return lax.all_to_all(value, "ctx", 0, 0, tiled=True)


def local(
    queries,
    keys,
    values,
    mixer_input,
    gate_input,
    segment_ids,
    conv_weight,
    conv_bias,
    select_weight,
    delta_weight,
    delta_bias,
    decay_log,
    skip_gain,
):
    ctx = lax.axis_size("ctx")
    shards = lax.axis_size("rep")
    place = lax.axis_index("ctx")
    rows, channels = mixer_input.shape[1:]
    rank = delta_weight.shape[0]
    states = decay_log.shape[1]
    width = max(channels // (shards * ctx), LANES)
    fold = width * shards * ctx // channels
    seg = segment_ids[0]
    toks = seg.shape[0]
    back = min(ctx - 1, -(-(toks // 2 - 1) // rows))

    slots = shards // fold

    def own_part(array):
        cut = array.reshape(array.shape[:-1] + (slots, fold, ctx // fold, width))
        cut = lax.dynamic_index_in_dim(cut, place // fold, cut.ndim - 2, keepdims=False)
        cut = lax.dynamic_index_in_dim(cut, place % fold, cut.ndim - 2, keepdims=False)
        return cut.reshape(array.shape[:-1] + (slots * width,))

    def own_columns(weight):
        return lax.dynamic_slice_in_dim(weight, place // fold * width, width, 1)

    def gathered(own):
        parts = lax.all_gather(own, "rep", axis=0)
        if fold > 1:
            parts = parts.reshape((slots, fold) + own.shape)
            parts = lax.dynamic_index_in_dim(parts, place % fold, 1, keepdims=False)
        return parts

    select_parts = gathered(own_columns(select_weight))
    packed = pack(mixer_input[0], ctx, fold, width)

    same = jnp.concatenate([jnp.zeros((1,), bool), seg[1:] == seg[:-1]])
    reset_col = jnp.where(same, 0.0, FAR)[:, None]
    seg_before = jnp.concatenate([jnp.full((3,), -1, jnp.int32), seg])
    match = jnp.stack([(seg_before[tap : tap + toks] == seg) for tap in range(3)], axis=1).astype(jnp.float32)
    seg_pad = jnp.concatenate([jnp.full((back * rows,), -1, jnp.int32), seg])
    seg_k = lax.dynamic_slice_in_dim(seg_pad, place * rows, (back + 1) * rows, 0)
    own = (
        own_part(delta_bias)[None, :],
        own_part(jnp.transpose(decay_log)),
        own_part(skip_gain)[None, :],
        reset_col,
        seg_k[back * rows :, None],
        seg_k[None, :],
        jnp.concatenate([keys[0], values[0]], axis=1),
        own_part(conv_weight),
        own_part(conv_bias)[None, :],
        match,
        own_columns(delta_weight),
    )
    pieces, own = lax.optimization_barrier((exchange(packed), own))
    bias, decay, gain, reset_col, seg_q, seg_k, both, conv_weight, conv_bias, match, delta_own = own
    delta_parts = gathered(delta_own)

    *convs, parts = conv_select(match, pieces, conv_weight, conv_bias, select_parts)
    low = normalise(exchange(parts), rank)

    low, both = lax.optimization_barrier((low, both))
    blocks = [shifted(both, "ctx", by) for by in range(back, 0, -1)] + [both]
    low = exchange(low).reshape(toks, low.shape[2])

    split = slots * 5 // 8
    scanned = [
        state_scan(reset_col, low, delta_parts, bias, decay, gain, convs, ctx, first, count)
        for first, count in ((0, split), (split, slots - split))
    ]
    scanned[0], blocks = lax.optimization_barrier((scanned[0], blocks))
    attended = attention(queries[0], blocks, seg_q, seg_k, 0, KEY_VALUE_HEADS)
    scanned = [exchange(part) for part in scanned]
    scanned[0], attended = lax.optimization_barrier((scanned[0], attended))
    mixed = apply_gate(scanned, gate_input[0], fold, width)
    return (attended[None], mixed[None])


def solution(mesh):
    placed = (
        P("rep", "ctx", None),
        P("rep", "ctx", None),
        P("rep", "ctx", None),
        P("rep", "ctx", None),
        P("rep", "ctx", None),
        P("rep", None),
        P(),
        P(),
        P(None, "rep"),
        P(None, "rep"),
        P(),
        P(),
        P(),
    )
    return jax.shard_map(
        local,
        mesh=mesh,
        in_specs=placed,
        out_specs=(P("rep", "ctx", None), P("rep", "ctx", None)),
        check_vma=False,
    )
```

```python
import functools
import math

import jax
import jax.numpy as jnp
from jax import lax
from jax.experimental import pallas as pl
from jax.experimental.pallas import tpu as pltpu
from jax.sharding import PartitionSpec as P

QUERY_HEADS = 32
KEY_VALUE_HEADS = 4
HEAD_WIDTH = 128
LANES = 128
SUBLANES = 8
LOG2E = 1.0 / math.log(2.0)
FAR = 1e30


def silu(value):
    half = 0.5 * value
    return half + half * jnp.tanh(half)


def attention_kernel(place_ref, seg_q_ref, seg_k_ref, q_ref, *refs):
    key_refs, value_refs, out_ref = refs[0:-1:2], refs[1:-1:2], refs[-1]
    rows = q_ref.shape[0]
    span = seg_k_ref.shape[1]
    groups = QUERY_HEADS // KEY_VALUE_HEADS
    row = lax.broadcasted_iota(jnp.int32, (rows, span), 0) + (span - rows)
    col = lax.broadcasted_iota(jnp.int32, (rows, span), 1)
    allowed = (col <= row) & (seg_q_ref[...] == seg_k_ref[...])
    shift = jnp.where(allowed, 0.0, -FAR)
    keys = jnp.concatenate([ref[0] for ref in key_refs], axis=0)
    vals = jnp.concatenate([ref[0] for ref in value_refs], axis=0)
    factor = LOG2E / math.sqrt(HEAD_WIDTH)
    batch = 4
    for first in range(0, groups, batch):
        cuts = [slice(head * HEAD_WIDTH, (head + 1) * HEAD_WIDTH) for head in range(first, first + batch)]
        scores = [
            lax.dot_general(q_ref[:, cut], keys, (((1,), (1,)), ((), ())), preferred_element_type=jnp.float32)
            for cut in cuts
        ]
        scores = [score + shift for score in scores]
        tops = [jnp.max(score, axis=-1, keepdims=True) for score in scores]
        weights = [jnp.exp2((score - top) * factor) for score, top in zip(scores, tops)]
        norms = [jnp.sum(weight, axis=-1, keepdims=True) for weight in weights]
        totals = [jnp.dot(weight.astype(jnp.bfloat16), vals, preferred_element_type=jnp.float32) for weight in weights]
        for cut, total, norm in zip(cuts, totals, norms):
            out_ref[:, cut] = (total / norm).astype(out_ref.dtype)


def attention(queries, blocks, seg_q, seg_k, place, back):
    rows = queries.shape[0]
    span = seg_k.shape[1]
    group_width = QUERY_HEADS // KEY_VALUE_HEADS * HEAD_WIDTH
    wide = pl.BlockSpec((rows, group_width), lambda h, p: (0, h))
    in_specs = [
        pl.BlockSpec((rows, 1), lambda h, p: (0, 0)),
        pl.BlockSpec((1, span), lambda h, p: (0, 0)),
        wide,
    ]
    for by in range(back, -1, -1):
        for first in (0, KEY_VALUE_HEADS):
            in_specs.append(
                pl.BlockSpec(
                    (1, rows, HEAD_WIDTH),
                    lambda h, p, by=by, first=first: (jnp.maximum(p[0] - by, 0), 0, first + h),
                )
            )
    return pl.pallas_call(
        attention_kernel,
        grid_spec=pltpu.PrefetchScalarGridSpec(
            num_scalar_prefetch=1, grid=(KEY_VALUE_HEADS,), in_specs=in_specs, out_specs=wide
        ),
        out_shape=jax.ShapeDtypeStruct(queries.shape, jnp.bfloat16),
        compiler_params=pltpu.CompilerParams(vmem_limit_bytes=54 << 20),
        cost_estimate=pl.CostEstimate(
            flops=4 * rows * span * QUERY_HEADS * HEAD_WIDTH,
            bytes_accessed=4 * queries.size,
            transcendentals=rows * span * QUERY_HEADS,
        ),
        name="attention",
    )(place, seg_q, seg_k, queries, *([blocks] * (2 * back + 2)))


def piece_lanes(slot, piece, ctx, fold, width):
    start = (slot * ctx + piece % fold * (ctx // fold) + piece // fold) * width
    return slice(start, start + width)


def pack_kernel(fold, width, x_ref, out_ref):
    ctx = out_ref.shape[0]
    for piece in range(ctx):
        for slot in range(out_ref.shape[2] // width):
            out_ref[piece, :, slot * width : (slot + 1) * width] = x_ref[:, piece_lanes(slot, piece, ctx, fold, width)]


def pack(value, ctx, fold, width):
    rows, channels = value.shape
    part = min(rows, 32)
    return pl.pallas_call(
        functools.partial(pack_kernel, fold, width),
        grid=(rows // part,),
        in_specs=[pl.BlockSpec((part, channels), lambda r: (r, 0))],
        out_specs=pl.BlockSpec((ctx, part, channels // ctx), lambda r: (0, r, 0)),
        out_shape=jax.ShapeDtypeStruct((ctx, rows, channels // ctx), value.dtype),
        compiler_params=pltpu.CompilerParams(vmem_limit_bytes=12 << 20),
        name="pack",
    )(value)


def conv_select_kernel(match_ref, x_ref, weight_ref, bias_ref, select_ref, early_ref, late_ref, part_ref, masks, padded, total):
    step = pl.program_id(0)
    pieces, rows, wide = x_ref.shape
    toks = pieces * rows
    tiles = wide // LANES
    slots, outputs, _ = select_ref.shape

    @pl.when(step == 0)
    def _():
        for tap in range(3):
            masks[tap] = jnp.broadcast_to(match_ref[:, tap : tap + 1], (toks, LANES))
        for tile in range(tiles):
            padded[tile, 0:SUBLANES, :] = jnp.zeros((SUBLANES, LANES), jnp.float32)

    outs = []
    for tile in range(tiles):
        lanes = slice(tile * LANES, (tile + 1) * LANES)
        for piece in range(pieces):
            first = SUBLANES + piece * rows
            padded[tile, first : first + rows, :] = x_ref[piece, :, lanes].astype(jnp.float32)
        half = jnp.broadcast_to(0.5 * bias_ref[0:1, lanes], (toks, LANES))
        for tap in range(4):
            moved = padded[tile, SUBLANES - 3 + tap : SUBLANES - 3 + tap + toks, :]
            term = (0.5 * weight_ref[tap : tap + 1, lanes]) * moved
            half = half + (term * masks[tap] if tap < 3 else term)
        outs.append((half + half * jnp.tanh(half)).astype(jnp.bfloat16))
    conv = jnp.concatenate(outs, axis=1)
    select = jnp.concatenate([select_ref[slot] for slot in range(slots)], axis=1)
    added = lax.dot_general(conv, select, (((1,), (1,)), ((), ())), preferred_element_type=jnp.float32)

    @pl.when(step == 0)
    def _():
        early_ref[...] = conv
        total[...] = added

    @pl.when(step == 1)
    def _():
        late_ref[...] = conv
        spare = part_ref.shape[1] - outputs
        part_ref[:, 0:outputs] = (total[...] + added).astype(part_ref.dtype)
        part_ref[:, outputs:] = jnp.zeros((toks, spare), part_ref.dtype)


def conv_select(match, pieces, conv_weight, conv_bias, select_parts):
    slots, outputs, width = select_parts.shape
    ctx, rows, columns = pieces.shape
    toks = ctx * rows
    padded_outputs = -(-outputs // LANES) * LANES
    wide = columns // 2
    half = pl.BlockSpec((toks, wide), lambda s: (0, 0))
    return pl.pallas_call(
        conv_select_kernel,
        grid=(2,),
        in_specs=[
            pl.BlockSpec(match.shape, lambda s: (0, 0)),
            pl.BlockSpec((ctx, rows, wide), lambda s: (0, 0, s)),
            pl.BlockSpec((4, wide), lambda s: (0, s)),
            pl.BlockSpec((1, wide), lambda s: (0, s)),
            pl.BlockSpec((slots // 2, outputs, width), lambda s: (s, 0, 0)),
        ],
        out_specs=[half, half, pl.BlockSpec((toks, padded_outputs), lambda s: (0, 0))],
        scratch_shapes=[
            pltpu.VMEM((3, toks, LANES), jnp.float32),
            pltpu.VMEM((wide // LANES, SUBLANES + toks, LANES), jnp.float32),
            pltpu.VMEM((toks, outputs), jnp.float32),
        ],
        out_shape=[
            jax.ShapeDtypeStruct((toks, wide), jnp.bfloat16),
            jax.ShapeDtypeStruct((toks, wide), jnp.bfloat16),
            jax.ShapeDtypeStruct((toks, padded_outputs), jnp.bfloat16),
        ],
        compiler_params=pltpu.CompilerParams(vmem_limit_bytes=32 << 20),
        cost_estimate=pl.CostEstimate(
            flops=2 * toks * slots * width * outputs,
            bytes_accessed=2 * pieces.size * 2 + 2 * select_parts.size,
            transcendentals=pieces.size,
        ),
        name="conv_select",
    )(match, pieces, conv_weight, conv_bias, select_parts)


def normalise_kernel(rank, select_ref, out_ref):
    low = select_ref[:, :rank].astype(jnp.float32)
    scale = lax.rsqrt(jnp.mean(low * low, axis=-1, keepdims=True) + 1e-06)
    out_ref[:, :rank] = (low * scale).astype(out_ref.dtype)
    out_ref[:, rank:] = select_ref[:, rank:]


def normalise(select, rank):
    return pl.pallas_call(
        functools.partial(normalise_kernel, rank),
        out_shape=jax.ShapeDtypeStruct(select.shape, jnp.bfloat16),
        compiler_params=pltpu.CompilerParams(vmem_limit_bytes=12 << 20),
        name="normalise",
    )(select)


def scan_kernel(rank, first_shard, reset_hbm, low_hbm, weight_hbm, bias_ref, decay_ref, gain_ref,
                early_hbm, late_hbm, out_ref, reset_ref, low_ref, weight_ref, conv_ref, sems, in_cols, out_diag, delta_rows, drive_rows, held_even, held_odd):
    toks = low_ref.shape[0]
    states = decay_ref.shape[0]
    shards = weight_ref.shape[0]
    width = weight_ref.shape[2]
    tiles = shards * width // LANES
    column = first_shard * width
    low_copy = pltpu.make_async_copy(low_hbm, low_ref, sems.at[0])
    reset_copy = pltpu.make_async_copy(reset_hbm, reset_ref, sems.at[1])
    low_copy.start()
    reset_copy.start()
    shard_copies = []
    for shard in range(shards):
        at = shard * width
        start = column + at
        middle = early_hbm.shape[1]
        source = early_hbm.at[:, pl.ds(start, width)] if start < middle else late_hbm.at[:, pl.ds(start - middle, width)]
        shard_copies += [
            pltpu.make_async_copy(weight_hbm.at[first_shard + shard], weight_ref.at[shard], sems.at[2 + 2 * shard]),
            pltpu.make_async_copy(source, conv_ref.at[:, pl.ds(at, width)], sems.at[3 + 2 * shard]),
        ]
    for copy in shard_copies:
        copy.start()
    low_copy.wait()
    rows = out_ref.shape[1]
    block = 16
    span = block * states
    count = toks // block

    in_cols[...] = jnp.transpose(low_ref[:, rank : rank + LANES].astype(jnp.float32))[0:states, :]
    bits = states.bit_length() - 1
    lane = lax.broadcasted_iota(jnp.int32, (states, span), 1)
    spread = jnp.where((lane & (states - 1)) == lax.broadcasted_iota(jnp.int32, (states, span), 0), 1.0, 0.0)
    spread_out = jnp.dot(
        low_ref[:, rank + states : rank + 2 * states], spread.astype(jnp.bfloat16), preferred_element_type=jnp.float32
    )
    here = lax.shift_right_logical(lax.broadcasted_iota(jnp.int32, (block, span), 1), bits)
    there = lax.broadcasted_iota(jnp.int32, (block, span), 0)
    keep = jnp.where(here == there, 1.0, 0.0)
    out_diag[...] = (spread_out.reshape(count, block, span) * keep[None]).reshape(toks, span).astype(jnp.bfloat16)

    reset_copy.wait()
    reset = jnp.broadcast_to(reset_ref[...], (toks, LANES))
    low = low_ref[:, 0:rank]
    for shard in range(shards):
        shard_copies[2 * shard].wait()
        shard_copies[2 * shard + 1].wait()
        pre = jnp.dot(low, weight_ref[shard], preferred_element_type=jnp.float32)
        for part in range(width // LANES):
            tile = shard * (width // LANES) + part
            lanes = slice(tile * LANES, (tile + 1) * LANES)
            value = pre[:, part * LANES : (part + 1) * LANES]
            value = value + bias_ref[:, column + tile * LANES : column + (tile + 1) * LANES]
            raised = jnp.exp2(jnp.minimum(value, 80.0) * LOG2E)
            small = raised - 0.5 * raised * raised
            delta = jnp.maximum(value, jnp.where(raised < 0.01, small, jnp.log(1.0 + raised)))
            delta_rows[:, tile] = (delta + reset).reshape(count, block, LANES)
            drive_rows[:, tile] = (delta * conv_ref[:, lanes].astype(jnp.float32)).reshape(count, block, LANES)

    rates = [
        -LOG2E * jnp.exp(decay_ref[:, column + tile * LANES : column + (tile + 1) * LANES]) for tile in range(tiles)
    ]

    wide = tiles * LANES
    cut = 2 * LANES
    cuts = -(-wide // cut)

    def finish(index, history, part):
        first = pl.multiple_of(index * block, block)
        lanes = slice(part * cut, min((part + 1) * cut, wide))
        mixed = jnp.dot(out_diag[pl.ds(first, block), :], history[:, lanes], preferred_element_type=jnp.float32)
        gain = gain_ref[:, column + lanes.start : column + lanes.stop]
        full = mixed + gain * conv_ref[pl.ds(first, block), lanes].astype(jnp.float32)
        place = pl.multiple_of(lax.rem(first, rows), block)
        out_ref[lax.div(first, rows), pl.ds(place, block), lanes] = full.astype(out_ref.dtype)

    def advance(index, held, history, before, before_history):
        held = list(held)
        per_row = LANES // block
        columns = in_cols[:, pl.ds(pl.multiple_of(lax.div(index, per_row) * LANES, LANES), LANES)]
        columns = pltpu.roll(columns, lax.rem(LANES - lax.rem(index, per_row) * block, LANES), 1)
        delta_now = delta_rows.at[index]
        drive_now = drive_rows.at[index]
        for inner in range(block):
            into = jnp.broadcast_to(columns[:, inner : inner + 1], (states, LANES))
            for tile in range(tiles):
                lanes = slice(tile * LANES, (tile + 1) * LANES)
                grow = jnp.exp2(delta_now[tile, inner : inner + 1, :] * rates[tile])
                held[tile] = grow * held[tile] + into * drive_now[tile, inner : inner + 1, :]
                history[inner * states : (inner + 1) * states, lanes] = held[tile].astype(jnp.bfloat16)
            if inner % (block // cuts) == 0 and inner // (block // cuts) < cuts:
                finish(before, before_history, inner // (block // cuts))
        return tuple(held)

    held_odd[...] = jnp.zeros_like(held_odd)

    def pair(index, held):
        held = advance(2 * index, held, held_even, jnp.maximum(2 * index - 1, 0), held_odd)
        return advance(2 * index + 1, held, held_odd, 2 * index, held_even)

    start = tuple(jnp.zeros((states, LANES), jnp.float32) for _ in range(tiles))
    lax.fori_loop(0, count // 2, pair, start)
    for part in range(cuts):
        finish(count - 1, held_odd, part)


def state_scan(reset_col, low, delta_parts, bias, decay, gain, convs, ctx, first_shard, shards):
    toks = low.shape[0]
    rank, width = delta_parts.shape[1:]
    states = decay.shape[0]
    rows = toks // ctx
    wide = shards * width
    steps = toks * wide * states
    whole = pl.BlockSpec(memory_space=pltpu.VMEM)
    left = pl.BlockSpec(memory_space=pl.ANY)
    return pl.pallas_call(
        functools.partial(scan_kernel, rank, first_shard),
        in_specs=[left, left, left, whole, whole, whole, left, left],
        out_specs=whole,
        out_shape=jax.ShapeDtypeStruct((ctx, rows, wide), jnp.bfloat16),
        scratch_shapes=[
            pltpu.VMEM(reset_col.shape, reset_col.dtype),
            pltpu.VMEM(low.shape, low.dtype),
            pltpu.VMEM((shards, rank, width), jnp.bfloat16),
            pltpu.VMEM((toks, wide), jnp.bfloat16),
            pltpu.SemaphoreType.DMA((2 + 2 * shards,)),
            pltpu.VMEM((states, toks), jnp.float32),
            pltpu.VMEM((toks, 16 * states), jnp.bfloat16),
            pltpu.VMEM((toks // 16, wide // LANES, 16, LANES), jnp.float32),
            pltpu.VMEM((toks // 16, wide // LANES, 16, LANES), jnp.float32),
            pltpu.VMEM((16 * states, wide), jnp.bfloat16),
            pltpu.VMEM((16 * states, wide), jnp.bfloat16),
        ],
        compiler_params=pltpu.CompilerParams(vmem_limit_bytes=54 << 20),
        cost_estimate=pl.CostEstimate(
            flops=6 * steps, bytes_accessed=2 * shards * rank * width + 4 * toks * wide, transcendentals=steps
        ),
        name=f"state_scan_{first_shard}",
    )(reset_col, low, delta_parts, bias, decay, gain, *convs)


def gate_kernel(fold, width, gate_ref, *refs):
    out_ref = refs[-1]
    slot = 0
    for y_ref in refs[:-1]:
        ctx, _, wide = y_ref.shape
        for place in range(wide // width):
            for piece in range(ctx):
                lanes = piece_lanes(slot, piece, ctx, fold, width)
                value = y_ref[piece, :, place * width : (place + 1) * width].astype(jnp.float32)
                out_ref[:, lanes] = (value * silu(gate_ref[:, lanes].astype(jnp.float32))).astype(out_ref.dtype)
            slot += 1


def apply_gate(parts, gate, fold, width):
    rows, channels = gate.shape
    ctx = parts[0].shape[0]
    part = min(rows, 32)
    columns = pl.BlockSpec((part, channels), lambda r: (r, 0))
    return pl.pallas_call(
        functools.partial(gate_kernel, fold, width),
        grid=(rows // part,),
        in_specs=[columns] + [pl.BlockSpec((ctx, part, array.shape[2]), lambda r: (0, r, 0)) for array in parts],
        out_specs=columns,
        out_shape=jax.ShapeDtypeStruct(gate.shape, jnp.bfloat16),
        compiler_params=pltpu.CompilerParams(vmem_limit_bytes=60 << 20),
        cost_estimate=pl.CostEstimate(flops=4 * gate.size, bytes_accessed=6 * gate.size, transcendentals=gate.size),
        name="gate",
    )(gate, *parts)


def exchange(value):
    return lax.all_to_all(value, "ctx", 0, 0, tiled=True)


def local(
    queries,
    keys,
    values,
    mixer_input,
    gate_input,
    segment_ids,
    conv_weight,
    conv_bias,
    select_weight,
    delta_weight,
    delta_bias,
    decay_log,
    skip_gain,
):
    ctx = lax.axis_size("ctx")
    shards = lax.axis_size("rep")
    place = lax.axis_index("ctx")
    rows, channels = mixer_input.shape[1:]
    rank = delta_weight.shape[0]
    states = decay_log.shape[1]
    width = max(channels // (shards * ctx), LANES)
    fold = width * shards * ctx // channels
    seg = segment_ids[0]
    toks = seg.shape[0]
    back = min(ctx - 1, -(-(toks // 2 - 1) // rows))

    slots = shards // fold

    def own_part(array):
        cut = array.reshape(array.shape[:-1] + (slots, fold, ctx // fold, width))
        cut = lax.dynamic_index_in_dim(cut, place // fold, cut.ndim - 2, keepdims=False)
        cut = lax.dynamic_index_in_dim(cut, place % fold, cut.ndim - 2, keepdims=False)
        return cut.reshape(array.shape[:-1] + (slots * width,))

    def own_columns(weight):
        return lax.dynamic_slice_in_dim(weight, place // fold * width, width, 1)

    def gathered(own):
        parts = lax.all_gather(own, "rep", axis=0)
        if fold > 1:
            parts = parts.reshape((slots, fold) + own.shape)
            parts = lax.dynamic_index_in_dim(parts, place % fold, 1, keepdims=False)
        return parts

    select_parts = gathered(own_columns(select_weight))
    packed = pack(mixer_input[0], ctx, fold, width)

    same = jnp.concatenate([jnp.zeros((1,), bool), seg[1:] == seg[:-1]])
    reset_col = jnp.where(same, 0.0, FAR)[:, None]
    seg_before = jnp.concatenate([jnp.full((3,), -1, jnp.int32), seg])
    match = jnp.stack([(seg_before[tap : tap + toks] == seg) for tap in range(3)], axis=1).astype(jnp.float32)
    seg_pad = jnp.concatenate([jnp.full((back * rows,), -1, jnp.int32), seg])
    seg_k = lax.dynamic_slice_in_dim(seg_pad, place * rows, (back + 1) * rows, 0)
    own = (
        own_part(delta_bias)[None, :],
        own_part(jnp.transpose(decay_log)),
        own_part(skip_gain)[None, :],
        reset_col,
        seg_k[back * rows :, None],
        seg_k[None, :],
        jnp.broadcast_to(jnp.concatenate([keys[0], values[0]], axis=1), (ctx, rows, keys.shape[2] + values.shape[2])),
        own_part(conv_weight),
        own_part(conv_bias)[None, :],
        match,
        own_columns(delta_weight),
    )
    pieces, own = lax.optimization_barrier((exchange(packed), own))
    bias, decay, gain, reset_col, seg_q, seg_k, both, conv_weight, conv_bias, match, delta_own = own
    delta_parts = gathered(delta_own)

    *convs, parts = conv_select(match, pieces, conv_weight, conv_bias, select_parts)
    low = normalise(lax.psum(parts, "ctx"), rank)

    low, both = lax.optimization_barrier((low, both))
    blocks = exchange(both)

    split = slots * 5 // 8
    scanned = [
        state_scan(reset_col, low, delta_parts, bias, decay, gain, convs, ctx, first, count)
        for first, count in ((0, split), (split, slots - split))
    ]
    scanned[0], blocks = lax.optimization_barrier((scanned[0], blocks))
    attended = attention(queries[0], blocks, seg_q, seg_k, jnp.reshape(place, (1,)).astype(jnp.int32), back)
    scanned = [exchange(part) for part in scanned]
    scanned[0], attended = lax.optimization_barrier((scanned[0], attended))
    mixed = apply_gate(scanned, gate_input[0], fold, width)
    return (attended[None], mixed[None])


def solution(mesh):
    placed = (
        P("rep", "ctx", None),
        P("rep", "ctx", None),
        P("rep", "ctx", None),
        P("rep", "ctx", None),
        P("rep", "ctx", None),
        P("rep", None),
        P(),
        P(),
        P(None, "rep"),
        P(None, "rep"),
        P(),
        P(),
        P(),
    )
    return jax.shard_map(
        local,
        mesh=mesh,
        in_specs=placed,
        out_specs=(P("rep", "ctx", None), P("rep", "ctx", None)),
        check_vma=False,
    )
```

```python
import functools
import math

import jax
import jax.numpy as jnp
from jax import lax
from jax.experimental import pallas as pl
from jax.experimental.pallas import tpu as pltpu
from jax.sharding import PartitionSpec as P

QUERY_HEADS = 32
KEY_VALUE_HEADS = 4
HEAD_WIDTH = 128
LANES = 128
SUBLANES = 8
LOG2E = 1.0 / math.log(2.0)
FAR = 1e30


def silu(value):
    half = 0.5 * value
    return half + half * jnp.tanh(half)


def attention_kernel(begin, seg_q_ref, seg_k_ref, q_ref, *refs):
    out_ref = refs[-1]
    refs = refs[: -1 if begin == 0 else -2]
    rows = q_ref.shape[0]
    span = seg_k_ref.shape[1]
    groups = QUERY_HEADS // KEY_VALUE_HEADS
    row = lax.broadcasted_iota(jnp.int32, (rows, span), 0) + (span - rows)
    col = lax.broadcasted_iota(jnp.int32, (rows, span), 1)
    allowed = (col <= row) & (seg_q_ref[...] == seg_k_ref[...])
    shift = jnp.where(allowed, 0.0, -FAR)
    keys = jnp.concatenate([ref[...] for ref in refs[0::2]], axis=0)
    vals = jnp.concatenate([ref[...] for ref in refs[1::2]], axis=0)
    factor = LOG2E / math.sqrt(HEAD_WIDTH)
    batch = 4
    for first in range(0, groups, batch):
        cuts = [slice(head * HEAD_WIDTH, (head + 1) * HEAD_WIDTH) for head in range(first, first + batch)]
        scores = [
            lax.dot_general(q_ref[:, cut], keys, (((1,), (1,)), ((), ())), preferred_element_type=jnp.float32)
            for cut in cuts
        ]
        scores = [score + shift for score in scores]
        tops = [jnp.max(score, axis=-1, keepdims=True) for score in scores]
        weights = [jnp.exp2((score - top) * factor) for score, top in zip(scores, tops)]
        norms = [jnp.sum(weight, axis=-1, keepdims=True) for weight in weights]
        totals = [jnp.dot(weight.astype(jnp.bfloat16), vals, preferred_element_type=jnp.float32) for weight in weights]
        for cut, total, norm in zip(cuts, totals, norms):
            out_ref[:, cut] = (total / norm).astype(out_ref.dtype)


def attention(queries, blocks, seg_q, seg_k, begin, end, before=None):
    rows = queries.shape[0]
    span = seg_k.shape[1]
    group_width = QUERY_HEADS // KEY_VALUE_HEADS * HEAD_WIDTH
    key_spec = pl.BlockSpec((rows, HEAD_WIDTH), lambda h: (0, begin + h))
    value_spec = pl.BlockSpec((rows, HEAD_WIDTH), lambda h: (0, KEY_VALUE_HEADS + begin + h))
    wide = pl.BlockSpec((rows, group_width), lambda h: (0, begin + h))
    operands = [seg_q, seg_k, queries] + [block for block in blocks for _ in range(2)]
    in_specs = [
        pl.BlockSpec((rows, 1), lambda h: (0, 0)),
        pl.BlockSpec((1, span), lambda h: (0, 0)),
        wide,
        *([key_spec, value_spec] * len(blocks)),
    ]
    aliases = {}
    if before is not None:
        aliases = {len(operands): 0}
        operands.append(before)
        in_specs.append(pl.BlockSpec(memory_space=pl.ANY))
    return pl.pallas_call(
        functools.partial(attention_kernel, begin),
        grid=(end - begin,),
        in_specs=in_specs,
        out_specs=wide,
        out_shape=jax.ShapeDtypeStruct(queries.shape, jnp.bfloat16),
        input_output_aliases=aliases,
        compiler_params=pltpu.CompilerParams(vmem_limit_bytes=54 << 20),
        cost_estimate=pl.CostEstimate(
            flops=4 * rows * span * group_width * (end - begin),
            bytes_accessed=4 * rows * group_width * (end - begin),
            transcendentals=rows * span * group_width // HEAD_WIDTH * (end - begin),
        ),
        name=f"attention_{begin}",
    )(*operands)


def piece_lanes(slot, piece, ctx, fold, width):
    start = (slot * ctx + piece % fold * (ctx // fold) + piece // fold) * width
    return slice(start, start + width)


def cut_kernel(fold, width, start_ref, x_hbm, weight_hbm, out_hbm, own_hbm, sems):
    ctx, _, columns = out_hbm.shape
    start = pl.multiple_of(start_ref[0], LANES)
    copies = [pltpu.make_async_copy(weight_hbm.at[:, pl.ds(start, width)], own_hbm, sems.at[0])]
    for slot in range(columns // width):
        for piece in range(ctx):
            source = x_hbm.at[:, piece_lanes(slot, piece, ctx, fold, width)]
            target = out_hbm.at[piece, :, slot * width : (slot + 1) * width]
            copies.append(pltpu.make_async_copy(source, target, sems.at[len(copies)]))
    for copy in copies:
        copy.start()
    for copy in copies:
        copy.wait()


def cut(start, value, weight, ctx, fold, width):
    rows, channels = value.shape
    left = pl.BlockSpec(memory_space=pl.ANY)
    return pl.pallas_call(
        functools.partial(cut_kernel, fold, width),
        grid_spec=pltpu.PrefetchScalarGridSpec(
            num_scalar_prefetch=1,
            grid=(1,),
            in_specs=[left, left],
            out_specs=[left, left],
            scratch_shapes=[pltpu.SemaphoreType.DMA((1 + channels // width,))],
        ),
        out_shape=[
            jax.ShapeDtypeStruct((ctx, rows, channels // ctx), value.dtype),
            jax.ShapeDtypeStruct((weight.shape[0], width), weight.dtype),
        ],
        compiler_params=pltpu.CompilerParams(vmem_limit_bytes=60 << 20),
        name="cut",
    )(start, value, weight)


def conv_kernel(match_ref, x_ref, weight_ref, bias_ref, conv_ref, masks, padded):
    pieces, rows, wide = x_ref.shape
    toks = pieces * rows
    tiles = wide // LANES

    @pl.when(pl.program_id(0) == 0)
    def _():
        for tap in range(3):
            masks[tap] = jnp.broadcast_to(match_ref[:, tap : tap + 1], (toks, LANES))
        for tile in range(tiles):
            padded[tile, 0:SUBLANES, :] = jnp.zeros((SUBLANES, LANES), jnp.float32)

    for tile in range(tiles):
        lanes = slice(tile * LANES, (tile + 1) * LANES)
        for piece in range(pieces):
            first = SUBLANES + piece * rows
            padded[tile, first : first + rows, :] = x_ref[piece, :, lanes].astype(jnp.float32)
        half = jnp.broadcast_to(0.5 * bias_ref[0:1, lanes], (toks, LANES))
        for tap in range(4):
            moved = padded[tile, SUBLANES - 3 + tap : SUBLANES - 3 + tap + toks, :]
            term = (0.5 * weight_ref[tap : tap + 1, lanes]) * moved
            half = half + (term * masks[tap] if tap < 3 else term)
        conv_ref[0, :, lanes] = (half + half * jnp.tanh(half)).astype(jnp.bfloat16)


def convolve(match, pieces, conv_weight, conv_bias):
    ctx, rows, columns = pieces.shape
    toks = ctx * rows
    wide = columns // 2
    return pl.pallas_call(
        conv_kernel,
        grid=(2,),
        in_specs=[
            pl.BlockSpec(match.shape, lambda s: (0, 0)),
            pl.BlockSpec((ctx, rows, wide), lambda s: (0, 0, s)),
            pl.BlockSpec((4, wide), lambda s: (0, s)),
            pl.BlockSpec((1, wide), lambda s: (0, s)),
        ],
        out_specs=pl.BlockSpec((1, toks, wide), lambda s: (s, 0, 0)),
        scratch_shapes=[
            pltpu.VMEM((3, toks, LANES), jnp.float32),
            pltpu.VMEM((wide // LANES, SUBLANES + toks, LANES), jnp.float32),
        ],
        out_shape=jax.ShapeDtypeStruct((2, toks, wide), jnp.bfloat16),
        compiler_params=pltpu.CompilerParams(vmem_limit_bytes=28 << 20),
        cost_estimate=pl.CostEstimate(
            flops=16 * pieces.size, bytes_accessed=4 * pieces.size, transcendentals=pieces.size
        ),
        name="convolve",
    )(match, pieces, conv_weight, conv_bias)


def select_kernel(conv_ref, select_ref, part_ref, total):
    step = pl.program_id(0)
    pieces, rows, _ = part_ref.shape
    slots, outputs, _ = select_ref.shape
    select = jnp.concatenate([select_ref[slot] for slot in range(slots)], axis=1)
    added = lax.dot_general(conv_ref[0], select, (((1,), (1,)), ((), ())), preferred_element_type=jnp.float32)

    @pl.when(step == 0)
    def _():
        total[...] = added

    @pl.when(step == 1)
    def _():
        spare = part_ref.shape[2] - outputs
        full = (total[...] + added).astype(part_ref.dtype)
        for piece in range(pieces):
            part_ref[piece, :, 0:outputs] = full[piece * rows : (piece + 1) * rows, :]
            part_ref[piece, :, outputs:] = jnp.zeros((rows, spare), part_ref.dtype)


def select_part(conv, select_parts, ctx):
    slots, outputs, width = select_parts.shape
    _, toks, wide = conv.shape
    shape = (ctx, toks // ctx, -(-outputs // LANES) * LANES)
    return pl.pallas_call(
        select_kernel,
        grid=(2,),
        in_specs=[
            pl.BlockSpec((1, toks, wide), lambda s: (s, 0, 0)),
            pl.BlockSpec((slots // 2, outputs, width), lambda s: (s, 0, 0)),
        ],
        out_specs=pl.BlockSpec(shape, lambda s: (0, 0, 0)),
        scratch_shapes=[pltpu.VMEM((toks, outputs), jnp.float32)],
        out_shape=jax.ShapeDtypeStruct(shape, jnp.bfloat16),
        compiler_params=pltpu.CompilerParams(vmem_limit_bytes=28 << 20),
        cost_estimate=pl.CostEstimate(
            flops=2 * conv.size * outputs, bytes_accessed=2 * conv.size + 2 * select_parts.size, transcendentals=0
        ),
        name="select",
    )(conv, select_parts)


def normalise_kernel(rank, part_ref, out_ref):
    pieces = part_ref.shape[0]
    total = part_ref[0].astype(jnp.float32)
    for piece in range(1, pieces):
        total = total + part_ref[piece].astype(jnp.float32)
    low = total[:, :rank]
    scale = lax.rsqrt(jnp.mean(low * low, axis=-1, keepdims=True) + 1e-06)
    low = (low * scale).astype(out_ref.dtype)
    maps = total[:, rank:].astype(out_ref.dtype)
    for piece in range(pieces):
        out_ref[piece, :, :rank] = low
        out_ref[piece, :, rank:] = maps


def normalise(parts, rank):
    return pl.pallas_call(
        functools.partial(normalise_kernel, rank),
        out_shape=jax.ShapeDtypeStruct(parts.shape, jnp.bfloat16),
        compiler_params=pltpu.CompilerParams(vmem_limit_bytes=12 << 20),
        name="normalise",
    )(parts)


def scan_kernel(rank, first_shard, reset_hbm, low_ref, weight_hbm, bias_ref, decay_ref, gain_ref,
                conv_hbm, out_ref, reset_ref, weight_ref, conv_ref, sems, in_cols, out_diag, delta_rows, drive_rows, held_even, held_odd):
    toks = low_ref.shape[0]
    states = decay_ref.shape[0]
    shards = weight_ref.shape[0]
    width = weight_ref.shape[2]
    tiles = shards * width // LANES
    column = first_shard * width
    reset_copy = pltpu.make_async_copy(reset_hbm, reset_ref, sems.at[0])
    reset_copy.start()
    shard_copies = []
    for shard in range(shards):
        at = shard * width
        start = column + at
        middle = conv_hbm.shape[2]
        source = conv_hbm.at[start // middle, :, pl.ds(start % middle, width)]
        shard_copies += [
            pltpu.make_async_copy(weight_hbm.at[first_shard + shard], weight_ref.at[shard], sems.at[1 + 2 * shard]),
            pltpu.make_async_copy(source, conv_ref.at[:, pl.ds(at, width)], sems.at[2 + 2 * shard]),
        ]
    for copy in shard_copies:
        copy.start()
    rows = out_ref.shape[1]
    block = 16
    span = block * states
    count = toks // block

    in_cols[...] = jnp.transpose(low_ref[:, rank : rank + LANES].astype(jnp.float32))[0:states, :]
    bits = states.bit_length() - 1
    lane = lax.broadcasted_iota(jnp.int32, (states, span), 1)
    spread = jnp.where((lane & (states - 1)) == lax.broadcasted_iota(jnp.int32, (states, span), 0), 1.0, 0.0)
    spread_out = jnp.dot(
        low_ref[:, rank + states : rank + 2 * states], spread.astype(jnp.bfloat16), preferred_element_type=jnp.float32
    )
    here = lax.shift_right_logical(lax.broadcasted_iota(jnp.int32, (block, span), 1), bits)
    there = lax.broadcasted_iota(jnp.int32, (block, span), 0)
    keep = jnp.where(here == there, 1.0, 0.0)
    out_diag[...] = (spread_out.reshape(count, block, span) * keep[None]).reshape(toks, span).astype(jnp.bfloat16)

    reset_copy.wait()
    reset = jnp.broadcast_to(reset_ref[...], (toks, LANES))
    low = low_ref[:, 0:rank]
    for shard in range(shards):
        shard_copies[2 * shard].wait()
        shard_copies[2 * shard + 1].wait()
        pre = jnp.dot(low, weight_ref[shard], preferred_element_type=jnp.float32)
        for part in range(width // LANES):
            tile = shard * (width // LANES) + part
            lanes = slice(tile * LANES, (tile + 1) * LANES)
            value = pre[:, part * LANES : (part + 1) * LANES]
            value = value + bias_ref[:, column + tile * LANES : column + (tile + 1) * LANES]
            raised = jnp.exp2(jnp.minimum(value, 80.0) * LOG2E)
            small = raised - 0.5 * raised * raised
            delta = jnp.maximum(value, jnp.where(raised < 0.01, small, jnp.log(1.0 + raised)))
            delta_rows[:, tile] = (delta + reset).reshape(count, block, LANES)
            drive_rows[:, tile] = (delta * conv_ref[:, lanes].astype(jnp.float32)).reshape(count, block, LANES)

    rates = [
        -LOG2E * jnp.exp(decay_ref[:, column + tile * LANES : column + (tile + 1) * LANES]) for tile in range(tiles)
    ]

    wide = tiles * LANES
    cut = 2 * LANES
    cuts = -(-wide // cut)

    def finish(index, history, part):
        first = pl.multiple_of(index * block, block)
        lanes = slice(part * cut, min((part + 1) * cut, wide))
        mixed = jnp.dot(out_diag[pl.ds(first, block), :], history[:, lanes], preferred_element_type=jnp.float32)
        gain = gain_ref[:, column + lanes.start : column + lanes.stop]
        full = mixed + gain * conv_ref[pl.ds(first, block), lanes].astype(jnp.float32)
        place = pl.multiple_of(lax.rem(first, rows), block)
        out_ref[lax.div(first, rows), pl.ds(place, block), lanes] = full.astype(out_ref.dtype)

    def advance(index, held, history, before, before_history):
        held = list(held)
        per_row = LANES // block
        columns = in_cols[:, pl.ds(pl.multiple_of(lax.div(index, per_row) * LANES, LANES), LANES)]
        columns = pltpu.roll(columns, lax.rem(LANES - lax.rem(index, per_row) * block, LANES), 1)
        delta_now = delta_rows.at[index]
        drive_now = drive_rows.at[index]
        for inner in range(block):
            into = jnp.broadcast_to(columns[:, inner : inner + 1], (states, LANES))
            for tile in range(tiles):
                lanes = slice(tile * LANES, (tile + 1) * LANES)
                grow = jnp.exp2(delta_now[tile, inner : inner + 1, :] * rates[tile])
                held[tile] = grow * held[tile] + into * drive_now[tile, inner : inner + 1, :]
                history[inner * states : (inner + 1) * states, lanes] = held[tile].astype(jnp.bfloat16)
            if inner % (block // cuts) == 0 and inner // (block // cuts) < cuts:
                finish(before, before_history, inner // (block // cuts))
        return tuple(held)

    held_odd[...] = jnp.zeros_like(held_odd)

    def pair(index, held):
        held = advance(2 * index, held, held_even, jnp.maximum(2 * index - 1, 0), held_odd)
        return advance(2 * index + 1, held, held_odd, 2 * index, held_even)

    start = tuple(jnp.zeros((states, LANES), jnp.float32) for _ in range(tiles))
    lax.fori_loop(0, count // 2, pair, start)
    for part in range(cuts):
        finish(count - 1, held_odd, part)


def state_scan(reset_col, low, delta_parts, bias, decay, gain, conv, ctx, first_shard, shards):
    toks = low.shape[0]
    rank, width = delta_parts.shape[1:]
    states = decay.shape[0]
    rows = toks // ctx
    wide = shards * width
    steps = toks * wide * states
    whole = pl.BlockSpec(memory_space=pltpu.VMEM)
    left = pl.BlockSpec(memory_space=pl.ANY)
    return pl.pallas_call(
        functools.partial(scan_kernel, rank, first_shard),
        in_specs=[left, whole, left, whole, whole, whole, left],
        out_specs=whole,
        out_shape=jax.ShapeDtypeStruct((ctx, rows, wide), jnp.bfloat16),
        scratch_shapes=[
            pltpu.VMEM(reset_col.shape, reset_col.dtype),
            pltpu.VMEM((shards, rank, width), jnp.bfloat16),
            pltpu.VMEM((toks, wide), jnp.bfloat16),
            pltpu.SemaphoreType.DMA((1 + 2 * shards,)),
            pltpu.VMEM((states, toks), jnp.float32),
            pltpu.VMEM((toks, 16 * states), jnp.bfloat16),
            pltpu.VMEM((toks // 16, wide // LANES, 16, LANES), jnp.float32),
            pltpu.VMEM((toks // 16, wide // LANES, 16, LANES), jnp.float32),
            pltpu.VMEM((16 * states, wide), jnp.bfloat16),
            pltpu.VMEM((16 * states, wide), jnp.bfloat16),
        ],
        compiler_params=pltpu.CompilerParams(vmem_limit_bytes=54 << 20),
        cost_estimate=pl.CostEstimate(
            flops=6 * steps, bytes_accessed=2 * shards * rank * width + 4 * toks * wide, transcendentals=steps
        ),
        name=f"state_scan_{first_shard}",
    )(reset_col, low, delta_parts, bias, decay, gain, conv)


def gate_kernel(fold, width, gate_ref, *refs):
    out_ref = refs[-1]
    slot = 0
    for y_ref in refs[:-1]:
        ctx, _, wide = y_ref.shape
        for place in range(wide // width):
            for piece in range(ctx):
                lanes = piece_lanes(slot, piece, ctx, fold, width)
                value = y_ref[piece, :, place * width : (place + 1) * width].astype(jnp.float32)
                out_ref[:, lanes] = (value * silu(gate_ref[:, lanes].astype(jnp.float32))).astype(out_ref.dtype)
            slot += 1


def apply_gate(parts, gate, fold, width):
    rows, channels = gate.shape
    ctx = parts[0].shape[0]
    part = min(rows, 32)
    columns = pl.BlockSpec((part, channels), lambda r: (r, 0))
    return pl.pallas_call(
        functools.partial(gate_kernel, fold, width),
        grid=(rows // part,),
        in_specs=[columns] + [pl.BlockSpec((ctx, part, array.shape[2]), lambda r: (0, r, 0)) for array in parts],
        out_specs=columns,
        out_shape=jax.ShapeDtypeStruct(gate.shape, jnp.bfloat16),
        compiler_params=pltpu.CompilerParams(vmem_limit_bytes=16 << 20),
        cost_estimate=pl.CostEstimate(flops=4 * gate.size, bytes_accessed=6 * gate.size, transcendentals=gate.size),
        name="gate",
    )(gate, *parts)


def shifted(value, axis, by):
    size = lax.axis_size(axis)
    pairs = [(i, i + by) for i in range(size) if 0 <= i + by < size]
    return lax.ppermute(value, axis, pairs)


def exchange(value):
    return lax.all_to_all(value, "ctx", 0, 0, tiled=True)


def local(
    queries,
    keys,
    values,
    mixer_input,
    gate_input,
    segment_ids,
    conv_weight,
    conv_bias,
    select_weight,
    delta_weight,
    delta_bias,
    decay_log,
    skip_gain,
):
    ctx = lax.axis_size("ctx")
    shards = lax.axis_size("rep")
    place = lax.axis_index("ctx")
    rows, channels = mixer_input.shape[1:]
    rank = delta_weight.shape[0]
    states = decay_log.shape[1]
    width = max(channels // (shards * ctx), LANES)
    fold = width * shards * ctx // channels
    seg = segment_ids[0]
    toks = seg.shape[0]
    back = min(ctx - 1, -(-(toks // 2 - 1) // rows))

    slots = shards // fold

    def own_part(array):
        cut = array.reshape(array.shape[:-1] + (slots, fold, ctx // fold, width))
        cut = lax.dynamic_index_in_dim(cut, place // fold, cut.ndim - 2, keepdims=False)
        cut = lax.dynamic_index_in_dim(cut, place % fold, cut.ndim - 2, keepdims=False)
        return cut.reshape(array.shape[:-1] + (slots * width,))

    def own_columns(weight):
        return lax.dynamic_slice_in_dim(weight, place // fold * width, width, 1)

    def gathered(own):
        parts = lax.all_gather(own, "rep", axis=0)
        if fold > 1:
            parts = parts.reshape((slots, fold) + own.shape)
            parts = lax.dynamic_index_in_dim(parts, place % fold, 1, keepdims=False)
        return parts

    start = jnp.reshape(place // fold * width, (1,)).astype(jnp.int32)
    packed, select_own = cut(start, mixer_input[0], select_weight, ctx, fold, width)
    select_parts = gathered(select_own)

    same = jnp.concatenate([jnp.zeros((1,), bool), seg[1:] == seg[:-1]])
    reset_col = jnp.where(same, 0.0, FAR)[:, None]
    seg_before = jnp.concatenate([jnp.full((3,), -1, jnp.int32), seg])
    match = jnp.stack([(seg_before[tap : tap + toks] == seg) for tap in range(3)], axis=1).astype(jnp.float32)
    seg_pad = jnp.concatenate([jnp.full((back * rows,), -1, jnp.int32), seg])
    seg_k = lax.dynamic_slice_in_dim(seg_pad, place * rows, (back + 1) * rows, 0)
    own = (
        own_part(delta_bias)[None, :],
        own_part(jnp.transpose(decay_log)),
        own_part(skip_gain)[None, :],
        reset_col,
        seg_k[back * rows :, None],
        seg_k[None, :],
        jnp.concatenate([keys[0], values[0]], axis=1),
        own_part(conv_weight),
        own_part(conv_bias)[None, :],
        match,
        own_columns(delta_weight),
    )
    pieces, own = lax.optimization_barrier((exchange(packed), own))
    bias, decay, gain, reset_col, seg_q, seg_k, both, conv_weight, conv_bias, match, delta_own = own
    delta_parts = gathered(delta_own)

    conv = convolve(match, pieces, conv_weight, conv_bias)
    parts = select_part(conv, select_parts, ctx)
    low = normalise(exchange(parts), rank)

    low, both = lax.optimization_barrier((low, both))
    blocks = [shifted(both, "ctx", by) for by in range(back, 0, -1)] + [both]
    low = exchange(low).reshape(toks, low.shape[2])

    split = slots * 5 // 8
    scanned = [
        state_scan(reset_col, low, delta_parts, bias, decay, gain, conv, ctx, first, count)
        for first, count in ((0, split), (split, slots - split))
    ]
    scanned[0], blocks = lax.optimization_barrier((scanned[0], blocks))
    attended = attention(queries[0], blocks, seg_q, seg_k, 0, KEY_VALUE_HEADS)
    scanned = [exchange(part) for part in scanned]
    scanned[0], attended = lax.optimization_barrier((scanned[0], attended))
    mixed = apply_gate(scanned, gate_input[0], fold, width)
    return (attended[None], mixed[None])


def solution(mesh):
    placed = (
        P("rep", "ctx", None),
        P("rep", "ctx", None),
        P("rep", "ctx", None),
        P("rep", "ctx", None),
        P("rep", "ctx", None),
        P("rep", None),
        P(),
        P(),
        P(None, "rep"),
        P(None, "rep"),
        P(),
        P(),
        P(),
    )
    return jax.shard_map(
        local,
        mesh=mesh,
        in_specs=placed,
        out_specs=(P("rep", "ctx", None), P("rep", "ctx", None)),
        check_vma=False,
    )
```

```python
import functools
import math

import jax
import jax.numpy as jnp
from jax import lax
from jax.experimental import pallas as pl
from jax.experimental.pallas import tpu as pltpu
from jax.sharding import PartitionSpec as P

QUERY_HEADS = 32
KEY_VALUE_HEADS = 4
HEAD_WIDTH = 128
LANES = 128
SUBLANES = 8
LOG2E = 1.0 / math.log(2.0)
FAR = 1e30


def silu(value):
    half = 0.5 * value
    return half + half * jnp.tanh(half)


def attention_kernel(begin, seg_q_ref, seg_k_ref, q_ref, *refs):
    out_ref = refs[-1]
    refs = refs[: -1 if begin == 0 else -2]
    rows = q_ref.shape[0]
    span = seg_k_ref.shape[1]
    groups = QUERY_HEADS // KEY_VALUE_HEADS
    row = lax.broadcasted_iota(jnp.int32, (rows, span), 0) + (span - rows)
    col = lax.broadcasted_iota(jnp.int32, (rows, span), 1)
    allowed = (col <= row) & (seg_q_ref[...] == seg_k_ref[...])
    shift = jnp.where(allowed, 0.0, -FAR)
    keys = jnp.concatenate([ref[...] for ref in refs[0::2]], axis=0)
    vals = jnp.concatenate([ref[...] for ref in refs[1::2]], axis=0)
    factor = LOG2E / math.sqrt(HEAD_WIDTH)
    batch = 4
    for first in range(0, groups, batch):
        cuts = [slice(head * HEAD_WIDTH, (head + 1) * HEAD_WIDTH) for head in range(first, first + batch)]
        scores = [
            lax.dot_general(q_ref[:, cut], keys, (((1,), (1,)), ((), ())), preferred_element_type=jnp.float32)
            for cut in cuts
        ]
        scores = [score + shift for score in scores]
        tops = [jnp.max(score, axis=-1, keepdims=True) for score in scores]
        weights = [jnp.exp2((score - top) * factor) for score, top in zip(scores, tops)]
        norms = [jnp.sum(weight, axis=-1, keepdims=True) for weight in weights]
        totals = [jnp.dot(weight.astype(jnp.bfloat16), vals, preferred_element_type=jnp.float32) for weight in weights]
        for cut, total, norm in zip(cuts, totals, norms):
            out_ref[:, cut] = (total / norm).astype(out_ref.dtype)


def attention(queries, blocks, seg_q, seg_k, begin, end, before=None):
    rows = queries.shape[0]
    span = seg_k.shape[1]
    group_width = QUERY_HEADS // KEY_VALUE_HEADS * HEAD_WIDTH
    key_spec = pl.BlockSpec((rows, HEAD_WIDTH), lambda h: (0, begin + h))
    value_spec = pl.BlockSpec((rows, HEAD_WIDTH), lambda h: (0, KEY_VALUE_HEADS + begin + h))
    wide = pl.BlockSpec((rows, group_width), lambda h: (0, begin + h))
    operands = [seg_q, seg_k, queries] + [block for block in blocks for _ in range(2)]
    in_specs = [
        pl.BlockSpec((rows, 1), lambda h: (0, 0)),
        pl.BlockSpec((1, span), lambda h: (0, 0)),
        wide,
        *([key_spec, value_spec] * len(blocks)),
    ]
    aliases = {}
    if before is not None:
        aliases = {len(operands): 0}
        operands.append(before)
        in_specs.append(pl.BlockSpec(memory_space=pl.ANY))
    return pl.pallas_call(
        functools.partial(attention_kernel, begin),
        grid=(end - begin,),
        in_specs=in_specs,
        out_specs=wide,
        out_shape=jax.ShapeDtypeStruct(queries.shape, jnp.bfloat16),
        input_output_aliases=aliases,
        compiler_params=pltpu.CompilerParams(vmem_limit_bytes=54 << 20),
        cost_estimate=pl.CostEstimate(
            flops=4 * rows * span * group_width * (end - begin),
            bytes_accessed=4 * rows * group_width * (end - begin),
            transcendentals=rows * span * group_width // HEAD_WIDTH * (end - begin),
        ),
        name=f"attention_{begin}",
    )(*operands)


def piece_lanes(slot, piece, ctx, fold, width):
    start = (slot * ctx + piece % fold * (ctx // fold) + piece // fold) * width
    return slice(start, start + width)


def pack_kernel(fold, width, x_ref, out_ref):
    ctx = out_ref.shape[0]
    for piece in range(ctx):
        for slot in range(out_ref.shape[2] // width):
            out_ref[piece, :, slot * width : (slot + 1) * width] = x_ref[:, piece_lanes(slot, piece, ctx, fold, width)]


def pack(value, ctx, fold, width):
    rows, channels = value.shape
    part = min(rows, 32)
    return pl.pallas_call(
        functools.partial(pack_kernel, fold, width),
        grid=(rows // part,),
        in_specs=[pl.BlockSpec((part, channels), lambda r: (r, 0))],
        out_specs=pl.BlockSpec((ctx, part, channels // ctx), lambda r: (0, r, 0)),
        out_shape=jax.ShapeDtypeStruct((ctx, rows, channels // ctx), value.dtype),
        compiler_params=pltpu.CompilerParams(vmem_limit_bytes=12 << 20),
        name="pack",
    )(value)


def conv_select_kernel(match_ref, x_ref, weight_ref, bias_ref, select_hbm, early_ref, late_ref, part_ref,
                       masks, padded, total, select_ref, sems):
    step = pl.program_id(0)
    pieces, rows, wide = x_ref.shape
    toks = pieces * rows
    tiles = wide // LANES
    _, slots, outputs, _ = select_ref.shape
    copies = [
        pltpu.make_async_copy(select_hbm.at[pl.ds(half * slots, slots)], select_ref.at[half], sems.at[half])
        for half in range(2)
    ]

    @pl.when(step == 0)
    def _():
        for copy in copies:
            copy.start()
        for tap in range(3):
            masks[tap] = jnp.broadcast_to(match_ref[:, tap : tap + 1], (toks, LANES))
        for tile in range(tiles):
            padded[tile, 0:SUBLANES, :] = jnp.zeros((SUBLANES, LANES), jnp.float32)

    outs = []
    for tile in range(tiles):
        lanes = slice(tile * LANES, (tile + 1) * LANES)
        for piece in range(pieces):
            first = SUBLANES + piece * rows
            padded[tile, first : first + rows, :] = x_ref[piece, :, lanes].astype(jnp.float32)
        half = jnp.broadcast_to(0.5 * bias_ref[0:1, lanes], (toks, LANES))
        for tap in range(4):
            moved = padded[tile, SUBLANES - 3 + tap : SUBLANES - 3 + tap + toks, :]
            term = (0.5 * weight_ref[tap : tap + 1, lanes]) * moved
            half = half + (term * masks[tap] if tap < 3 else term)
        outs.append((half + half * jnp.tanh(half)).astype(jnp.bfloat16))
    conv = jnp.concatenate(outs, axis=1)

    def product(half):
        copies[half].wait()
        select = jnp.concatenate([select_ref[half, slot] for slot in range(slots)], axis=1)
        return lax.dot_general(conv, select, (((1,), (1,)), ((), ())), preferred_element_type=jnp.float32)

    @pl.when(step == 0)
    def _():
        early_ref[...] = conv
        total[...] = product(0)

    @pl.when(step == 1)
    def _():
        late_ref[...] = conv
        added = product(1)
        spare = part_ref.shape[2] - outputs
        full = (total[...] + added).astype(part_ref.dtype)
        for piece in range(pieces):
            part_ref[piece, :, 0:outputs] = full[piece * rows : (piece + 1) * rows, :]
            part_ref[piece, :, outputs:] = jnp.zeros((rows, spare), part_ref.dtype)


def conv_select(match, pieces, conv_weight, conv_bias, select_parts):
    slots, outputs, width = select_parts.shape
    ctx, rows, columns = pieces.shape
    toks = ctx * rows
    padded_outputs = -(-outputs // LANES) * LANES
    wide = columns // 2
    half = pl.BlockSpec((toks, wide), lambda s: (0, 0))
    return pl.pallas_call(
        conv_select_kernel,
        grid=(2,),
        in_specs=[
            pl.BlockSpec(match.shape, lambda s: (0, 0)),
            pl.BlockSpec((ctx, rows, wide), lambda s: (0, 0, s)),
            pl.BlockSpec((4, wide), lambda s: (0, s)),
            pl.BlockSpec((1, wide), lambda s: (0, s)),
            pl.BlockSpec(memory_space=pl.ANY),
        ],
        out_specs=[half, half, pl.BlockSpec((ctx, rows, padded_outputs), lambda s: (0, 0, 0))],
        scratch_shapes=[
            pltpu.VMEM((3, toks, LANES), jnp.float32),
            pltpu.VMEM((wide // LANES, SUBLANES + toks, LANES), jnp.float32),
            pltpu.VMEM((toks, outputs), jnp.float32),
            pltpu.VMEM((2, slots // 2, outputs, width), jnp.bfloat16),
            pltpu.SemaphoreType.DMA((2,)),
        ],
        out_shape=[
            jax.ShapeDtypeStruct((toks, wide), jnp.bfloat16),
            jax.ShapeDtypeStruct((toks, wide), jnp.bfloat16),
            jax.ShapeDtypeStruct((ctx, rows, padded_outputs), jnp.bfloat16),
        ],
        compiler_params=pltpu.CompilerParams(vmem_limit_bytes=54 << 20),
        cost_estimate=pl.CostEstimate(
            flops=2 * toks * slots * width * outputs,
            bytes_accessed=2 * pieces.size * 2 + 2 * select_parts.size,
            transcendentals=pieces.size,
        ),
        name="conv_select",
    )(match, pieces, conv_weight, conv_bias, select_parts)


def normalise_kernel(rank, part_ref, out_ref):
    pieces = part_ref.shape[0]
    total = part_ref[0].astype(jnp.float32)
    for piece in range(1, pieces):
        total = total + part_ref[piece].astype(jnp.float32)
    low = total[:, :rank]
    scale = lax.rsqrt(jnp.mean(low * low, axis=-1, keepdims=True) + 1e-06)
    low = (low * scale).astype(out_ref.dtype)
    maps = total[:, rank:].astype(out_ref.dtype)
    for piece in range(pieces):
        out_ref[piece, :, :rank] = low
        out_ref[piece, :, rank:] = maps


def normalise(parts, rank):
    return pl.pallas_call(
        functools.partial(normalise_kernel, rank),
        out_shape=jax.ShapeDtypeStruct(parts.shape, jnp.bfloat16),
        compiler_params=pltpu.CompilerParams(vmem_limit_bytes=12 << 20),
        name="normalise",
    )(parts)


def scan_kernel(rank, first_shard, reset_hbm, low_hbm, weight_hbm, bias_ref, decay_ref, gain_ref,
                early_hbm, late_hbm, out_ref, reset_ref, low_ref, weight_ref, conv_ref, sems, in_cols, out_diag, delta_rows, drive_rows, held_even, held_odd):
    toks = low_ref.shape[0]
    states = decay_ref.shape[0]
    shards = weight_ref.shape[0]
    width = weight_ref.shape[2]
    tiles = shards * width // LANES
    column = first_shard * width
    low_copy = pltpu.make_async_copy(low_hbm, low_ref, sems.at[0])
    reset_copy = pltpu.make_async_copy(reset_hbm, reset_ref, sems.at[1])
    low_copy.start()
    reset_copy.start()
    shard_copies = []
    for shard in range(shards):
        at = shard * width
        start = column + at
        middle = early_hbm.shape[1]
        source = early_hbm.at[:, pl.ds(start, width)] if start < middle else late_hbm.at[:, pl.ds(start - middle, width)]
        shard_copies += [
            pltpu.make_async_copy(weight_hbm.at[first_shard + shard], weight_ref.at[shard], sems.at[2 + 2 * shard]),
            pltpu.make_async_copy(source, conv_ref.at[:, pl.ds(at, width)], sems.at[3 + 2 * shard]),
        ]
    for copy in shard_copies:
        copy.start()
    low_copy.wait()
    rows = out_ref.shape[1]
    block = 16
    span = block * states
    count = toks // block

    in_cols[...] = jnp.transpose(low_ref[:, rank : rank + LANES].astype(jnp.float32))[0:states, :]
    bits = states.bit_length() - 1
    lane = lax.broadcasted_iota(jnp.int32, (states, span), 1)
    spread = jnp.where((lane & (states - 1)) == lax.broadcasted_iota(jnp.int32, (states, span), 0), 1.0, 0.0)
    spread_out = jnp.dot(
        low_ref[:, rank + states : rank + 2 * states], spread.astype(jnp.bfloat16), preferred_element_type=jnp.float32
    )
    here = lax.shift_right_logical(lax.broadcasted_iota(jnp.int32, (block, span), 1), bits)
    there = lax.broadcasted_iota(jnp.int32, (block, span), 0)
    keep = jnp.where(here == there, 1.0, 0.0)
    out_diag[...] = (spread_out.reshape(count, block, span) * keep[None]).reshape(toks, span).astype(jnp.bfloat16)

    reset_copy.wait()
    reset = jnp.broadcast_to(reset_ref[...], (toks, LANES))
    low = low_ref[:, 0:rank]
    for shard in range(shards):
        shard_copies[2 * shard].wait()
        shard_copies[2 * shard + 1].wait()
        pre = jnp.dot(low, weight_ref[shard], preferred_element_type=jnp.float32)
        for part in range(width // LANES):
            tile = shard * (width // LANES) + part
            lanes = slice(tile * LANES, (tile + 1) * LANES)
            value = pre[:, part * LANES : (part + 1) * LANES]
            value = value + bias_ref[:, column + tile * LANES : column + (tile + 1) * LANES]
            raised = jnp.exp2(jnp.minimum(value, 80.0) * LOG2E)
            small = raised - 0.5 * raised * raised
            delta = jnp.maximum(value, jnp.where(raised < 0.01, small, jnp.log(1.0 + raised)))
            delta_rows[:, tile] = (delta + reset).reshape(count, block, LANES)
            drive_rows[:, tile] = (delta * conv_ref[:, lanes].astype(jnp.float32)).reshape(count, block, LANES)

    rates = [
        -LOG2E * jnp.exp(decay_ref[:, column + tile * LANES : column + (tile + 1) * LANES]) for tile in range(tiles)
    ]

    wide = tiles * LANES
    cut = 2 * LANES
    cuts = -(-wide // cut)

    def finish(index, history, part):
        first = pl.multiple_of(index * block, block)
        lanes = slice(part * cut, min((part + 1) * cut, wide))
        mixed = jnp.dot(out_diag[pl.ds(first, block), :], history[:, lanes], preferred_element_type=jnp.float32)
        gain = gain_ref[:, column + lanes.start : column + lanes.stop]
        full = mixed + gain * conv_ref[pl.ds(first, block), lanes].astype(jnp.float32)
        place = pl.multiple_of(lax.rem(first, rows), block)
        out_ref[lax.div(first, rows), pl.ds(place, block), lanes] = full.astype(out_ref.dtype)

    def advance(index, held, history, before, before_history):
        held = list(held)
        per_row = LANES // block
        columns = in_cols[:, pl.ds(pl.multiple_of(lax.div(index, per_row) * LANES, LANES), LANES)]
        columns = pltpu.roll(columns, lax.rem(LANES - lax.rem(index, per_row) * block, LANES), 1)
        delta_now = delta_rows.at[index]
        drive_now = drive_rows.at[index]
        for inner in range(block):
            into = jnp.broadcast_to(columns[:, inner : inner + 1], (states, LANES))
            for tile in range(tiles):
                lanes = slice(tile * LANES, (tile + 1) * LANES)
                grow = jnp.exp2(delta_now[tile, inner : inner + 1, :] * rates[tile])
                held[tile] = grow * held[tile] + into * drive_now[tile, inner : inner + 1, :]
                history[inner * states : (inner + 1) * states, lanes] = held[tile].astype(jnp.bfloat16)
            if inner % (block // cuts) == 0 and inner // (block // cuts) < cuts:
                finish(before, before_history, inner // (block // cuts))
        return tuple(held)

    held_odd[...] = jnp.zeros_like(held_odd)

    def pair(index, held):
        held = advance(2 * index, held, held_even, jnp.maximum(2 * index - 1, 0), held_odd)
        return advance(2 * index + 1, held, held_odd, 2 * index, held_even)

    start = tuple(jnp.zeros((states, LANES), jnp.float32) for _ in range(tiles))
    lax.fori_loop(0, count // 2, pair, start)
    for part in range(cuts):
        finish(count - 1, held_odd, part)


def state_scan(reset_col, low, delta_parts, bias, decay, gain, convs, ctx, first_shard, shards):
    toks = low.shape[0]
    rank, width = delta_parts.shape[1:]
    states = decay.shape[0]
    rows = toks // ctx
    wide = shards * width
    steps = toks * wide * states
    whole = pl.BlockSpec(memory_space=pltpu.VMEM)
    left = pl.BlockSpec(memory_space=pl.ANY)
    return pl.pallas_call(
        functools.partial(scan_kernel, rank, first_shard),
        in_specs=[left, left, left, whole, whole, whole, left, left],
        out_specs=whole,
        out_shape=jax.ShapeDtypeStruct((ctx, rows, wide), jnp.bfloat16),
        scratch_shapes=[
            pltpu.VMEM(reset_col.shape, reset_col.dtype),
            pltpu.VMEM(low.shape, low.dtype),
            pltpu.VMEM((shards, rank, width), jnp.bfloat16),
            pltpu.VMEM((toks, wide), jnp.bfloat16),
            pltpu.SemaphoreType.DMA((2 + 2 * shards,)),
            pltpu.VMEM((states, toks), jnp.float32),
            pltpu.VMEM((toks, 16 * states), jnp.bfloat16),
            pltpu.VMEM((toks // 16, wide // LANES, 16, LANES), jnp.float32),
            pltpu.VMEM((toks // 16, wide // LANES, 16, LANES), jnp.float32),
            pltpu.VMEM((16 * states, wide), jnp.bfloat16),
            pltpu.VMEM((16 * states, wide), jnp.bfloat16),
        ],
        compiler_params=pltpu.CompilerParams(vmem_limit_bytes=54 << 20),
        cost_estimate=pl.CostEstimate(
            flops=6 * steps, bytes_accessed=2 * shards * rank * width + 4 * toks * wide, transcendentals=steps
        ),
        name=f"state_scan_{first_shard}",
    )(reset_col, low, delta_parts, bias, decay, gain, *convs)


def gate_kernel(fold, width, first_slot, y_ref, gate_hbm, *refs):
    out_hbm, gate_ref, mixed_ref, in_sems, out_sems = refs[-5:]
    ctx, _, wide = y_ref.shape
    slots = wide // width
    column = first_slot * ctx * width
    ins, outs = [], []
    for slot in range(slots):
        here = pl.ds(slot * ctx * width, ctx * width)
        there = pl.ds(column + slot * ctx * width, ctx * width)
        ins.append(pltpu.make_async_copy(gate_hbm.at[:, there], gate_ref.at[:, here], in_sems.at[slot]))
        outs.append(pltpu.make_async_copy(mixed_ref.at[:, here], out_hbm.at[:, there], out_sems.at[slot]))
        ins[slot].start()
    for slot in range(slots):
        ins[slot].wait()
        for piece in range(ctx):
            lanes = piece_lanes(slot, piece, ctx, fold, width)
            value = y_ref[piece, :, slot * width : (slot + 1) * width].astype(jnp.float32)
            mixed_ref[:, lanes] = (value * silu(gate_ref[:, lanes].astype(jnp.float32))).astype(mixed_ref.dtype)
        outs[slot].start()
    for copy in outs:
        copy.wait()


def apply_gate(pieces, gate, fold, width, first_slot, before=None):
    rows = gate.shape[0]
    ctx, _, wide = pieces.shape
    left = pl.BlockSpec(memory_space=pl.ANY)
    operands = [pieces, gate] + ([] if before is None else [before])
    return pl.pallas_call(
        functools.partial(gate_kernel, fold, width, first_slot),
        in_specs=[pl.BlockSpec(memory_space=pltpu.VMEM)] + [left] * (len(operands) - 1),
        out_specs=left,
        out_shape=jax.ShapeDtypeStruct(gate.shape, jnp.bfloat16),
        scratch_shapes=[
            pltpu.VMEM((rows, ctx * wide), gate.dtype),
            pltpu.VMEM((rows, ctx * wide), gate.dtype),
            pltpu.SemaphoreType.DMA((wide // width,)),
            pltpu.SemaphoreType.DMA((wide // width,)),
        ],
        input_output_aliases={} if before is None else {2: 0},
        compiler_params=pltpu.CompilerParams(vmem_limit_bytes=54 << 20),
        cost_estimate=pl.CostEstimate(
            flops=4 * pieces.size, bytes_accessed=6 * pieces.size, transcendentals=pieces.size
        ),
        name=f"gate_{first_slot}",
    )(*operands)


def shifted(value, axis, by):
    size = lax.axis_size(axis)
    pairs = [(i, i + by) for i in range(size) if 0 <= i + by < size]
    return lax.ppermute(value, axis, pairs)


def exchange(value):
    return lax.all_to_all(value, "ctx", 0, 0, tiled=True)


def local(
    queries,
    keys,
    values,
    mixer_input,
    gate_input,
    segment_ids,
    conv_weight,
    conv_bias,
    select_weight,
    delta_weight,
    delta_bias,
    decay_log,
    skip_gain,
):
    ctx = lax.axis_size("ctx")
    shards = lax.axis_size("rep")
    place = lax.axis_index("ctx")
    rows, channels = mixer_input.shape[1:]
    rank = delta_weight.shape[0]
    states = decay_log.shape[1]
    width = max(channels // (shards * ctx), LANES)
    fold = width * shards * ctx // channels
    seg = segment_ids[0]
    toks = seg.shape[0]
    back = min(ctx - 1, -(-(toks // 2 - 1) // rows))

    slots = shards // fold

    def own_part(array):
        cut = array.reshape(array.shape[:-1] + (slots, fold, ctx // fold, width))
        cut = lax.dynamic_index_in_dim(cut, place // fold, cut.ndim - 2, keepdims=False)
        cut = lax.dynamic_index_in_dim(cut, place % fold, cut.ndim - 2, keepdims=False)
        return cut.reshape(array.shape[:-1] + (slots * width,))

    def own_columns(weight):
        return lax.dynamic_slice_in_dim(weight, place // fold * width, width, 1)

    def gathered(own):
        parts = lax.all_gather(own, "rep", axis=0)
        if fold > 1:
            parts = parts.reshape((slots, fold) + own.shape)
            parts = lax.dynamic_index_in_dim(parts, place % fold, 1, keepdims=False)
        return parts

    select_parts = gathered(own_columns(select_weight))
    packed = pack(mixer_input[0], ctx, fold, width)

    same = jnp.concatenate([jnp.zeros((1,), bool), seg[1:] == seg[:-1]])
    reset_col = jnp.where(same, 0.0, FAR)[:, None]
    seg_before = jnp.concatenate([jnp.full((3,), -1, jnp.int32), seg])
    match = jnp.stack([(seg_before[tap : tap + toks] == seg) for tap in range(3)], axis=1).astype(jnp.float32)
    seg_pad = jnp.concatenate([jnp.full((back * rows,), -1, jnp.int32), seg])
    seg_k = lax.dynamic_slice_in_dim(seg_pad, place * rows, (back + 1) * rows, 0)
    own = (
        own_part(delta_bias)[None, :],
        own_part(jnp.transpose(decay_log)),
        own_part(skip_gain)[None, :],
        reset_col,
        seg_k[back * rows :, None],
        seg_k[None, :],
        jnp.concatenate([keys[0], values[0]], axis=1),
        own_part(conv_weight),
        own_part(conv_bias)[None, :],
        match,
        own_columns(delta_weight),
    )
    pieces, own = lax.optimization_barrier((exchange(packed), own))
    bias, decay, gain, reset_col, seg_q, seg_k, both, conv_weight, conv_bias, match, delta_own = own
    delta_parts = gathered(delta_own)

    *convs, parts = conv_select(match, pieces, conv_weight, conv_bias, select_parts)
    low = normalise(exchange(parts), rank)

    low, both = lax.optimization_barrier((low, both))
    blocks = [shifted(both, "ctx", by) for by in range(back, 0, -1)] + [both]
    low = exchange(low).reshape(toks, low.shape[2])

    split = slots * 5 // 8
    scanned = [
        state_scan(reset_col, low, delta_parts, bias, decay, gain, convs, ctx, first, count)
        for first, count in ((0, split), (split, slots - split))
    ]
    scanned[0], blocks = lax.optimization_barrier((scanned[0], blocks))
    attended = attention(queries[0], blocks, seg_q, seg_k, 0, KEY_VALUE_HEADS)
    scanned = [exchange(part) for part in scanned]
    scanned[0], attended = lax.optimization_barrier((scanned[0], attended))
    mixed = apply_gate(scanned[0], gate_input[0], fold, width, 0)
    scanned[1], mixed = lax.optimization_barrier((scanned[1], mixed))
    mixed = apply_gate(scanned[1], gate_input[0], fold, width, split, mixed)
    return (attended[None], mixed[None])


def solution(mesh):
    placed = (
        P("rep", "ctx", None),
        P("rep", "ctx", None),
        P("rep", "ctx", None),
        P("rep", "ctx", None),
        P("rep", "ctx", None),
        P("rep", None),
        P(),
        P(),
        P(None, "rep"),
        P(None, "rep"),
        P(),
        P(),
        P(),
    )
    return jax.shard_map(
        local,
        mesh=mesh,
        in_specs=placed,
        out_specs=(P("rep", "ctx", None), P("rep", "ctx", None)),
        check_vma=False,
    )
```

```python
import functools
import math

import jax
import jax.numpy as jnp
from jax import lax
from jax.experimental import pallas as pl
from jax.experimental.pallas import tpu as pltpu
from jax.sharding import PartitionSpec as P

QUERY_HEADS = 32
KEY_VALUE_HEADS = 4
HEAD_WIDTH = 128
LANES = 128
SUBLANES = 8
LOG2E = 1.0 / math.log(2.0)
FAR = 1e30


def silu(value):
    half = 0.5 * value
    return half + half * jnp.tanh(half)


def attention_kernel(begin, seg_q_ref, seg_k_ref, q_ref, *refs):
    out_ref = refs[-1]
    refs = refs[: -1 if begin == 0 else -2]
    rows = q_ref.shape[0]
    span = seg_k_ref.shape[1]
    groups = QUERY_HEADS // KEY_VALUE_HEADS
    row = lax.broadcasted_iota(jnp.int32, (rows, span), 0) + (span - rows)
    col = lax.broadcasted_iota(jnp.int32, (rows, span), 1)
    allowed = (col <= row) & (seg_q_ref[...] == seg_k_ref[...])
    shift = jnp.where(allowed, 0.0, -FAR)
    keys = jnp.concatenate([ref[...] for ref in refs[0::2]], axis=0)
    vals = jnp.concatenate([ref[...] for ref in refs[1::2]], axis=0)
    factor = LOG2E / math.sqrt(HEAD_WIDTH)
    batch = 4
    for first in range(0, groups, batch):
        cuts = [slice(head * HEAD_WIDTH, (head + 1) * HEAD_WIDTH) for head in range(first, first + batch)]
        scores = [
            lax.dot_general(q_ref[:, cut], keys, (((1,), (1,)), ((), ())), preferred_element_type=jnp.float32)
            for cut in cuts
        ]
        scores = [score + shift for score in scores]
        tops = [jnp.max(score, axis=-1, keepdims=True) for score in scores]
        weights = [jnp.exp2((score - top) * factor) for score, top in zip(scores, tops)]
        norms = [jnp.sum(weight, axis=-1, keepdims=True) for weight in weights]
        totals = [jnp.dot(weight.astype(jnp.bfloat16), vals, preferred_element_type=jnp.float32) for weight in weights]
        for cut, total, norm in zip(cuts, totals, norms):
            out_ref[:, cut] = (total / norm).astype(out_ref.dtype)


def attention(queries, blocks, seg_q, seg_k, begin, end, before=None):
    rows = queries.shape[0]
    span = seg_k.shape[1]
    group_width = QUERY_HEADS // KEY_VALUE_HEADS * HEAD_WIDTH
    key_spec = pl.BlockSpec((rows, HEAD_WIDTH), lambda h: (0, begin + h))
    value_spec = pl.BlockSpec((rows, HEAD_WIDTH), lambda h: (0, KEY_VALUE_HEADS + begin + h))
    wide = pl.BlockSpec((rows, group_width), lambda h: (0, begin + h))
    operands = [seg_q, seg_k, queries] + [block for block in blocks for _ in range(2)]
    in_specs = [
        pl.BlockSpec((rows, 1), lambda h: (0, 0)),
        pl.BlockSpec((1, span), lambda h: (0, 0)),
        wide,
        *([key_spec, value_spec] * len(blocks)),
    ]
    aliases = {}
    if before is not None:
        aliases = {len(operands): 0}
        operands.append(before)
        in_specs.append(pl.BlockSpec(memory_space=pl.ANY))
    return pl.pallas_call(
        functools.partial(attention_kernel, begin),
        grid=(end - begin,),
        in_specs=in_specs,
        out_specs=wide,
        out_shape=jax.ShapeDtypeStruct(queries.shape, jnp.bfloat16),
        input_output_aliases=aliases,
        compiler_params=pltpu.CompilerParams(vmem_limit_bytes=54 << 20),
        cost_estimate=pl.CostEstimate(
            flops=4 * rows * span * group_width * (end - begin),
            bytes_accessed=4 * rows * group_width * (end - begin),
            transcendentals=rows * span * group_width // HEAD_WIDTH * (end - begin),
        ),
        name=f"attention_{begin}",
    )(*operands)


def piece_lanes(slot, piece, ctx, fold, width):
    start = (slot * ctx + piece % fold * (ctx // fold) + piece // fold) * width
    return slice(start, start + width)


def pack_kernel(fold, width, x_ref, out_ref):
    ctx = out_ref.shape[0]
    for piece in range(ctx):
        for slot in range(out_ref.shape[2] // width):
            out_ref[piece, :, slot * width : (slot + 1) * width] = x_ref[:, piece_lanes(slot, piece, ctx, fold, width)]


def pack(value, ctx, fold, width):
    rows, channels = value.shape
    part = min(rows, 32)
    return pl.pallas_call(
        functools.partial(pack_kernel, fold, width),
        grid=(rows // part,),
        in_specs=[pl.BlockSpec((part, channels), lambda r: (r, 0))],
        out_specs=pl.BlockSpec((ctx, part, channels // ctx), lambda r: (0, r, 0)),
        out_shape=jax.ShapeDtypeStruct((ctx, rows, channels // ctx), value.dtype),
        compiler_params=pltpu.CompilerParams(vmem_limit_bytes=12 << 20),
        name="pack",
    )(value)


def conv_select_kernel(match_ref, x_ref, weight_ref, bias_ref, select_ref, early_ref, late_ref, part_ref, masks, padded, total):
    step = pl.program_id(0)
    pieces, rows, wide = x_ref.shape
    toks = pieces * rows
    tiles = wide // LANES
    slots, outputs, _ = select_ref.shape

    @pl.when(step == 0)
    def _():
        for tap in range(3):
            masks[tap] = jnp.broadcast_to(match_ref[:, tap : tap + 1], (toks, LANES))
        for tile in range(tiles):
            padded[tile, 0:SUBLANES, :] = jnp.zeros((SUBLANES, LANES), jnp.float32)

    outs = []
    for tile in range(tiles):
        lanes = slice(tile * LANES, (tile + 1) * LANES)
        for piece in range(pieces):
            first = SUBLANES + piece * rows
            padded[tile, first : first + rows, :] = x_ref[piece, :, lanes].astype(jnp.float32)
        half = jnp.broadcast_to(0.5 * bias_ref[0:1, lanes], (toks, LANES))
        for tap in range(4):
            moved = padded[tile, SUBLANES - 3 + tap : SUBLANES - 3 + tap + toks, :]
            term = (0.5 * weight_ref[tap : tap + 1, lanes]) * moved
            half = half + (term * masks[tap] if tap < 3 else term)
        outs.append((half + half * jnp.tanh(half)).astype(jnp.bfloat16))
    conv = jnp.concatenate(outs, axis=1)
    select = jnp.concatenate([select_ref[slot] for slot in range(slots)], axis=1)
    added = lax.dot_general(conv, select, (((1,), (1,)), ((), ())), preferred_element_type=jnp.float32)

    @pl.when(step == 0)
    def _():
        early_ref[...] = conv
        total[...] = added

    @pl.when(step == 1)
    def _():
        late_ref[...] = conv
        spare = part_ref.shape[2] - outputs
        full = (total[...] + added).astype(part_ref.dtype)
        for piece in range(pieces):
            part_ref[piece, :, 0:outputs] = full[piece * rows : (piece + 1) * rows, :]
            part_ref[piece, :, outputs:] = jnp.zeros((rows, spare), part_ref.dtype)


def conv_select(match, pieces, conv_weight, conv_bias, select_parts):
    slots, outputs, width = select_parts.shape
    ctx, rows, columns = pieces.shape
    toks = ctx * rows
    padded_outputs = -(-outputs // LANES) * LANES
    wide = columns // 2
    half = pl.BlockSpec((toks, wide), lambda s: (0, 0))
    return pl.pallas_call(
        conv_select_kernel,
        grid=(2,),
        in_specs=[
            pl.BlockSpec(match.shape, lambda s: (0, 0)),
            pl.BlockSpec((ctx, rows, wide), lambda s: (0, 0, s)),
            pl.BlockSpec((4, wide), lambda s: (0, s)),
            pl.BlockSpec((1, wide), lambda s: (0, s)),
            pl.BlockSpec((slots // 2, outputs, width), lambda s: (s, 0, 0)),
        ],
        out_specs=[half, half, pl.BlockSpec((ctx, rows, padded_outputs), lambda s: (0, 0, 0))],
        scratch_shapes=[
            pltpu.VMEM((3, toks, LANES), jnp.float32),
            pltpu.VMEM((wide // LANES, SUBLANES + toks, LANES), jnp.float32),
            pltpu.VMEM((toks, outputs), jnp.float32),
        ],
        out_shape=[
            jax.ShapeDtypeStruct((toks, wide), jnp.bfloat16),
            jax.ShapeDtypeStruct((toks, wide), jnp.bfloat16),
            jax.ShapeDtypeStruct((ctx, rows, padded_outputs), jnp.bfloat16),
        ],
        compiler_params=pltpu.CompilerParams(vmem_limit_bytes=32 << 20),
        cost_estimate=pl.CostEstimate(
            flops=2 * toks * slots * width * outputs,
            bytes_accessed=2 * pieces.size * 2 + 2 * select_parts.size,
            transcendentals=pieces.size,
        ),
        name="conv_select",
    )(match, pieces, conv_weight, conv_bias, select_parts)


def normalise_kernel(rank, part_ref, out_ref):
    pieces = part_ref.shape[0]
    total = part_ref[0].astype(jnp.float32)
    for piece in range(1, pieces):
        total = total + part_ref[piece].astype(jnp.float32)
    low = total[:, :rank]
    scale = lax.rsqrt(jnp.mean(low * low, axis=-1, keepdims=True) + 1e-06)
    low = (low * scale).astype(out_ref.dtype)
    maps = total[:, rank:].astype(out_ref.dtype)
    for piece in range(pieces):
        out_ref[piece, :, :rank] = low
        out_ref[piece, :, rank:] = maps


def normalise(parts, rank):
    return pl.pallas_call(
        functools.partial(normalise_kernel, rank),
        out_shape=jax.ShapeDtypeStruct(parts.shape, jnp.bfloat16),
        compiler_params=pltpu.CompilerParams(vmem_limit_bytes=12 << 20),
        name="normalise",
    )(parts)


def scan_kernel(rank, first_shard, reset_hbm, low_ref, weight_hbm, bias_ref, decay_ref, gain_ref,
                early_hbm, late_hbm, out_ref, reset_ref, weight_ref, conv_ref, sems, in_cols, out_diag, delta_rows, drive_rows, held_even, held_odd):
    toks = low_ref.shape[0]
    states = decay_ref.shape[0]
    shards = weight_ref.shape[0]
    width = weight_ref.shape[2]
    tiles = shards * width // LANES
    column = first_shard * width
    reset_copy = pltpu.make_async_copy(reset_hbm, reset_ref, sems.at[0])
    reset_copy.start()
    shard_copies = []
    for shard in range(shards):
        at = shard * width
        start = column + at
        middle = early_hbm.shape[1]
        source = early_hbm.at[:, pl.ds(start, width)] if start < middle else late_hbm.at[:, pl.ds(start - middle, width)]
        shard_copies += [
            pltpu.make_async_copy(weight_hbm.at[first_shard + shard], weight_ref.at[shard], sems.at[1 + 2 * shard]),
            pltpu.make_async_copy(source, conv_ref.at[:, pl.ds(at, width)], sems.at[2 + 2 * shard]),
        ]
    for copy in shard_copies:
        copy.start()
    rows = out_ref.shape[1]
    block = 16
    span = block * states
    count = toks // block

    in_cols[...] = jnp.transpose(low_ref[:, rank : rank + LANES].astype(jnp.float32))[0:states, :]
    bits = states.bit_length() - 1
    lane = lax.broadcasted_iota(jnp.int32, (states, span), 1)
    spread = jnp.where((lane & (states - 1)) == lax.broadcasted_iota(jnp.int32, (states, span), 0), 1.0, 0.0)
    spread_out = jnp.dot(
        low_ref[:, rank + states : rank + 2 * states], spread.astype(jnp.bfloat16), preferred_element_type=jnp.float32
    )
    here = lax.shift_right_logical(lax.broadcasted_iota(jnp.int32, (block, span), 1), bits)
    there = lax.broadcasted_iota(jnp.int32, (block, span), 0)
    keep = jnp.where(here == there, 1.0, 0.0)
    out_diag[...] = (spread_out.reshape(count, block, span) * keep[None]).reshape(toks, span).astype(jnp.bfloat16)

    reset_copy.wait()
    reset = jnp.broadcast_to(reset_ref[...], (toks, LANES))
    low = low_ref[:, 0:rank]
    for shard in range(shards):
        shard_copies[2 * shard].wait()
        shard_copies[2 * shard + 1].wait()
        pre = jnp.dot(low, weight_ref[shard], preferred_element_type=jnp.float32)
        for part in range(width // LANES):
            tile = shard * (width // LANES) + part
            lanes = slice(tile * LANES, (tile + 1) * LANES)
            value = pre[:, part * LANES : (part + 1) * LANES]
            value = value + bias_ref[:, column + tile * LANES : column + (tile + 1) * LANES]
            raised = jnp.exp2(jnp.minimum(value, 80.0) * LOG2E)
            small = raised - 0.5 * raised * raised
            delta = jnp.maximum(value, jnp.where(raised < 0.01, small, jnp.log(1.0 + raised)))
            delta_rows[:, tile] = (delta + reset).reshape(count, block, LANES)
            drive_rows[:, tile] = (delta * conv_ref[:, lanes].astype(jnp.float32)).reshape(count, block, LANES)

    rates = [
        -LOG2E * jnp.exp(decay_ref[:, column + tile * LANES : column + (tile + 1) * LANES]) for tile in range(tiles)
    ]

    wide = tiles * LANES
    cut = 2 * LANES
    cuts = -(-wide // cut)

    def finish(index, history, part):
        first = pl.multiple_of(index * block, block)
        lanes = slice(part * cut, min((part + 1) * cut, wide))
        mixed = jnp.dot(out_diag[pl.ds(first, block), :], history[:, lanes], preferred_element_type=jnp.float32)
        gain = gain_ref[:, column + lanes.start : column + lanes.stop]
        full = mixed + gain * conv_ref[pl.ds(first, block), lanes].astype(jnp.float32)
        place = pl.multiple_of(lax.rem(first, rows), block)
        out_ref[lax.div(first, rows), pl.ds(place, block), lanes] = full.astype(out_ref.dtype)

    def advance(index, held, history, before, before_history):
        held = list(held)
        per_row = LANES // block
        columns = in_cols[:, pl.ds(pl.multiple_of(lax.div(index, per_row) * LANES, LANES), LANES)]
        columns = pltpu.roll(columns, lax.rem(LANES - lax.rem(index, per_row) * block, LANES), 1)
        delta_now = delta_rows.at[index]
        drive_now = drive_rows.at[index]
        for inner in range(block):
            into = jnp.broadcast_to(columns[:, inner : inner + 1], (states, LANES))
            for tile in range(tiles):
                lanes = slice(tile * LANES, (tile + 1) * LANES)
                grow = jnp.exp2(delta_now[tile, inner : inner + 1, :] * rates[tile])
                held[tile] = grow * held[tile] + into * drive_now[tile, inner : inner + 1, :]
                history[inner * states : (inner + 1) * states, lanes] = held[tile].astype(jnp.bfloat16)
            if inner % (block // cuts) == 0 and inner // (block // cuts) < cuts:
                finish(before, before_history, inner // (block // cuts))
        return tuple(held)

    held_odd[...] = jnp.zeros_like(held_odd)

    def pair(index, held):
        held = advance(2 * index, held, held_even, jnp.maximum(2 * index - 1, 0), held_odd)
        return advance(2 * index + 1, held, held_odd, 2 * index, held_even)

    start = tuple(jnp.zeros((states, LANES), jnp.float32) for _ in range(tiles))
    lax.fori_loop(0, count // 2, pair, start)
    for part in range(cuts):
        finish(count - 1, held_odd, part)


def state_scan(reset_col, low, delta_parts, bias, decay, gain, convs, ctx, first_shard, shards):
    toks = low.shape[0]
    rank, width = delta_parts.shape[1:]
    states = decay.shape[0]
    rows = toks // ctx
    wide = shards * width
    steps = toks * wide * states
    whole = pl.BlockSpec(memory_space=pltpu.VMEM)
    left = pl.BlockSpec(memory_space=pl.ANY)
    return pl.pallas_call(
        functools.partial(scan_kernel, rank, first_shard),
        in_specs=[left, whole, left, whole, whole, whole, left, left],
        out_specs=whole,
        out_shape=jax.ShapeDtypeStruct((ctx, rows, wide), jnp.bfloat16),
        scratch_shapes=[
            pltpu.VMEM(reset_col.shape, reset_col.dtype),
            pltpu.VMEM((shards, rank, width), jnp.bfloat16),
            pltpu.VMEM((toks, wide), jnp.bfloat16),
            pltpu.SemaphoreType.DMA((1 + 2 * shards,)),
            pltpu.VMEM((states, toks), jnp.float32),
            pltpu.VMEM((toks, 16 * states), jnp.bfloat16),
            pltpu.VMEM((toks // 16, wide // LANES, 16, LANES), jnp.float32),
            pltpu.VMEM((toks // 16, wide // LANES, 16, LANES), jnp.float32),
            pltpu.VMEM((16 * states, wide), jnp.bfloat16),
            pltpu.VMEM((16 * states, wide), jnp.bfloat16),
        ],
        compiler_params=pltpu.CompilerParams(vmem_limit_bytes=52 << 20),
        cost_estimate=pl.CostEstimate(
            flops=6 * steps, bytes_accessed=2 * shards * rank * width + 4 * toks * wide, transcendentals=steps
        ),
        name=f"state_scan_{first_shard}",
    )(reset_col, low, delta_parts, bias, decay, gain, *convs)


def silu_kernel(gate_ref, out_ref):
    out_ref[...] = silu(gate_ref[...].astype(jnp.float32)).astype(out_ref.dtype)


def silu_rows(gate):
    rows, channels = gate.shape
    block = pl.BlockSpec((min(rows, 32), channels), lambda r: (r, 0))
    return pl.pallas_call(
        silu_kernel,
        grid=(rows // min(rows, 32),),
        in_specs=[block],
        out_specs=block,
        out_shape=jax.ShapeDtypeStruct(gate.shape, gate.dtype),
        compiler_params=pltpu.CompilerParams(vmem_limit_bytes=16 << 20),
        cost_estimate=pl.CostEstimate(flops=4 * gate.size, bytes_accessed=4 * gate.size, transcendentals=gate.size),
        name="silu",
    )(gate)


def gate_kernel(fold, width, gate_ref, *refs):
    out_ref = refs[-1]
    slot = 0
    for y_ref in refs[:-1]:
        ctx, _, wide = y_ref.shape
        for place in range(wide // width):
            for piece in range(ctx):
                lanes = piece_lanes(slot, piece, ctx, fold, width)
                out_ref[:, lanes] = y_ref[piece, :, place * width : (place + 1) * width] * gate_ref[:, lanes]
            slot += 1


def apply_gate(parts, gate, fold, width):
    rows, channels = gate.shape
    ctx = parts[0].shape[0]
    part = min(rows, 32)
    columns = pl.BlockSpec((part, channels), lambda r: (r, 0))
    return pl.pallas_call(
        functools.partial(gate_kernel, fold, width),
        grid=(rows // part,),
        in_specs=[columns] + [pl.BlockSpec((ctx, part, array.shape[2]), lambda r: (0, r, 0)) for array in parts],
        out_specs=columns,
        out_shape=jax.ShapeDtypeStruct(gate.shape, jnp.bfloat16),
        compiler_params=pltpu.CompilerParams(vmem_limit_bytes=16 << 20),
        cost_estimate=pl.CostEstimate(flops=4 * gate.size, bytes_accessed=6 * gate.size, transcendentals=gate.size),
        name="gate",
    )(gate, *parts)


def shifted(value, axis, by):
    size = lax.axis_size(axis)
    pairs = [(i, i + by) for i in range(size) if 0 <= i + by < size]
    return lax.ppermute(value, axis, pairs)


def exchange(value):
    return lax.all_to_all(value, "ctx", 0, 0, tiled=True)


def local(
    queries,
    keys,
    values,
    mixer_input,
    gate_input,
    segment_ids,
    conv_weight,
    conv_bias,
    select_weight,
    delta_weight,
    delta_bias,
    decay_log,
    skip_gain,
):
    ctx = lax.axis_size("ctx")
    shards = lax.axis_size("rep")
    place = lax.axis_index("ctx")
    rows, channels = mixer_input.shape[1:]
    rank = delta_weight.shape[0]
    states = decay_log.shape[1]
    width = max(channels // (shards * ctx), LANES)
    fold = width * shards * ctx // channels
    seg = segment_ids[0]
    toks = seg.shape[0]
    back = min(ctx - 1, -(-(toks // 2 - 1) // rows))

    slots = shards // fold

    def own_part(array):
        cut = array.reshape(array.shape[:-1] + (slots, fold, ctx // fold, width))
        cut = lax.dynamic_index_in_dim(cut, place // fold, cut.ndim - 2, keepdims=False)
        cut = lax.dynamic_index_in_dim(cut, place % fold, cut.ndim - 2, keepdims=False)
        return cut.reshape(array.shape[:-1] + (slots * width,))

    def own_columns(weight):
        return lax.dynamic_slice_in_dim(weight, place // fold * width, width, 1)

    def gathered(own):
        parts = lax.all_gather(own, "rep", axis=0)
        if fold > 1:
            parts = parts.reshape((slots, fold) + own.shape)
            parts = lax.dynamic_index_in_dim(parts, place % fold, 1, keepdims=False)
        return parts

    select_parts = gathered(own_columns(select_weight))
    packed = pack(mixer_input[0], ctx, fold, width)

    same = jnp.concatenate([jnp.zeros((1,), bool), seg[1:] == seg[:-1]])
    reset_col = jnp.where(same, 0.0, FAR)[:, None]
    seg_before = jnp.concatenate([jnp.full((3,), -1, jnp.int32), seg])
    match = jnp.stack([(seg_before[tap : tap + toks] == seg) for tap in range(3)], axis=1).astype(jnp.float32)
    seg_pad = jnp.concatenate([jnp.full((back * rows,), -1, jnp.int32), seg])
    seg_k = lax.dynamic_slice_in_dim(seg_pad, place * rows, (back + 1) * rows, 0)
    own = (
        own_part(delta_bias)[None, :],
        own_part(jnp.transpose(decay_log)),
        own_part(skip_gain)[None, :],
        reset_col,
        seg_k[back * rows :, None],
        seg_k[None, :],
        jnp.concatenate([keys[0], values[0]], axis=1),
        own_part(conv_weight),
        own_part(conv_bias)[None, :],
        match,
        own_columns(delta_weight),
    )
    pieces, own = lax.optimization_barrier((exchange(packed), own))
    bias, decay, gain, reset_col, seg_q, seg_k, both, conv_weight, conv_bias, match, delta_own = own
    delta_parts = gathered(delta_own)

    *convs, parts = conv_select(match, pieces, conv_weight, conv_bias, select_parts)
    parts, gate = lax.optimization_barrier((parts, gate_input[0]))
    parts, gate = lax.optimization_barrier((exchange(parts), silu_rows(gate)))
    low = normalise(parts, rank)

    low, both = lax.optimization_barrier((low, both))
    blocks = [shifted(both, "ctx", by) for by in range(back, 0, -1)] + [both]
    low = exchange(low).reshape(toks, low.shape[2])

    split = slots * 5 // 8
    scanned = [
        state_scan(reset_col, low, delta_parts, bias, decay, gain, convs, ctx, first, count)
        for first, count in ((0, split), (split, slots - split))
    ]
    scanned[0], blocks = lax.optimization_barrier((scanned[0], blocks))
    attended = attention(queries[0], blocks, seg_q, seg_k, 0, KEY_VALUE_HEADS)
    scanned = [exchange(part) for part in scanned]
    scanned[0], attended = lax.optimization_barrier((scanned[0], attended))
    mixed = apply_gate(scanned, gate, fold, width)
    return (attended[None], mixed[None])


def solution(mesh):
    placed = (
        P("rep", "ctx", None),
        P("rep", "ctx", None),
        P("rep", "ctx", None),
        P("rep", "ctx", None),
        P("rep", "ctx", None),
        P("rep", None),
        P(),
        P(),
        P(None, "rep"),
        P(None, "rep"),
        P(),
        P(),
        P(),
    )
    return jax.shard_map(
        local,
        mesh=mesh,
        in_specs=placed,
        out_specs=(P("rep", "ctx", None), P("rep", "ctx", None)),
        check_vma=False,
    )
```

```python
import functools
import math

import jax
import jax.numpy as jnp
from jax import lax
from jax.experimental import pallas as pl
from jax.experimental.pallas import tpu as pltpu
from jax.sharding import PartitionSpec as P

QUERY_HEADS = 32
KEY_VALUE_HEADS = 4
HEAD_WIDTH = 128
LANES = 128
SUBLANES = 8
LOG2E = 1.0 / math.log(2.0)
FAR = 1e30


def silu(value):
    half = 0.5 * value
    return half + half * jnp.tanh(half)


def attention_kernel(begin, seg_q_ref, seg_k_ref, q_ref, *refs):
    out_ref = refs[-1]
    refs = refs[: -1 if begin == 0 else -2]
    rows = q_ref.shape[0]
    span = seg_k_ref.shape[1]
    groups = QUERY_HEADS // KEY_VALUE_HEADS
    row = lax.broadcasted_iota(jnp.int32, (rows, span), 0) + (span - rows)
    col = lax.broadcasted_iota(jnp.int32, (rows, span), 1)
    allowed = (col <= row) & (seg_q_ref[...] == seg_k_ref[...])
    shift = jnp.where(allowed, 0.0, -FAR)
    keys = jnp.concatenate([ref[...] for ref in refs[0::2]], axis=0)
    vals = jnp.concatenate([ref[...] for ref in refs[1::2]], axis=0)
    factor = LOG2E / math.sqrt(HEAD_WIDTH)
    batch = 4
    for first in range(0, groups, batch):
        cuts = [slice(head * HEAD_WIDTH, (head + 1) * HEAD_WIDTH) for head in range(first, first + batch)]
        scores = [
            lax.dot_general(q_ref[:, cut], keys, (((1,), (1,)), ((), ())), preferred_element_type=jnp.float32)
            for cut in cuts
        ]
        scores = [score + shift for score in scores]
        tops = [jnp.max(score, axis=-1, keepdims=True) for score in scores]
        weights = [jnp.exp2((score - top) * factor) for score, top in zip(scores, tops)]
        norms = [jnp.sum(weight, axis=-1, keepdims=True) for weight in weights]
        totals = [jnp.dot(weight.astype(jnp.bfloat16), vals, preferred_element_type=jnp.float32) for weight in weights]
        for cut, total, norm in zip(cuts, totals, norms):
            out_ref[:, cut] = (total / norm).astype(out_ref.dtype)


def attention(queries, blocks, seg_q, seg_k, begin, end, before=None):
    rows = queries.shape[0]
    span = seg_k.shape[1]
    group_width = QUERY_HEADS // KEY_VALUE_HEADS * HEAD_WIDTH
    key_spec = pl.BlockSpec((rows, HEAD_WIDTH), lambda h: (0, begin + h))
    value_spec = pl.BlockSpec((rows, HEAD_WIDTH), lambda h: (0, KEY_VALUE_HEADS + begin + h))
    wide = pl.BlockSpec((rows, group_width), lambda h: (0, begin + h))
    operands = [seg_q, seg_k, queries] + [block for block in blocks for _ in range(2)]
    in_specs = [
        pl.BlockSpec((rows, 1), lambda h: (0, 0)),
        pl.BlockSpec((1, span), lambda h: (0, 0)),
        wide,
        *([key_spec, value_spec] * len(blocks)),
    ]
    aliases = {}
    if before is not None:
        aliases = {len(operands): 0}
        operands.append(before)
        in_specs.append(pl.BlockSpec(memory_space=pl.ANY))
    return pl.pallas_call(
        functools.partial(attention_kernel, begin),
        grid=(end - begin,),
        in_specs=in_specs,
        out_specs=wide,
        out_shape=jax.ShapeDtypeStruct(queries.shape, jnp.bfloat16),
        input_output_aliases=aliases,
        compiler_params=pltpu.CompilerParams(vmem_limit_bytes=54 << 20),
        cost_estimate=pl.CostEstimate(
            flops=4 * rows * span * group_width * (end - begin),
            bytes_accessed=4 * rows * group_width * (end - begin),
            transcendentals=rows * span * group_width // HEAD_WIDTH * (end - begin),
        ),
        name=f"attention_{begin}",
    )(*operands)


def piece_lanes(slot, piece, ctx, fold, width):
    start = (slot * ctx + piece % fold * (ctx // fold) + piece // fold) * width
    return slice(start, start + width)


def pack_kernel(fold, width, x_ref, out_ref):
    ctx = out_ref.shape[0]
    for piece in range(ctx):
        for slot in range(out_ref.shape[2] // width):
            out_ref[piece, :, slot * width : (slot + 1) * width] = x_ref[:, piece_lanes(slot, piece, ctx, fold, width)]


def pack(value, ctx, fold, width):
    rows, channels = value.shape
    part = min(rows, 32)
    return pl.pallas_call(
        functools.partial(pack_kernel, fold, width),
        grid=(rows // part,),
        in_specs=[pl.BlockSpec((part, channels), lambda r: (r, 0))],
        out_specs=pl.BlockSpec((ctx, part, channels // ctx), lambda r: (0, r, 0)),
        out_shape=jax.ShapeDtypeStruct((ctx, rows, channels // ctx), value.dtype),
        compiler_params=pltpu.CompilerParams(vmem_limit_bytes=12 << 20),
        name="pack",
    )(value)


def conv_select_kernel(match_ref, x_ref, weight_ref, bias_ref, select_ref, early_ref, late_ref, part_ref, masks, padded, total):
    step = pl.program_id(0)
    pieces, rows, wide = x_ref.shape
    toks = pieces * rows
    tiles = wide // LANES
    slots, outputs, _ = select_ref.shape

    @pl.when(step == 0)
    def _():
        for tap in range(3):
            masks[tap] = jnp.broadcast_to(match_ref[:, tap : tap + 1], (toks, LANES))
        for tile in range(tiles):
            padded[tile, 0:SUBLANES, :] = jnp.zeros((SUBLANES, LANES), jnp.float32)

    outs = []
    for tile in range(tiles):
        lanes = slice(tile * LANES, (tile + 1) * LANES)
        for piece in range(pieces):
            first = SUBLANES + piece * rows
            padded[tile, first : first + rows, :] = x_ref[piece, :, lanes].astype(jnp.float32)
        half = jnp.broadcast_to(0.5 * bias_ref[0:1, lanes], (toks, LANES))
        for tap in range(4):
            moved = padded[tile, SUBLANES - 3 + tap : SUBLANES - 3 + tap + toks, :]
            term = (0.5 * weight_ref[tap : tap + 1, lanes]) * moved
            half = half + (term * masks[tap] if tap < 3 else term)
        outs.append((half + half * jnp.tanh(half)).astype(jnp.bfloat16))
    conv = jnp.concatenate(outs, axis=1)
    select = jnp.concatenate([select_ref[slot] for slot in range(slots)], axis=1)
    added = lax.dot_general(conv, select, (((1,), (1,)), ((), ())), preferred_element_type=jnp.float32)

    @pl.when(step == 0)
    def _():
        early_ref[...] = conv
        total[...] = added

    @pl.when(step == 1)
    def _():
        late_ref[...] = conv
        spare = part_ref.shape[2] - outputs
        full = (total[...] + added).astype(part_ref.dtype)
        for piece in range(pieces):
            part_ref[piece, :, 0:outputs] = full[piece * rows : (piece + 1) * rows, :]
            part_ref[piece, :, outputs:] = jnp.zeros((rows, spare), part_ref.dtype)


def conv_select(match, pieces, conv_weight, conv_bias, select_parts):
    slots, outputs, width = select_parts.shape
    ctx, rows, columns = pieces.shape
    toks = ctx * rows
    padded_outputs = -(-outputs // LANES) * LANES
    wide = columns // 2
    half = pl.BlockSpec((toks, wide), lambda s: (0, 0))
    return pl.pallas_call(
        conv_select_kernel,
        grid=(2,),
        in_specs=[
            pl.BlockSpec(match.shape, lambda s: (0, 0)),
            pl.BlockSpec((ctx, rows, wide), lambda s: (0, 0, s)),
            pl.BlockSpec((4, wide), lambda s: (0, s)),
            pl.BlockSpec((1, wide), lambda s: (0, s)),
            pl.BlockSpec((slots // 2, outputs, width), lambda s: (s, 0, 0)),
        ],
        out_specs=[half, half, pl.BlockSpec((ctx, rows, padded_outputs), lambda s: (0, 0, 0))],
        scratch_shapes=[
            pltpu.VMEM((3, toks, LANES), jnp.float32),
            pltpu.VMEM((wide // LANES, SUBLANES + toks, LANES), jnp.float32),
            pltpu.VMEM((toks, outputs), jnp.float32),
        ],
        out_shape=[
            jax.ShapeDtypeStruct((toks, wide), jnp.bfloat16),
            jax.ShapeDtypeStruct((toks, wide), jnp.bfloat16),
            jax.ShapeDtypeStruct((ctx, rows, padded_outputs), jnp.bfloat16),
        ],
        compiler_params=pltpu.CompilerParams(vmem_limit_bytes=32 << 20),
        cost_estimate=pl.CostEstimate(
            flops=2 * toks * slots * width * outputs,
            bytes_accessed=2 * pieces.size * 2 + 2 * select_parts.size,
            transcendentals=pieces.size,
        ),
        name="conv_select",
    )(match, pieces, conv_weight, conv_bias, select_parts)


def normalise_kernel(rank, part_ref, out_ref):
    pieces = part_ref.shape[0]
    total = part_ref[0].astype(jnp.float32)
    for piece in range(1, pieces):
        total = total + part_ref[piece].astype(jnp.float32)
    low = total[:, :rank]
    scale = lax.rsqrt(jnp.mean(low * low, axis=-1, keepdims=True) + 1e-06)
    low = (low * scale).astype(out_ref.dtype)
    maps = total[:, rank:].astype(out_ref.dtype)
    for piece in range(pieces):
        out_ref[piece, :, :rank] = low
        out_ref[piece, :, rank:] = maps


def normalise(parts, rank):
    return pl.pallas_call(
        functools.partial(normalise_kernel, rank),
        out_shape=jax.ShapeDtypeStruct(parts.shape, jnp.bfloat16),
        compiler_params=pltpu.CompilerParams(vmem_limit_bytes=12 << 20),
        name="normalise",
    )(parts)


def scan_kernel(rank, first_shard, reset_hbm, low_hbm, weight_hbm, bias_ref, decay_ref, gain_ref,
                early_hbm, late_hbm, out_ref, reset_ref, low_ref, weight_ref, conv_ref, sems, in_cols, out_diag, delta_rows, drive_rows, held_even, held_odd):
    toks = low_ref.shape[0]
    states = decay_ref.shape[0]
    shards = weight_ref.shape[0]
    width = weight_ref.shape[2]
    tiles = shards * width // LANES
    column = first_shard * width
    low_copy = pltpu.make_async_copy(low_hbm, low_ref, sems.at[0])
    reset_copy = pltpu.make_async_copy(reset_hbm, reset_ref, sems.at[1])
    low_copy.start()
    reset_copy.start()
    shard_copies = []
    for shard in range(shards):
        at = shard * width
        start = column + at
        middle = early_hbm.shape[1]
        source = early_hbm.at[:, pl.ds(start, width)] if start < middle else late_hbm.at[:, pl.ds(start - middle, width)]
        shard_copies += [
            pltpu.make_async_copy(weight_hbm.at[first_shard + shard], weight_ref.at[shard], sems.at[2 + 2 * shard]),
            pltpu.make_async_copy(source, conv_ref.at[:, pl.ds(at, width)], sems.at[3 + 2 * shard]),
        ]
    for copy in shard_copies:
        copy.start()
    low_copy.wait()
    rows = out_ref.shape[1]
    block = 16
    span = block * states
    count = toks // block

    in_cols[...] = jnp.transpose(low_ref[:, rank : rank + LANES].astype(jnp.float32))[0:states, :]
    bits = states.bit_length() - 1
    lane = lax.broadcasted_iota(jnp.int32, (states, span), 1)
    spread = jnp.where((lane & (states - 1)) == lax.broadcasted_iota(jnp.int32, (states, span), 0), 1.0, 0.0)
    spread_out = jnp.dot(
        low_ref[:, rank + states : rank + 2 * states], spread.astype(jnp.bfloat16), preferred_element_type=jnp.float32
    )
    here = lax.shift_right_logical(lax.broadcasted_iota(jnp.int32, (block, span), 1), bits)
    there = lax.broadcasted_iota(jnp.int32, (block, span), 0)
    keep = jnp.where(here == there, 1.0, 0.0)
    out_diag[...] = (spread_out.reshape(count, block, span) * keep[None]).reshape(toks, span).astype(jnp.bfloat16)

    reset_copy.wait()
    reset = jnp.broadcast_to(reset_ref[...], (toks, LANES))
    low = low_ref[:, 0:rank]
    for shard in range(shards):
        shard_copies[2 * shard].wait()
        shard_copies[2 * shard + 1].wait()
        pre = jnp.dot(low, weight_ref[shard], preferred_element_type=jnp.float32)
        for part in range(width // LANES):
            tile = shard * (width // LANES) + part
            lanes = slice(tile * LANES, (tile + 1) * LANES)
            value = pre[:, part * LANES : (part + 1) * LANES]
            value = value + bias_ref[:, column + tile * LANES : column + (tile + 1) * LANES]
            raised = jnp.exp2(jnp.minimum(value, 80.0) * LOG2E)
            small = raised - 0.5 * raised * raised
            delta = jnp.maximum(value, jnp.where(raised < 0.01, small, jnp.log(1.0 + raised)))
            delta_rows[:, tile] = (delta + reset).reshape(count, block, LANES)
            drive_rows[:, tile] = (delta * conv_ref[:, lanes].astype(jnp.float32)).reshape(count, block, LANES)

    rates = [
        -LOG2E * jnp.exp(decay_ref[:, column + tile * LANES : column + (tile + 1) * LANES]) for tile in range(tiles)
    ]

    wide = tiles * LANES
    cut = 2 * LANES
    cuts = -(-wide // cut)

    def finish(index, history, part):
        first = pl.multiple_of(index * block, block)
        lanes = slice(part * cut, min((part + 1) * cut, wide))
        mixed = jnp.dot(out_diag[pl.ds(first, block), :], history[:, lanes], preferred_element_type=jnp.float32)
        gain = gain_ref[:, column + lanes.start : column + lanes.stop]
        full = mixed + gain * conv_ref[pl.ds(first, block), lanes].astype(jnp.float32)
        place = pl.multiple_of(lax.rem(first, rows), block)
        out_ref[lax.div(first, rows), pl.ds(place, block), lanes] = full.astype(out_ref.dtype)

    def advance(index, held, history, before, before_history):
        held = list(held)
        per_row = LANES // block
        columns = in_cols[:, pl.ds(pl.multiple_of(lax.div(index, per_row) * LANES, LANES), LANES)]
        columns = pltpu.roll(columns, lax.rem(LANES - lax.rem(index, per_row) * block, LANES), 1)
        delta_now = delta_rows.at[index]
        drive_now = drive_rows.at[index]
        for inner in range(block):
            into = jnp.broadcast_to(columns[:, inner : inner + 1], (states, LANES))
            for tile in range(tiles):
                lanes = slice(tile * LANES, (tile + 1) * LANES)
                grow = jnp.exp2(delta_now[tile, inner : inner + 1, :] * rates[tile])
                held[tile] = grow * held[tile] + into * drive_now[tile, inner : inner + 1, :]
                history[inner * states : (inner + 1) * states, lanes] = held[tile].astype(jnp.bfloat16)
            if inner % (block // cuts) == 0 and inner // (block // cuts) < cuts:
                finish(before, before_history, inner // (block // cuts))
        return tuple(held)

    held_odd[...] = jnp.zeros_like(held_odd)

    def pair(index, held):
        held = advance(2 * index, held, held_even, jnp.maximum(2 * index - 1, 0), held_odd)
        return advance(2 * index + 1, held, held_odd, 2 * index, held_even)

    start = tuple(jnp.zeros((states, LANES), jnp.float32) for _ in range(tiles))
    lax.fori_loop(0, count // 2, pair, start)
    for part in range(cuts):
        finish(count - 1, held_odd, part)


def state_scan(reset_col, low, delta_parts, bias, decay, gain, convs, ctx, first_shard, shards):
    toks = low.shape[0]
    rank, width = delta_parts.shape[1:]
    states = decay.shape[0]
    rows = toks // ctx
    wide = shards * width
    steps = toks * wide * states
    whole = pl.BlockSpec(memory_space=pltpu.VMEM)
    left = pl.BlockSpec(memory_space=pl.ANY)
    return pl.pallas_call(
        functools.partial(scan_kernel, rank, first_shard),
        in_specs=[left, left, left, whole, whole, whole, left, left],
        out_specs=whole,
        out_shape=jax.ShapeDtypeStruct((ctx, rows, wide), jnp.bfloat16),
        scratch_shapes=[
            pltpu.VMEM(reset_col.shape, reset_col.dtype),
            pltpu.VMEM(low.shape, low.dtype),
            pltpu.VMEM((shards, rank, width), jnp.bfloat16),
            pltpu.VMEM((toks, wide), jnp.bfloat16),
            pltpu.SemaphoreType.DMA((2 + 2 * shards,)),
            pltpu.VMEM((states, toks), jnp.float32),
            pltpu.VMEM((toks, 16 * states), jnp.bfloat16),
            pltpu.VMEM((toks // 16, wide // LANES, 16, LANES), jnp.float32),
            pltpu.VMEM((toks // 16, wide // LANES, 16, LANES), jnp.float32),
            pltpu.VMEM((16 * states, wide), jnp.bfloat16),
            pltpu.VMEM((16 * states, wide), jnp.bfloat16),
        ],
        compiler_params=pltpu.CompilerParams(vmem_limit_bytes=54 << 20),
        cost_estimate=pl.CostEstimate(
            flops=6 * steps, bytes_accessed=2 * shards * rank * width + 4 * toks * wide, transcendentals=steps
        ),
        name=f"state_scan_{first_shard}",
    )(reset_col, low, delta_parts, bias, decay, gain, *convs)


def gate_kernel(fold, width, gate_ref, *refs):
    out_ref = refs[-1]
    slot = 0
    for y_ref in refs[:-1]:
        ctx, _, wide = y_ref.shape
        for place in range(wide // width):
            for piece in range(ctx):
                lanes = piece_lanes(slot, piece, ctx, fold, width)
                value = y_ref[piece, :, place * width : (place + 1) * width].astype(jnp.float32)
                out_ref[:, lanes] = (value * silu(gate_ref[:, lanes].astype(jnp.float32))).astype(out_ref.dtype)
            slot += 1


def apply_gate(parts, gate, fold, width):
    rows, channels = gate.shape
    ctx = parts[0].shape[0]
    part = min(rows, 32)
    columns = pl.BlockSpec((part, channels), lambda r: (r, 0))
    return pl.pallas_call(
        functools.partial(gate_kernel, fold, width),
        grid=(rows // part,),
        in_specs=[columns] + [pl.BlockSpec((ctx, part, array.shape[2]), lambda r: (0, r, 0)) for array in parts],
        out_specs=columns,
        out_shape=jax.ShapeDtypeStruct(gate.shape, jnp.bfloat16),
        compiler_params=pltpu.CompilerParams(vmem_limit_bytes=16 << 20),
        cost_estimate=pl.CostEstimate(flops=4 * gate.size, bytes_accessed=6 * gate.size, transcendentals=gate.size),
        name="gate",
    )(gate, *parts)


def shifted(value, axis, by):
    size = lax.axis_size(axis)
    pairs = [(i, i + by) for i in range(size) if 0 <= i + by < size]
    return lax.ppermute(value, axis, pairs)


def exchange(value):
    return lax.all_to_all(value, "ctx", 0, 0, tiled=True)


def local(
    queries,
    keys,
    values,
    mixer_input,
    gate_input,
    segment_ids,
    conv_weight,
    conv_bias,
    select_weight,
    delta_weight,
    delta_bias,
    decay_log,
    skip_gain,
):
    ctx = lax.axis_size("ctx")
    shards = lax.axis_size("rep")
    place = lax.axis_index("ctx")
    rows, channels = mixer_input.shape[1:]
    rank = delta_weight.shape[0]
    states = decay_log.shape[1]
    width = max(channels // (shards * ctx), LANES)
    fold = width * shards * ctx // channels
    seg = segment_ids[0]
    toks = seg.shape[0]
    back = min(ctx - 1, -(-(toks // 2 - 1) // rows))

    slots = shards // fold

    def own_part(array):
        cut = array.reshape(array.shape[:-1] + (slots, fold, ctx // fold, width))
        cut = lax.dynamic_index_in_dim(cut, place // fold, cut.ndim - 2, keepdims=False)
        cut = lax.dynamic_index_in_dim(cut, place % fold, cut.ndim - 2, keepdims=False)
        return cut.reshape(array.shape[:-1] + (slots * width,))

    def own_columns(weight):
        return lax.dynamic_slice_in_dim(weight, place // fold * width, width, 1)

    def gathered(own):
        parts = lax.all_gather(own, "rep", axis=0)
        if fold > 1:
            parts = parts.reshape((slots, fold) + own.shape)
            parts = lax.dynamic_index_in_dim(parts, place % fold, 1, keepdims=False)
        return parts

    select_parts = gathered(own_columns(select_weight))
    packed = pack(mixer_input[0], ctx, fold, width)

    same = jnp.concatenate([jnp.zeros((1,), bool), seg[1:] == seg[:-1]])
    reset_col = jnp.where(same, 0.0, FAR)[:, None]
    seg_before = jnp.concatenate([jnp.full((3,), -1, jnp.int32), seg])
    match = jnp.stack([(seg_before[tap : tap + toks] == seg) for tap in range(3)], axis=1).astype(jnp.float32)
    seg_pad = jnp.concatenate([jnp.full((back * rows,), -1, jnp.int32), seg])
    seg_k = lax.dynamic_slice_in_dim(seg_pad, place * rows, (back + 1) * rows, 0)
    own = (
        own_part(delta_bias)[None, :],
        own_part(jnp.transpose(decay_log)),
        own_part(skip_gain)[None, :],
        reset_col,
        seg_k[back * rows :, None],
        seg_k[None, :],
        jnp.concatenate([keys[0], values[0]], axis=1),
        own_part(conv_weight),
        own_part(conv_bias)[None, :],
        match,
        own_columns(delta_weight),
    )
    pieces, own = lax.optimization_barrier((exchange(packed), own))
    bias, decay, gain, reset_col, seg_q, seg_k, both, conv_weight, conv_bias, match, delta_own = own
    delta_parts = gathered(delta_own)

    *convs, parts = conv_select(match, pieces, conv_weight, conv_bias, select_parts)
    parts, both = lax.optimization_barrier((parts, both))
    blocks = [shifted(both, "ctx", by) for by in range(back, 0, -1)] + [both]
    low = normalise(exchange(parts), rank)
    low = exchange(low).reshape(toks, low.shape[2])

    split = slots * 5 // 8
    scanned = [
        state_scan(reset_col, low, delta_parts, bias, decay, gain, convs, ctx, first, count)
        for first, count in ((0, split), (split, slots - split))
    ]
    scanned[0], blocks = lax.optimization_barrier((scanned[0], blocks))
    attended = attention(queries[0], blocks, seg_q, seg_k, 0, KEY_VALUE_HEADS)
    scanned = [exchange(part) for part in scanned]
    scanned[0], attended = lax.optimization_barrier((scanned[0], attended))
    mixed = apply_gate(scanned, gate_input[0], fold, width)
    return (attended[None], mixed[None])


def solution(mesh):
    placed = (
        P("rep", "ctx", None),
        P("rep", "ctx", None),
        P("rep", "ctx", None),
        P("rep", "ctx", None),
        P("rep", "ctx", None),
        P("rep", None),
        P(),
        P(),
        P(None, "rep"),
        P(None, "rep"),
        P(),
        P(),
        P(),
    )
    return jax.shard_map(
        local,
        mesh=mesh,
        in_specs=placed,
        out_specs=(P("rep", "ctx", None), P("rep", "ctx", None)),
        check_vma=False,
    )
```
